32 devices in a mesh: group: 2 (over y), expert: 16 (over z, x, core), dp: 1.
Axes of the slice: x: 2, y: 2, z: 4, core: 2. Of those that a mesh axis runs over, the one named last changes fastest.
Arguments:
- tokens: bfloat16 [1536, 3584], P(('group', 'expert', 'dp')), parts along dimension 0, may hold values from -6 to 6
- expert_ids: int32 [1536, 8], P(('group', 'expert', 'dp')), parts along dimension 0, may hold values from 0 to 15, all different within a row; in each aligned block of 48 rows (0 to 47, 48 to 95, ...) at most 36 rows name the same one
- route_probs: float32 [1536, 8], P(('group', 'expert', 'dp')), parts along dimension 0, may hold values from 0.1 to 1
- cotangents: bfloat16 [1536, 8, 2560], P(('group', 'expert', 'dp')), parts along dimension 0, may hold values from -6 to 6
- sketch: float32 [2560, 32], replicated, may hold values from -6 to 6
Outputs:
- basis: float32 [32, 32, 3584], P(('group', 'expert'), None, 'dp'), parts along dimension 0
- coeffs: float32 [32, 32, 2560], P(('group', 'expert'), None, 'dp'), parts along dimension 0
The draws below stay inside these ranges and needn't reach their ends.
There are 2 independent parts, one for each index of `group`. The reference program is written for one: setup_inputs(seed, part) draws one part's arguments, and reference() takes and returns one part's arrays. A program takes and returns all parts, laid end to end along the dimension named above; an argument that names none is the same for every part. Nothing has to cross between parts.
Inputs may be any that keep to these rules, and one draw needn't show every extreme that they name: `expert_ids`: each row names 8 different experts. In the rows of one device no expert is named more than 36 times, and exactly 36 times for some expert in some devices.
All inputs are finite; a program needn't handle non-finite values.
Results may differ from the reference program's by a relative error of at most 0.019.
Values may be sent and summed in bfloat16 or wider, within the bound.
No kernel may reach another device: no remote copies, remote signals or barrier semaphores. Data moves between devices by JAX's collectives and lax.ppermute only.
A program may use at most 128 MiB of HBM per device.

```python
import math
import jax
import jax.numpy as jnp
import numpy as np
from jax import lax

D = 3584
FF = 2560
TOP = 8
K = 32
TOK_DEV = 48
EXPERTS = 16
TOKENS = 768
CAP = 36
N_EXPERT = 16
N_DP = 1


def block_scale(own_key, extent, pieces, least, top_value):
    gain, own = 1.0, jax.random.fold_in(own_key, 6)
    for position, blocks in pieces:
        draws = jnp.exp(jax.random.uniform(jax.random.fold_in(own, position), (blocks,), jnp.float32, least / len(pieces), top_value / len(pieces)))
        gain = gain * jnp.repeat(draws, extent[position] // blocks).reshape([-1 if axis == position else 1 for axis in range(len(extent))])
    return gain


def assign_block(rng, own, number, rows, count, top, limit, slope):
    sequence = jax.random.permutation(rng, count)
    heavy_load, common = load_shares(count, rows * top, limit, slope, True), load_shares(count, rows * top, limit, slope, False)
    places = jnp.arange(count)

    def named(lengths, turn):
        used = int((lengths > 0).sum())
        fixed = max(1, used // 4)
        moved = fixed + (places - fixed + turn * (used - fixed)) % max(1, count - fixed)
        return jnp.zeros((count,), jnp.int32).at[sequence[jnp.where(places < fixed, places, moved)]].set(jnp.asarray(lengths, jnp.int32))

    lengths = jnp.where(number % 4 == 0, named(heavy_load, number // 4), named(common, number - number // 4 - 1))
    mixed = jax.random.permutation(jax.random.fold_in(own, 3), count)
    source_of, receiver = mixed[0:count // 2 * 2:2], mixed[1:count // 2 * 2:2]
    margin = jnp.minimum(lengths[source_of] - 1, limit - lengths[receiver]) // 2
    margin = jnp.where((source_of == sequence[0]) | (receiver == sequence[0]) | (lengths[receiver] == 0), 0, jnp.maximum(margin, 0))
    moved = jax.random.randint(jax.random.fold_in(own, 4), (count // 2,), 0, 1 << 20) % (margin + 1)
    lengths = lengths.at[source_of].add(-moved).at[receiver].add(moved)
    items = jnp.searchsorted(jnp.cumsum(lengths), jnp.arange(rows * top), side="right").astype(jnp.int32)
    grid = items.reshape(top, rows).T
    grid = grid[jax.random.permutation(jax.random.fold_in(own, 1), rows)]
    turn = jax.random.randint(jax.random.fold_in(own, 2), (rows, 1), 0, top)
    return jnp.take_along_axis(grid, (jnp.arange(top)[None, :] + turn) % top, axis=1)


def load_shares(count, total, bound, lean, full):
    loads = [(1 << 20) // math.isqrt(standing ** lean) + 1 for standing in range(1, count + 1)]
    largest = bound if full else min(bound, max(-(-total // count), total * loads[0] // sum(loads)))
    least = 1 if total - largest >= count - 1 else 0
    holding, spare = [largest] + [least] * (count - 1), total - largest - least * (count - 1)
    while spare > 0:
        movable = [i for i in range(1, count) if holding[i] < largest] or [i for i in range(1, count) if holding[i] < bound]
        pool, remaining = sum([loads[i] for i in movable]), spare
        for i in movable:
            more = min(bound - holding[i], max(1, remaining * loads[i] // pool), spare)
            holding[i] = holding[i] + more
            spare = spare - more
    return np.array(holding)


def normal_values(own_key, shape, width, reach, shards=(), kind=jnp.bfloat16):
    gain = block_scale(own_key, shape, shards, -0.22, 0.18) if shards else 1.0
    array = jax.random.normal(own_key, shape, jnp.float32) * width * gain
    return jnp.minimum(jnp.maximum(array, -reach), reach).astype(kind)


def setup_inputs(seed: int = 0, part: int = 0) -> dict:
    arg_keys = jax.random.split(jax.random.key(seed), 6)
    own_keys = jax.random.split(jax.random.fold_in(arg_keys[5], part), 6)
    tokens = normal_values(own_keys[0], (TOKENS, D), 1.0, 6.0, ((0, 16),))
    expert_ids_keys = jax.random.split(jax.random.fold_in(own_keys[1], 1), TOKENS // TOK_DEV)
    expert_ids_turns = jax.random.permutation(jax.random.fold_in(own_keys[1], 3), TOKENS // TOK_DEV)
    expert_ids = jax.vmap(lambda own, number: assign_block(jax.random.fold_in(own_keys[1], 2), own, number, TOK_DEV, EXPERTS, TOP, CAP, 2))(expert_ids_keys, expert_ids_turns).reshape((TOKENS, TOP))
    route_probs = jnp.clip(0.1 + 0.9 * jax.random.uniform(own_keys[2], (TOKENS, TOP), jnp.float32) ** block_scale(own_keys[2], (TOKENS, TOP), ((0, 16),), -0.2, 0.2), 0.1, 1.0)
    cotangents = normal_values(own_keys[3], (TOKENS, TOP, FF), 1.0, 6.0, ((0, 16),))
    sketch = normal_values(arg_keys[4], (FF, K), 1.0, 6.0, (), jnp.float32)
    return dict(tokens=tokens, expert_ids=expert_ids, route_probs=route_probs, cotangents=cotangents, sketch=sketch)


def orthonormal(range_rows):
    high = lax.Precision.HIGHEST
    gram = jnp.dot(range_rows.T, range_rows, precision=high)
    lower = jnp.linalg.cholesky(gram)
    return jax.scipy.linalg.solve_triangular(lower, range_rows.T, lower=True)

def reference(tokens, expert_ids, route_probs, cotangents, sketch):
    high = lax.Precision.HIGHEST
    rows_all = TOKENS * TOP
    ids_flat = expert_ids.reshape(-1).astype(jnp.int32)
    half_of = (jnp.arange(rows_all, dtype=jnp.int32) // (TOK_DEV * TOP) % N_DP).astype(jnp.int32)
    keys = (ids_flat * N_DP + half_of).astype(jnp.int32)
    order = jnp.argsort(keys, stable=True).astype(jnp.int32)
    counts = lax.optimization_barrier(jnp.sum((keys[:, None] == jnp.arange(EXPERTS * N_DP, dtype=jnp.int32)[None, :]).astype(jnp.int32), axis=0))
    starts = (jnp.cumsum(counts) - counts).astype(jnp.int32)
    room = N_EXPERT * CAP
    order_pad = jnp.concatenate([order, jnp.zeros((room,), jnp.int32)])
    weighted = (route_probs[..., None] * cotangents.astype(jnp.float32)).astype(jnp.bfloat16).reshape(rows_all, FF)
    scale = 1.0 / math.sqrt(TOK_DEV * TOP)

    def one_expert(expert):
        grad = jnp.zeros((D, FF), jnp.float32)
        for half in range(N_DP):
            slot = expert * N_DP + half
            picked = lax.dynamic_slice(order_pad, (starts[slot].astype(jnp.int32),), (room,))
            live = jnp.arange(room, dtype=jnp.int32) < counts[slot]
            rows_x = tokens[picked // TOP]
            rows_w = jnp.where(live[:, None], weighted[picked], jnp.zeros((), jnp.bfloat16))
            partial_value = (jnp.dot(rows_x.T.astype(jnp.float32), rows_w.astype(jnp.float32), preferred_element_type=jnp.float32) * scale).astype(jnp.bfloat16)
            grad = grad + partial_value.astype(jnp.float32)
        range_rows = jnp.dot(grad, sketch, precision=high)
        ortho = orthonormal(range_rows)
        return (math.sqrt(D) * ortho, jnp.dot(ortho, grad, precision=high))
    basis, coeffs = lax.map(one_expert, jnp.arange(EXPERTS, dtype=jnp.int32))
    return (basis, coeffs)
```

```python
import math

import jax
import jax.numpy as jnp
from jax import lax
from jax.sharding import PartitionSpec as P

AXES = ("expert", "dp")
HIGH = lax.Precision.HIGHEST


def dot(left, right, dims):
    return lax.dot_general(left, right, (dims, ((), ())), preferred_element_type=jnp.float32)


def shards(tokens, expert_ids, route_probs, cotangents, sketch):
    n_expert = lax.axis_size("expert")
    n_dp = lax.axis_size("dp")
    tok, width = tokens.shape
    top = expert_ids.shape[1]
    hidden, rank = sketch.shape
    rows = tok * top
    scale = 1.0 / math.sqrt(rows)
    cot = cotangents.reshape(rows, hidden)

    x_all = lax.all_gather(tokens, AXES, axis=0, tiled=True)

    high = sketch.astype(jnp.bfloat16)
    low = (sketch - high.astype(jnp.float32)).astype(jnp.bfloat16)
    both = dot(cot, jnp.concatenate([high, low], axis=1), ((1,), (0,)))
    pair = (both[:, :rank] + both[:, rank:]).reshape(tok, top, rank) * route_probs[..., None]
    chosen = expert_ids[..., None] == jnp.arange(n_expert, dtype=jnp.int32)
    y = jnp.sum(jnp.where(chosen[..., None], pair[:, :, None, :], 0.0), axis=1)
    y = y.reshape(tok, n_expert * rank).astype(jnp.bfloat16)
    y_all = lax.all_gather(y, AXES, axis=0, tiled=True)

    near = dot(tokens, x_all, ((1,), (1,))).astype(jnp.bfloat16)
    z = dot(near, y_all, ((1,), (0,)))
    weights = jnp.where(chosen, route_probs[..., None], 0.0)
    spread = z.reshape(tok, 1, n_expert, rank) * weights[..., None]
    spread = spread.reshape(rows, n_expert * rank).astype(jnp.bfloat16)
    part = dot(spread, cot, ((0,), (0,))).astype(jnp.bfloat16)
    if n_dp > 1:
        part = part.reshape(n_expert, rank, n_dp, hidden // n_dp).swapaxes(1, 2)
        part = part.reshape(n_expert * n_dp * rank, hidden // n_dp)
    total = lax.psum_scatter(part, AXES, scatter_dimension=0, tiled=True).astype(jnp.float32)

    own = lax.axis_index("expert")
    y_own = lax.dynamic_slice_in_dim(y_all, own * rank, rank, axis=1)
    range_rows = dot(y_own, x_all, ((0,), (0,)))
    gram = lax.dot_general(range_rows, range_rows, (((1,), (1,)), ((), ())), precision=HIGH)
    lower = jnp.linalg.cholesky(gram)
    inverse = jax.scipy.linalg.solve_triangular(
        lower, jnp.eye(rank, dtype=jnp.float32), lower=True
    )
    share = width // n_dp
    kept = lax.dynamic_slice_in_dim(range_rows, lax.axis_index("dp") * share, share, axis=1)
    basis = jnp.dot(inverse * math.sqrt(width), kept, precision=HIGH)
    coeffs = jnp.dot(inverse * scale, total, precision=HIGH)
    return basis[None], coeffs[None]


def solution(mesh):
    in_specs = (
        P(("group", "expert", "dp"), None),
        P(("group", "expert", "dp"), None),
        P(("group", "expert", "dp"), None),
        P(("group", "expert", "dp"), None, None),
        P(),
    )
    out_specs = (P(("group", "expert"), None, "dp"), P(("group", "expert"), None, "dp"))
    return jax.shard_map(shards, mesh=mesh, in_specs=in_specs, out_specs=out_specs, check_vma=False)
```

```python
import math

import jax
import jax.numpy as jnp
from jax import lax
from jax.sharding import PartitionSpec as P

AXES = ("expert", "dp")
HIGH = lax.Precision.HIGHEST
CHUNKS = 2


def dot(left, right, dims):
    return lax.dot_general(left, right, (dims, ((), ())), preferred_element_type=jnp.float32)


def exchange(block, step, count):
    return lax.ppermute(block, AXES, [(i, i ^ step) for i in range(count)])


def scatter_sum(blocks, count):
    step = 1
    while blocks.shape[0] > 4:
        pairs = blocks.reshape(-1, 2, *blocks.shape[1:])
        other = exchange(pairs[:, 1], step, count)
        blocks = (pairs[:, 0].astype(jnp.float32) + other.astype(jnp.float32)).astype(jnp.bfloat16)
        step *= 2
    total = blocks[0].astype(jnp.float32)
    others = [exchange(blocks[j], j * step, count) for j in range(1, blocks.shape[0])]
    for other in others:
        total = total + other.astype(jnp.float32)
    return total


def shards(tokens, expert_ids, route_probs, cotangents, sketch):
    n_expert = lax.axis_size("expert")
    n_dp = lax.axis_size("dp")
    count = n_expert * n_dp
    tok, width = tokens.shape
    top = expert_ids.shape[1]
    hidden, rank = sketch.shape
    rows = tok * top
    share = width // count
    lanes = -(-(share + top) // 128) * 128
    scale = 1.0 / math.sqrt(rows)
    cot = cotangents.reshape(rows, hidden)
    own = lax.axis_index("expert")
    half = lax.axis_index("dp")

    cut = tokens.reshape(tok, count, share).swapaxes(0, 1)
    names = jnp.broadcast_to(expert_ids.astype(jnp.bfloat16)[None], (count, tok, top))
    cut = jnp.concatenate(
        [cut, names, jnp.zeros((count, tok, lanes - share - top), jnp.bfloat16)], axis=2
    )
    cut = lax.all_to_all(cut, AXES, split_axis=0, concat_axis=0, tiled=True)
    cut = cut.reshape(count * tok, lanes)
    names_all = cut[:, share : share + top]
    x = jnp.where(jnp.arange(lanes) < share, cut, jnp.zeros((), jnp.bfloat16))

    block = jnp.arange(n_expert * rank, dtype=jnp.int32) // rank
    ids = expert_ids.reshape(rows, 1)
    probs = route_probs.reshape(rows, 1)
    wide = jnp.tile(sketch.astype(jnp.bfloat16), (1, n_expert))
    y = jnp.where(ids == block, dot(cot, wide, ((1,), (0,))) * probs, 0.0)
    y = jnp.sum(y.reshape(tok, top, n_expert * rank), axis=1).astype(jnp.bfloat16)
    y_all = lax.all_gather(y, AXES, axis=0, tiled=True)

    columns = dot(y_all, x, ((0,), (0,))).astype(jnp.bfloat16)
    z = dot(x, columns, ((1,), (1,)))
    fold = (jnp.arange(n_expert * rank)[:, None] % rank == jnp.arange(rank)).astype(jnp.bfloat16)
    taken = [
        dot(
            jnp.where(names_all[:, s : s + 1] == block.astype(jnp.bfloat16), z, 0.0).astype(
                jnp.bfloat16
            ),
            fold,
            ((1,), (0,)),
        ).astype(jnp.bfloat16)
        for s in range(top)
    ]
    z = jnp.concatenate(taken, axis=1).reshape(count, tok, top * rank)
    z = lax.all_to_all(z, AXES, split_axis=0, concat_axis=0, tiled=True)
    columns = jnp.repeat(columns.reshape(n_expert, rank, lanes), n_dp, axis=0)
    columns = lax.all_to_all(columns, AXES, split_axis=0, concat_axis=0, tiled=True)

    z = jnp.repeat(jnp.sum(z.astype(jnp.float32), axis=0), top, axis=0) * probs
    slot = jnp.arange(top * rank) // rank
    z = jnp.where(jnp.arange(rows)[:, None] % top == slot, z, 0.0).astype(jnp.bfloat16)
    spread = jnp.arange(top * rank)[:, None] % rank == jnp.arange(n_expert * rank) % rank
    spread = dot(z, spread.astype(jnp.bfloat16), ((1,), (0,)))
    spread = jnp.where((ids ^ own) == block, spread, 0.0).astype(jnp.bfloat16)
    piece = hidden // n_dp // CHUNKS
    totals = []
    for chunk in range(CHUNKS):
        terms = []
        for h in range(n_dp):
            start = (half ^ h) * (hidden // n_dp) + chunk * piece
            columns_cot = (
                lax.dynamic_slice_in_dim(cot, start, piece, axis=1)
                if n_dp > 1
                else cot[:, chunk * piece : (chunk + 1) * piece]
            )
            part = dot(spread, columns_cot, ((0,), (0,))).astype(jnp.bfloat16)
            terms.append(part.reshape(n_expert, rank, piece))
        totals.append(scatter_sum(jnp.stack(terms, axis=1).reshape(count, rank, piece), count))
    total = jnp.concatenate(totals, axis=1)

    range_rows = columns[:, :, :share].swapaxes(0, 1).reshape(rank, width).astype(jnp.float32)
    gram = lax.dot_general(range_rows, range_rows, (((1,), (1,)), ((), ())), precision=HIGH)
    lower = jnp.linalg.cholesky(gram)
    inverse = jax.scipy.linalg.solve_triangular(
        lower, jnp.eye(rank, dtype=jnp.float32), lower=True
    )
    kept = lax.dynamic_slice_in_dim(range_rows, half * (width // n_dp), width // n_dp, axis=1)
    basis = jnp.dot(inverse * math.sqrt(width), kept, precision=HIGH)
    coeffs = jnp.dot(inverse * scale, total, precision=HIGH)
    return basis[None], coeffs[None]


def solution(mesh):
    in_specs = (
        P(("group", "expert", "dp"), None),
        P(("group", "expert", "dp"), None),
        P(("group", "expert", "dp"), None),
        P(("group", "expert", "dp"), None, None),
        P(),
    )
    out_specs = (P(("group", "expert"), None, "dp"), P(("group", "expert"), None, "dp"))
    return jax.shard_map(shards, mesh=mesh, in_specs=in_specs, out_specs=out_specs, check_vma=False)
```

```python
import math

import jax
import jax.numpy as jnp
from jax import lax
from jax.sharding import PartitionSpec as P

AXES = ("expert", "dp")
HIGH = lax.Precision.HIGHEST
CHUNKS = 2
SLICES = 4


def dot(left, right, dims):
    return lax.dot_general(left, right, (dims, ((), ())), preferred_element_type=jnp.float32)


def exchange(block, step, count):
    return lax.ppermute(block, AXES, [(i, i ^ step) for i in range(count)])


def scatter_sum(blocks, count):
    step = 1
    while blocks.shape[0] > SLICES:
        pairs = blocks.reshape(-1, 2, *blocks.shape[1:])
        other = exchange(pairs[:, 1], step, count)
        blocks = (pairs[:, 0].astype(jnp.float32) + other.astype(jnp.float32)).astype(jnp.bfloat16)
        step *= 2
    return line_sum([blocks[j] for j in range(blocks.shape[0])], count)


def line_sum(blocks, count):
    line = count // SLICES
    others = [exchange(blocks[j], j * line, count) for j in range(1, SLICES)]
    total = blocks[0].astype(jnp.float32)
    for other in others:
        total = total + other.astype(jnp.float32)
    return total


def spread_rows(rows, count):
    step = count // SLICES // 2
    while step:
        rows = jnp.concatenate([rows, exchange(rows, step, count)], axis=0)
        step //= 2
    return rows


def shards(tokens, expert_ids, route_probs, cotangents, sketch):
    n_expert = lax.axis_size("expert")
    n_dp = lax.axis_size("dp")
    count = n_expert * n_dp
    line = count // SLICES
    tok, width = tokens.shape
    top = expert_ids.shape[1]
    hidden, rank = sketch.shape
    rows = tok * top
    share = width // SLICES
    scale = 1.0 / math.sqrt(rows)
    cot = cotangents.reshape(rows, hidden)
    own = lax.axis_index("expert")
    half = lax.axis_index("dp")
    place = lax.axis_index(AXES) // line

    cuts = [
        lax.dynamic_slice_in_dim(tokens, (place ^ j) * share, share, axis=1) for j in range(SLICES)
    ]
    x_line = jnp.concatenate(
        [cuts[0]] + [exchange(cuts[j], j * line, count) for j in range(1, SLICES)], axis=0
    )
    x = spread_rows(x_line, count)

    block = jnp.arange(n_expert * rank, dtype=jnp.int32) // rank
    ids = expert_ids.reshape(rows, 1)
    probs = route_probs.reshape(rows, 1)
    wide = jnp.tile(sketch.astype(jnp.bfloat16), (1, n_expert))
    y = jnp.where(ids == block, dot(cot, wide, ((1,), (0,))) * probs, 0.0)
    y = jnp.sum(y.reshape(tok, top, n_expert * rank), axis=1).astype(jnp.bfloat16)
    y = jnp.concatenate([y] + [exchange(y, j * line, count) for j in range(1, SLICES)], axis=0)
    y = spread_rows(y, count)

    columns = dot(y, x, ((0,), (0,))).astype(jnp.bfloat16)
    z = dot(x_line, columns, ((1,), (1,))).astype(jnp.bfloat16)
    z = line_sum([z[j * tok : (j + 1) * tok] for j in range(SLICES)], count)

    lane = jnp.arange(n_expert * rank, dtype=jnp.int32)
    turn = lane[:, None] == (((lane // rank) ^ own) * rank + lane % rank)
    z = dot(z.astype(jnp.bfloat16), turn.astype(jnp.bfloat16), ((1,), (0,)))
    spread = jnp.where((ids ^ own) == block, jnp.repeat(z, top, axis=0) * probs, 0.0)
    spread = spread.astype(jnp.bfloat16)
    piece = hidden // n_dp // CHUNKS
    totals = []
    for chunk in range(CHUNKS):
        terms = []
        for h in range(n_dp):
            start = (half ^ h) * (hidden // n_dp) + chunk * piece
            part_cot = (
                lax.dynamic_slice_in_dim(cot, start, piece, axis=1)
                if n_dp > 1
                else cot[:, chunk * piece : (chunk + 1) * piece]
            )
            part = dot(spread, part_cot, ((0,), (0,))).astype(jnp.bfloat16)
            terms.append(part.reshape(n_expert, rank, piece))
        totals.append(scatter_sum(jnp.stack(terms, axis=1).reshape(count, rank, piece), count))
    total = jnp.concatenate(totals, axis=1)

    parts = []
    for j in range(SLICES):
        expert = own ^ (j * n_expert // SLICES)
        part = lax.dynamic_slice_in_dim(columns, expert * rank, rank, axis=0)
        parts.append(exchange(part, j * line, count) if j else part)
    parts = jnp.stack(parts)
    parts = [lax.dynamic_index_in_dim(parts, place ^ j, 0, False) for j in range(SLICES)]
    range_rows = jnp.concatenate(parts, axis=1).astype(jnp.float32)
    gram = lax.dot_general(range_rows, range_rows, (((1,), (1,)), ((), ())), precision=HIGH)
    lower = jnp.linalg.cholesky(gram)
    inverse = jax.scipy.linalg.solve_triangular(
        lower, jnp.eye(rank, dtype=jnp.float32), lower=True
    )
    kept = lax.dynamic_slice_in_dim(range_rows, half * (width // n_dp), width // n_dp, axis=1)
    basis = jnp.dot(inverse * math.sqrt(width), kept, precision=HIGH)
    coeffs = jnp.dot(inverse * scale, total, precision=HIGH)
    return basis[None], coeffs[None]


def solution(mesh):
    in_specs = (
        P(("group", "expert", "dp"), None),
        P(("group", "expert", "dp"), None),
        P(("group", "expert", "dp"), None),
        P(("group", "expert", "dp"), None, None),
        P(),
    )
    out_specs = (P(("group", "expert"), None, "dp"), P(("group", "expert"), None, "dp"))
    return jax.shard_map(shards, mesh=mesh, in_specs=in_specs, out_specs=out_specs, check_vma=False)
```

```python
import functools
import math

import jax
import jax.numpy as jnp
from jax import lax
from jax.experimental import pallas as pl
from jax.experimental.pallas import tpu as pltpu
from jax.sharding import PartitionSpec as P

AXES = ("expert", "dp")
HIGH = lax.Precision.HIGHEST
CHUNKS = 2
SLICES = 4
VMEM = pl.BlockSpec(memory_space=pltpu.VMEM)
SMEM = pl.BlockSpec(memory_space=pltpu.SMEM)
BF16 = jnp.bfloat16
F32 = jnp.float32


def dot(left, right, left_dim, right_dim):
    dims = (((left_dim,), (right_dim,)), ((), ()))
    return lax.dot_general(left, right, dims, preferred_element_type=F32)


def iota(shape, dim):
    return lax.broadcasted_iota(jnp.int32, shape, dim)


def call(body, shapes, flops, size, *args, spaces=None):
    return pl.pallas_call(
        body,
        out_shape=shapes,
        in_specs=spaces or [VMEM] * len(args),
        out_specs=jax.tree.map(lambda _: VMEM, shapes),
        compiler_params=pltpu.CompilerParams(vmem_limit_bytes=48 * 1024 * 1024),
        cost_estimate=pl.CostEstimate(flops=flops, bytes_accessed=size, transcendentals=0),
    )(*args)


def pair_columns(ids, probs):
    tok, top = ids.shape
    rows = tok * top
    pick = (iota((rows, tok), 0) // top == iota((rows, tok), 1)).astype(BF16)
    here = iota((rows, top), 0) % top == iota((rows, top), 1)
    names = dot(pick, ids.astype(BF16), 1, 0)
    weights, rest = jnp.zeros((rows, top), F32), probs
    for _ in range(3):
        piece = rest.astype(BF16)
        weights = weights + dot(pick, piece, 1, 0)
        rest = rest - piece.astype(F32)
    names = jnp.sum(jnp.where(here, names, 0.0), axis=1, keepdims=True)
    weights = jnp.sum(jnp.where(here, weights, 0.0), axis=1, keepdims=True)
    return names, weights


def lane_names(n_expert, rank, groups):
    block = iota((1, n_expert * rank), 1) // rank
    per = n_expert // groups
    return ((block % per) * groups + block // per).astype(F32)


def y_kernel(groups, cot, sketch, ids, probs, *outs):
    rows, _ = cot.shape
    tok, top = ids.shape
    rank = sketch.shape[1]
    lanes = outs[0].shape[1] * len(outs)
    high = sketch[...].astype(BF16)
    low = (sketch[...] - high.astype(F32)).astype(BF16)
    pair = dot(cot[...], high, 1, 0) + dot(cot[...], low, 1, 0)
    names, weights = pair_columns(ids[...], probs[...])
    pair = (pair * weights).astype(BF16)
    tile = (iota((rank, lanes), 0) == iota((rank, lanes), 1) % rank).astype(BF16)
    y = jnp.where(names == lane_names(lanes // rank, rank, groups), dot(pair, tile, 1, 0), 0.0)
    y = jnp.sum(y.reshape(tok, top, lanes), axis=1).astype(BF16)
    each = lanes // len(outs)
    for i, out in enumerate(outs):
        out[...] = y[:, i * each : (i + 1) * each]


def z_kernel(n, *refs):
    xs, ys, (columns, z) = refs[: 2 * n], refs[2 * n : 3 * n], refs[3 * n :]
    total = 0.0
    for b in range(n):
        for core in range(2):
            y = jnp.concatenate([ys[b][i, core] for i in range(SLICES)], axis=0)
            x = jnp.concatenate([xs[2 * b + core][i] for i in range(SLICES)], axis=0)
            total = total + dot(y, x, 0, 0)
    total = total.astype(BF16)
    columns[...] = total
    for core in range(2):
        tok = xs[core].shape[1]
        x = jnp.concatenate([xs[core][i] for i in range(SLICES)], axis=0)
        part = dot(x, total, 1, 1).astype(BF16)
        for i in range(SLICES):
            z[i, core] = part[i * tok : (i + 1) * tok]


def shards(tokens, expert_ids, route_probs, cotangents, sketch):
    n_expert = lax.axis_size("expert")
    n_dp = lax.axis_size("dp")
    count = n_expert * n_dp
    line = count // SLICES
    low = line // 2
    groups = 2 // n_dp
    tok, width = tokens.shape
    top = expert_ids.shape[1]
    hidden, rank = sketch.shape
    rows = tok * top
    share = width // SLICES
    lanes = count // 2 * rank
    part = hidden // n_dp
    scale = 1.0 / math.sqrt(rows)
    own = lax.axis_index("expert")
    half = lax.axis_index("dp")
    me = lax.axis_index(AXES)
    core = me % 2
    place = me // line

    def exchange(block, step):
        return lax.ppermute(block, AXES, [(i, i ^ step) for i in range(count)])

    def along(blocks):
        lists = [[i + j * line for j in range(SLICES)] for i in range(line)]
        return lax.all_to_all(
            blocks, AXES, split_axis=0, concat_axis=0, axis_index_groups=lists, tiled=True
        )

    xs = [along(tokens.reshape(tok, SLICES, share).swapaxes(0, 1))]

    cot = cotangents.reshape(rows, hidden)
    if n_dp > 1:
        mine = lax.dynamic_slice_in_dim(cot, half * part, part, axis=1)
        other = exchange(lax.dynamic_slice_in_dim(cot, (1 - half) * part, part, axis=1), 1)
    else:
        mine, other = cot, exchange(cot, 1)
    names = expert_ids ^ core if groups == 2 else expert_ids
    pairs = jnp.concatenate([expert_ids.astype(F32), route_probs], axis=1)
    pairs = jnp.stack([pairs, exchange(pairs, 1)])

    y = call(
        functools.partial(y_kernel, groups),
        [jax.ShapeDtypeStruct((tok, lanes), BF16)] * groups,
        4 * rows * hidden * rank,
        2 * rows * hidden,
        cot,
        sketch,
        names,
        route_probs,
    )
    y = jnp.stack([y[0], exchange(y[-1], 1)])
    ys = [along(jnp.broadcast_to(y[None], (SLICES, 2, tok, lanes)))]
    step = 2
    while step < line:
        ys = ys + [exchange(b, step) for b in ys]
        xs = xs + [exchange(b, step) for b in xs]
        step *= 2
    xs = [b for x in xs for b in (x, exchange(x, 1))]

    small = n_dp == 1
    if small:
        columns, z = call(
            functools.partial(z_kernel, len(ys)),
            [
                jax.ShapeDtypeStruct((lanes, share), BF16),
                jax.ShapeDtypeStruct((SLICES, 2, tok, lanes), BF16),
            ],
            2 * count * tok * lanes * share * 3 // 2,
            2 * count * tok * (lanes + share),
            *xs,
            *ys,
        )
    else:
        left = jnp.concatenate(ys, axis=0).reshape(-1, lanes)
        right = [jnp.stack(xs[i : i + 2], axis=1) for i in range(0, len(xs), 2)]
        right = jnp.concatenate(right, axis=0).reshape(-1, share)
        columns = dot(left, right, 0, 0)
        columns = columns.astype(BF16)
        z = jnp.stack(
            [dot(x.reshape(SLICES * tok, share), columns, 1, 1).astype(BF16) for x in xs[:2]]
        )
        z = z.reshape(2, SLICES, tok, lanes).swapaxes(0, 1)
    z = along(z)
    columns, z = lax.optimization_barrier((columns, z))

    z = jnp.sum(z.astype(F32), axis=0).reshape(2 * tok, lanes)
    pairs = pairs.reshape(2 * tok, 2 * top)
    ids = pairs[:, :top].reshape(2 * rows, 1).astype(jnp.int32)
    probs = pairs[:, top:].reshape(2 * rows, 1)
    block = jnp.arange(lanes, dtype=jnp.int32) // rank * groups + (core if groups == 2 else 0)
    spread = jnp.where(ids == block, jnp.repeat(z, top, axis=0) * probs, 0.0).astype(BF16).T
    spread = spread.reshape(SLICES, low, rank, 2 * rows)
    lower = me // 2 % low
    spread = [
        lax.dynamic_index_in_dim(spread, r ^ lower, 1, False).reshape(SLICES * rank, 2 * rows)
        for r in range(low)
    ]
    piece = part // CHUNKS
    sums = []
    for chunk in range(CHUNKS):
        cut = slice(chunk * piece, (chunk + 1) * piece)
        terms = [
            (dot(s[:, :rows], mine[:, cut], 1, 0) + dot(s[:, rows:], other[:, cut], 1, 0))
            .astype(BF16)
            .reshape(SLICES, rank, piece)
            for s in spread
        ]
        step = 2
        while len(terms) > 1:
            terms = [
                (keep.astype(F32) + exchange(send, step).astype(F32)).astype(BF16)
                for keep, send in zip(terms[::2], terms[1::2])
            ]
            step *= 2
        sums.append(terms[0])
    totals = [jnp.sum(along(s).astype(F32), axis=0) for s in sums]

    columns, _ = lax.optimization_barrier((columns, sums[0]))
    parts = columns.reshape(SLICES, n_expert // SLICES // groups, rank, share)
    parts = lax.dynamic_index_in_dim(parts, own % (n_expert // SLICES) // groups, 1, False)
    range_rows = along(parts).swapaxes(0, 1).reshape(rank, width).astype(F32)
    gram = lax.dot_general(range_rows, range_rows, (((1,), (1,)), ((), ())), precision=HIGH)
    lower = jnp.linalg.cholesky(gram)
    inverse = jax.scipy.linalg.solve_triangular(lower, jnp.eye(rank, dtype=F32), lower=True)
    kept = lax.dynamic_slice_in_dim(range_rows, half * (width // n_dp), width // n_dp, axis=1)
    basis = jnp.dot(inverse * math.sqrt(width), kept, precision=HIGH)
    coeffs = [jnp.dot(inverse * scale, total, precision=HIGH) for total in totals]
    return basis[None], jnp.concatenate(coeffs, axis=1)[None]


def solution(mesh):
    in_specs = (
        P(("group", "expert", "dp"), None),
        P(("group", "expert", "dp"), None),
        P(("group", "expert", "dp"), None),
        P(("group", "expert", "dp"), None, None),
        P(),
    )
    out_specs = (P(("group", "expert"), None, "dp"), P(("group", "expert"), None, "dp"))
    return jax.shard_map(shards, mesh=mesh, in_specs=in_specs, out_specs=out_specs, check_vma=False)
```

```python
import functools
import math

import jax
import jax.numpy as jnp
from jax import lax
from jax.experimental import pallas as pl
from jax.experimental.pallas import tpu as pltpu
from jax.sharding import PartitionSpec as P

AXES = ("expert", "dp")
HIGH = lax.Precision.HIGHEST
CHUNKS = 2
SLICES = 4
LIMIT = 24 * 1024 * 1024
VMEM = pl.BlockSpec(memory_space=pltpu.VMEM)
SMEM = pl.BlockSpec(memory_space=pltpu.SMEM)
BF16 = jnp.bfloat16
F32 = jnp.float32


def dot(left, right, left_dim, right_dim):
    dims = (((left_dim,), (right_dim,)), ((), ()))
    return lax.dot_general(left, right, dims, preferred_element_type=F32)


def iota(shape, dim):
    return lax.broadcasted_iota(jnp.int32, shape, dim)


def call(body, shapes, flops, size, *args, spaces=None):
    return pl.pallas_call(
        body,
        out_shape=shapes,
        in_specs=spaces or [VMEM] * len(args),
        out_specs=jax.tree.map(lambda _: VMEM, shapes),
        compiler_params=pltpu.CompilerParams(vmem_limit_bytes=LIMIT),
        cost_estimate=pl.CostEstimate(flops=flops, bytes_accessed=size, transcendentals=0),
    )(*args)


def pair_columns(ids, probs):
    top, tok = ids.shape
    rows = tok * top
    pick = (iota((rows, tok), 0) // top == iota((rows, tok), 1)).astype(BF16)
    here = iota((rows, top), 0) % top == iota((rows, top), 1)
    names = dot(pick, ids.astype(BF16), 1, 1)
    weights, rest = jnp.zeros((rows, top), F32), probs
    for _ in range(3):
        piece = rest.astype(BF16)
        weights = weights + dot(pick, piece, 1, 1)
        rest = rest - piece.astype(F32)
    names = jnp.sum(jnp.where(here, names, 0.0), axis=1, keepdims=True)
    weights = jnp.sum(jnp.where(here, weights, 0.0), axis=1, keepdims=True)
    return names, weights


def y_kernel(groups, core, cot, sketch, pairs, *outs):
    rows = cot.shape[0]
    tok = pairs.shape[1]
    top = rows // tok
    rank = sketch.shape[0]
    lanes = outs[0].shape[1]
    high = sketch[...].astype(BF16)
    low = (sketch[...] - high.astype(F32)).astype(BF16)
    pair = dot(cot[...], high, 1, 1) + dot(cot[...], low, 1, 1)
    names, weights = pair_columns(pairs[:top], pairs[top:])
    pair = (pair * weights).astype(BF16)
    lane = iota((rank, lanes), 1)
    tiled = dot(pair, (iota((rank, lanes), 0) == lane % rank).astype(BF16), 1, 0)
    block = iota((1, lanes), 1) // rank * groups
    for i, out in enumerate(outs):
        name = block + (core[0] ^ i) if groups == 2 else block
        y = jnp.where(names == name.astype(F32), tiled, 0.0)
        out[...] = jnp.sum(y.reshape(tok, top, lanes), axis=1).astype(BF16)


def z_kernel(n, *refs):
    xs, ys, columns, zs = refs[: 2 * n], refs[2 * n : 3 * n], refs[3 * n], refs[3 * n + 1 :]
    total = 0.0
    for b in range(n):
        for core in range(2):
            y = ys[b][:, core].reshape(-1, columns.shape[0])
            total = total + dot(y, xs[2 * b + core][...], 0, 0)
    total = total.astype(BF16)
    columns[...] = total
    tok = zs[0].shape[1]
    each = xs[0].shape[0] // tok
    for core in range(2):
        for b in range(len(zs) // each):
            part = dot(xs[2 * b + core][...], total, 1, 1).astype(BF16)
            for i in range(each):
                zs[b * each + i][core] = part[i * tok : (i + 1) * tok]


def spread_kernel(groups, at, *refs):
    zs, pairs, outs = refs[:SLICES], refs[SLICES : SLICES + 2], refs[SLICES + 2 : -1]
    work = refs[-1]
    _, tok, lanes = zs[0].shape
    top = pairs[0].shape[0] // 2
    rows = tok * top
    rank = outs[0].shape[0] // SLICES
    block = iota((1, lanes), 1) // rank * groups + (at[0] if groups == 2 else 0)
    for core in range(2):
        z = zs[0][core].astype(F32)
        for other in zs[1:]:
            z = z + other[core].astype(F32)
        names, weights = pair_columns(pairs[core][:top], pairs[core][top:])
        z = jnp.broadcast_to(z[:, None], (tok, top, lanes)).reshape(rows, lanes)
        z = jnp.where(names == block.astype(F32), z * weights, 0.0).astype(BF16)
        work[:, core * rows : (core + 1) * rows] = z.T
    for r, out in enumerate(outs):
        for j in range(SLICES):
            start = pl.multiple_of((j * len(outs) + (at[1] ^ r)) * rank, rank)
            out[j * rank : (j + 1) * rank] = work[pl.ds(start, rank)]


def part_kernel(spread, mine, other, *outs):
    rows = mine.shape[0]
    start = 0
    for out in outs:
        size = out.shape[1]
        part = dot(spread[:, :rows], mine[:, start : start + size], 1, 0)
        part = part + dot(spread[:, rows:], other[:, start : start + size], 1, 0)
        out[...] = part.astype(BF16)
        start += size


def shards(tokens, expert_ids, route_probs, cotangents, sketch):
    n_expert = lax.axis_size("expert")
    n_dp = lax.axis_size("dp")
    count = n_expert * n_dp
    line = count // SLICES
    low = line // 2
    groups = 2 // n_dp
    tok, width = tokens.shape
    top = expert_ids.shape[1]
    hidden, rank = sketch.shape
    rows = tok * top
    share = width // SLICES
    lanes = count // 2 * rank
    part = hidden // n_dp
    scale = 1.0 / math.sqrt(rows)
    own = lax.axis_index("expert")
    half = lax.axis_index("dp")
    me = lax.axis_index(AXES)
    core = me % 2
    place = me // line
    lower = me // 2 % low
    shape = jax.ShapeDtypeStruct

    def exchange(block, step):
        return lax.ppermute(block, AXES, [(i, i ^ step) for i in range(count)])

    cuts = [
        lax.dynamic_slice_in_dim(tokens, (place ^ j) * share, share, axis=1) for j in range(SLICES)
    ]
    cuts = cuts[:1] + [exchange(cuts[j], j * line) for j in range(1, SLICES)]
    xs = [jnp.concatenate(cuts[i : i + 2], axis=0) for i in range(0, SLICES, 2)]

    cot = cotangents.reshape(rows, hidden)
    if n_dp > 1:
        mine = lax.dynamic_slice_in_dim(cot, half * part, part, axis=1)
        other = exchange(lax.dynamic_slice_in_dim(cot, (1 - half) * part, part, axis=1), 1)
    else:
        mine, other = cot, exchange(cot, 1)
    pairs = jnp.concatenate([expert_ids.T.astype(F32), route_probs.T], axis=0)
    pairs = [pairs, exchange(pairs, 1)]

    y = call(
        functools.partial(y_kernel, groups),
        [shape((tok, lanes), BF16)] * groups,
        4 * rows * hidden * rank,
        2 * rows * hidden,
        core.reshape(1),
        cot,
        sketch.T,
        pairs[0],
        spaces=[SMEM] + [VMEM] * 3,
    )
    y = jnp.stack([y[0], exchange(y[-1], 1)])
    ys = [y] + [exchange(y, j * line) for j in range(1, SLICES)]
    ys = [jnp.stack(ys[i : i + 2]) for i in range(0, SLICES, 2)]
    step = 2
    while step < line:
        ys = ys + [exchange(b, step) for b in ys]
        xs = xs + [exchange(b, step) for b in xs]
        step *= 2
    xs = [b for x in xs for b in (x, exchange(x, 1))]

    if n_dp == 1:
        columns, *zs = call(
            functools.partial(z_kernel, len(ys)),
            [shape((lanes, share), BF16)] + [shape((2, tok, lanes), BF16)] * SLICES,
            2 * count * tok * lanes * share * 3 // 2,
            2 * count * tok * (lanes + share),
            *xs,
            *ys,
        )
    else:
        left = jnp.concatenate(ys, axis=0).reshape(-1, lanes)
        right = [jnp.stack([xs[i], xs[i + 1]]) for i in range(0, len(xs), 2)]
        right = jnp.stack(right).reshape(-1, 2, 2, tok, share).swapaxes(1, 2)
        columns = dot(left, right.reshape(-1, share), 0, 0).astype(BF16)
        zs = [
            jnp.stack([dot(x[i : i + tok], columns, 1, 1).astype(BF16) for x in xs[b : b + 2]])
            for b in (0, 2)
            for i in (0, tok)
        ]
    zs = zs[:1] + [exchange(zs[j], j * line) for j in range(1, SLICES)]

    spread = pl.pallas_call(
        functools.partial(spread_kernel, groups),
        out_shape=[shape((SLICES * rank, 2 * rows), BF16)] * low,
        in_specs=[SMEM] + [VMEM] * (SLICES + 2),
        out_specs=[VMEM] * low,
        scratch_shapes=[pltpu.VMEM((lanes, 2 * rows), BF16)],
        compiler_params=pltpu.CompilerParams(vmem_limit_bytes=LIMIT),
        cost_estimate=pl.CostEstimate(
            flops=0, bytes_accessed=8 * rows * lanes, transcendentals=0
        ),
    )(jnp.stack([core, lower]), *zs, *pairs)
    piece = part // CHUNKS
    terms = [
        call(
            part_kernel,
            [shape((SLICES * rank, piece), BF16)] * CHUNKS,
            4 * rows * SLICES * rank * part,
            4 * rows * part,
            s,
            mine,
            other,
        )
        for s in spread[::-1]
    ][::-1]
    sums = []
    for chunk in range(CHUNKS):
        blocks = [term[chunk].reshape(SLICES, rank, piece) for term in terms]
        step = 2
        while len(blocks) > 1:
            blocks = [
                (keep.astype(F32) + exchange(send, step).astype(F32)).astype(BF16)
                for keep, send in zip(blocks[::2], blocks[1::2])
            ]
            step *= 2
        sums.append(blocks[0])
    totals = []
    for block in sums:
        gone = [
            exchange(lax.dynamic_index_in_dim(block, place ^ j, 0, False), j * line)
            for j in range(1, SLICES)
        ]
        total = lax.dynamic_index_in_dim(block, place, 0, False).astype(F32)
        for other in gone:
            total = total + other.astype(F32)
        totals.append(total)

    columns, _ = lax.optimization_barrier((columns, terms[0]))
    parts = columns.reshape(SLICES, n_expert // SLICES // groups, rank, share)
    parts = lax.dynamic_index_in_dim(parts, own % (n_expert // SLICES) // groups, 1, False)
    parts = [lax.dynamic_index_in_dim(parts, place ^ j, 0, False) for j in range(SLICES)]
    parts = jnp.stack(parts[:1] + [exchange(parts[j], j * line) for j in range(1, SLICES)])
    parts = [lax.dynamic_index_in_dim(parts, place ^ j, 0, False) for j in range(SLICES)]
    range_rows = jnp.concatenate(parts, axis=1).astype(F32)
    gram = lax.dot_general(range_rows, range_rows, (((1,), (1,)), ((), ())), precision=HIGH)
    lower = jnp.linalg.cholesky(gram)
    inverse = jax.scipy.linalg.solve_triangular(lower, jnp.eye(rank, dtype=F32), lower=True)
    kept = lax.dynamic_slice_in_dim(range_rows, half * (width // n_dp), width // n_dp, axis=1)
    basis = jnp.dot(inverse * math.sqrt(width), kept, precision=HIGH)
    coeffs = [jnp.dot(inverse * scale, total, precision=HIGH) for total in totals]
    return basis[None], jnp.concatenate(coeffs, axis=1)[None]


def solution(mesh):
    in_specs = (
        P(("group", "expert", "dp"), None),
        P(("group", "expert", "dp"), None),
        P(("group", "expert", "dp"), None),
        P(("group", "expert", "dp"), None, None),
        P(),
    )
    out_specs = (P(("group", "expert"), None, "dp"), P(("group", "expert"), None, "dp"))
    return jax.shard_map(shards, mesh=mesh, in_specs=in_specs, out_specs=out_specs, check_vma=False)
```

```python
import functools
import math

import jax
import jax.numpy as jnp
from jax import lax
from jax.experimental import pallas as pl
from jax.experimental.pallas import tpu as pltpu
from jax.sharding import PartitionSpec as P

AXES = ("expert", "dp")
HIGH = lax.Precision.HIGHEST
CHUNKS = 2
SLICES = 4
LIMIT = 24 * 1024 * 1024
VMEM = pl.BlockSpec(memory_space=pltpu.VMEM)
SMEM = pl.BlockSpec(memory_space=pltpu.SMEM)
ANY = pl.BlockSpec(memory_space=pl.ANY)
BF16 = jnp.bfloat16
F32 = jnp.float32


def dot(left, right, left_dim, right_dim):
    dims = (((left_dim,), (right_dim,)), ((), ()))
    return lax.dot_general(left, right, dims, preferred_element_type=F32)


def iota(shape, dim):
    return lax.broadcasted_iota(jnp.int32, shape, dim)


def call(body, shapes, flops, size, spaces, scratch, *args):
    return pl.pallas_call(
        body,
        out_shape=shapes,
        in_specs=spaces,
        out_specs=[VMEM] * len(shapes),
        scratch_shapes=scratch,
        compiler_params=pltpu.CompilerParams(vmem_limit_bytes=LIMIT),
        cost_estimate=pl.CostEstimate(flops=flops, bytes_accessed=size, transcendentals=0),
    )(*args)


def pair_columns(ids, probs):
    top, tok = ids.shape
    rows = tok * top
    pick = (iota((rows, tok), 0) // top == iota((rows, tok), 1)).astype(BF16)
    here = iota((rows, top), 0) % top == iota((rows, top), 1)
    names = dot(pick, ids.astype(BF16), 1, 1)
    weights, rest = jnp.zeros((rows, top), F32), probs
    for _ in range(3):
        piece = rest.astype(BF16)
        weights = weights + dot(pick, piece, 1, 1)
        rest = rest - piece.astype(F32)
    names = jnp.sum(jnp.where(here, names, 0.0), axis=1, keepdims=True)
    weights = jnp.sum(jnp.where(here, weights, 0.0), axis=1, keepdims=True)
    return names, weights


def load(pairs, sems):
    copies = [pltpu.make_async_copy(src, dst, sems.at[i]) for i, (src, dst) in enumerate(pairs)]
    for copy in copies:
        copy.start()
    return copies


def y_kernel(groups, core, cot_at, sketch_at, ids_at, probs_at, *refs):
    outs, pairs, (cot, sketch, ids, probs, sems) = refs[:groups], refs[groups], refs[groups + 1 :]
    rows = cot.shape[0]
    tok = pairs.shape[1]
    top = rows // tok
    rank = sketch.shape[0]
    lanes = outs[0].shape[1]
    parts = 4
    piece = rows // parts
    sources = [(ids_at, ids), (probs_at, probs), (sketch_at, sketch)]
    for i in range(parts):
        cut = pl.ds(i * piece, piece)
        sources.append((cot_at.at[cut], cot.at[cut]))
    copies = load(sources, sems)
    copies[0].wait()
    copies[1].wait()
    pairs[:top] = ids[...].astype(F32)
    pairs[top:] = probs[...]
    names, weights = pair_columns(pairs[:top], pairs[top:])
    copies[2].wait()
    high = sketch[...].astype(BF16)
    low = (sketch[...] - high.astype(F32)).astype(BF16)
    lane = iota((rank, lanes), 1)
    tile = (iota((rank, lanes), 0) == lane % rank).astype(BF16)
    block = iota((1, lanes), 1) // rank * groups
    for i in range(parts):
        copies[3 + i].wait()
        here = slice(i * piece, (i + 1) * piece)
        there = slice(i * piece // top, (i + 1) * piece // top)
        pair = dot(cot[here], high, 1, 1) + dot(cot[here], low, 1, 1)
        tiled = dot((pair * weights[here]).astype(BF16), tile, 1, 0)
        for j, out in enumerate(outs):
            name = block + (core[0] ^ j) if groups == 2 else block
            y = jnp.where(names[here] == name.astype(F32), tiled, 0.0)
            out[there] = jnp.sum(y.reshape(piece // top, top, lanes), axis=1).astype(BF16)


def z_kernel(n, *refs):
    xs, ys, columns, zs = refs[: 2 * n], refs[2 * n : -8], refs[-8], refs[-7:-3]
    x, y, sems = refs[-3:]
    rows = xs[0].shape[0]
    tok = zs[0].shape[1]
    each = rows // tok
    sources = [(x_at, x.at[pl.ds(i * rows, rows)]) for i, x_at in enumerate(xs)]
    for b, y_at in enumerate(ys):
        for i in range(SLICES // each):
            for core in range(2):
                block = 2 * (b * (SLICES // each) + i) + core
                sources.append((y_at.at[pl.ds(i * each, each), core], y.at[block]))
    for copy in load(sources, sems):
        copy.wait()
    total = dot(y[...].reshape(x.shape[0], -1), x[...], 0, 0).astype(BF16)
    columns[...] = total
    part = dot(x[: 2 * SLICES * tok], total, 1, 1).astype(BF16)
    for j in range(SLICES):
        for core in range(2):
            start = ((j // each * 2 + core) * each + j % each) * tok
            zs[j][core] = part[start : start + tok]


def spread_rows(groups, at, zs, pairs, work, spread, low, rank):
    _, tok, lanes = zs[0].shape
    top = pairs[0].shape[0] // 2
    rows = tok * top
    block = iota((1, lanes), 1) // rank * groups + (at[0] if groups == 2 else 0)
    for core in range(2):
        z = zs[0][core].astype(F32)
        for other in zs[1:]:
            z = z + other[core].astype(F32)
        names, weights = pair_columns(pairs[core][:top], pairs[core][top:])
        z = jnp.broadcast_to(z[:, None], (tok, top, lanes)).reshape(rows, lanes)
        z = jnp.where(names == block.astype(F32), z * weights, 0.0).astype(BF16)
        work[:, core * rows : (core + 1) * rows] = z.T
    for r in range(low):
        for j in range(SLICES):
            start = pl.multiple_of((j * low + (at[1] ^ r)) * rank, rank)
            spread[(r * SLICES + j) * rank : (r * SLICES + j + 1) * rank] = work[
                pl.ds(start, rank)
            ]


def cot_copies(start, mine, other, cot, sems):
    rows, size = mine.shape[0], cot.shape[1]
    cut = pl.ds(start, size)
    sources = [(mine.at[:, cut], cot.at[pl.ds(0, rows)])]
    return load(sources + [(other.at[:, cut], cot.at[pl.ds(rows, rows)])], sems)


def terms(spread, cot, outs):
    size = outs[0].shape[0]
    part = dot(spread[...], cot[...], 1, 0).astype(BF16)
    for r, out in enumerate(outs):
        out[...] = part[r * size : (r + 1) * size]


def first_kernel(groups, at, z0, z1, z2, z3, own, pair, mine, other, spread, *refs):
    outs, (work, cot, sems) = refs[:-3], refs[-3:]
    copies = cot_copies(0, mine, other, cot, sems)
    rank = outs[0].shape[0] // SLICES
    spread_rows(groups, at, (z0, z1, z2, z3), (own, pair), work, spread, len(outs), rank)
    for copy in copies:
        copy.wait()
    terms(spread, cot, outs)


def next_kernel(start, spread, mine, other, *refs):
    outs, (cot, sems) = refs[:-2], refs[-2:]
    for copy in cot_copies(start, mine, other, cot, sems):
        copy.wait()
    terms(spread, cot, outs)


def shards(tokens, expert_ids, route_probs, cotangents, sketch):
    n_expert = lax.axis_size("expert")
    n_dp = lax.axis_size("dp")
    count = n_expert * n_dp
    line = count // SLICES
    low = line // 2
    groups = 2 // n_dp
    tok, width = tokens.shape
    top = expert_ids.shape[1]
    hidden, rank = sketch.shape
    rows = tok * top
    share = width // SLICES
    lanes = count // 2 * rank
    part = hidden // n_dp
    scale = 1.0 / math.sqrt(rows)
    own = lax.axis_index("expert")
    half = lax.axis_index("dp")
    me = lax.axis_index(AXES)
    core = me % 2
    place = me // line
    lower = me // 2 % low
    shape = jax.ShapeDtypeStruct

    def exchange(block, step):
        return lax.ppermute(block, AXES, [(i, i ^ step) for i in range(count)])

    cuts = [
        lax.dynamic_slice_in_dim(tokens, (place ^ j) * share, share, axis=1) for j in range(SLICES)
    ]
    cuts = cuts[:1] + [exchange(cuts[j], j * line) for j in range(1, SLICES)]
    xs = [jnp.concatenate(cuts[i : i + 2], axis=0) for i in range(0, SLICES, 2)]

    cot = cotangents.reshape(rows, hidden)
    if n_dp > 1:
        mine = lax.dynamic_slice_in_dim(cot, half * part, part, axis=1)
        other = exchange(lax.dynamic_slice_in_dim(cot, (1 - half) * part, part, axis=1), 1)
    else:
        mine, other = cot, exchange(cot, 1)

    *y, pairs = call(
        functools.partial(y_kernel, groups),
        [shape((tok, lanes), BF16)] * groups + [shape((2 * top, tok), F32)],
        4 * rows * hidden * rank,
        2 * rows * hidden,
        [SMEM] + [ANY] * 4,
        [
            pltpu.VMEM((rows, hidden), BF16),
            pltpu.VMEM((rank, hidden), F32),
            pltpu.VMEM((top, tok), jnp.int32),
            pltpu.VMEM((top, tok), F32),
            pltpu.SemaphoreType.DMA((7,)),
        ],
        core.reshape(1),
        cot,
        sketch.T,
        expert_ids.T,
        route_probs.T,
    )
    send, xs = lax.optimization_barrier((y[-1], xs))
    pairs = [pairs, exchange(pairs, 1)]
    y = jnp.stack([y[0], exchange(send, 1)])
    ys = [jnp.stack([y] + [exchange(y, j * line) for j in range(1, SLICES)])]
    step = 2
    while step < line:
        ys = ys + [exchange(b, step) for b in ys]
        xs = xs + [exchange(b, step) for b in xs]
        step *= 2
    xs = [b for x in xs for b in (x, exchange(x, 1))]

    if n_dp == 1:
        columns, *zs = call(
            functools.partial(z_kernel, len(xs) // 2),
            [shape((lanes, share), BF16)] + [shape((2, tok, lanes), BF16)] * SLICES,
            2 * count * tok * lanes * share * 3 // 2,
            2 * count * tok * (lanes + share),
            [ANY] * (len(xs) + len(ys)),
            [
                pltpu.VMEM((count * tok, share), BF16),
                pltpu.VMEM((len(xs), 2, tok, lanes), BF16),
                pltpu.SemaphoreType.DMA((2 * len(xs),)),
            ],
            *xs,
            *ys,
        )
    else:
        left = jnp.concatenate(ys, axis=0).reshape(-1, lanes)
        right = [jnp.stack([xs[i], xs[i + 1]]) for i in range(0, len(xs), 2)]
        right = jnp.stack(right).reshape(-1, 2, 2, tok, share).swapaxes(1, 2)
        columns = dot(left, right.reshape(-1, share), 0, 0).astype(BF16)
        zs = [
            jnp.stack([dot(x[i : i + tok], columns, 1, 1).astype(BF16) for x in xs[b : b + 2]])
            for b in (0, 2)
            for i in (0, tok)
        ]
    zs = zs[:1] + [exchange(zs[j], j * line) for j in range(1, SLICES)]

    piece = part // CHUNKS
    flops = 4 * rows * SLICES * rank * piece
    outs = [shape((SLICES * rank, piece), BF16)] * low
    work = [pltpu.VMEM((2 * rows, piece), BF16), pltpu.SemaphoreType.DMA((2,))]
    spread, *blocks = call(
        functools.partial(first_kernel, groups),
        [shape((lanes, 2 * rows), BF16)] + outs,
        flops,
        4 * rows * piece,
        [SMEM] + [VMEM] * (SLICES + 2) + [ANY] * 2,
        [pltpu.VMEM((lanes, 2 * rows), BF16)] + work,
        jnp.stack([core, lower]),
        *zs,
        *pairs,
        mine,
        other,
    )
    chunks = [blocks]
    for chunk in range(1, CHUNKS):
        chunks.append(
            call(
                functools.partial(next_kernel, chunk * piece),
                outs,
                flops,
                4 * rows * piece,
                [VMEM] + [ANY] * 2,
                work,
                spread,
                mine,
                other,
            )
        )
    sums = []
    for chunk in chunks:
        blocks = [term.reshape(SLICES, rank, piece) for term in chunk]
        step = 2
        while len(blocks) > 1:
            blocks = [
                (keep.astype(F32) + exchange(send, step).astype(F32)).astype(BF16)
                for keep, send in zip(blocks[::2], blocks[1::2])
            ]
            step *= 2
        sums.append(blocks[0])
    totals = []
    for block in sums:
        gone = [
            exchange(lax.dynamic_index_in_dim(block, place ^ j, 0, False), j * line)
            for j in range(1, SLICES)
        ]
        total = lax.dynamic_index_in_dim(block, place, 0, False).astype(F32)
        for other in gone:
            total = total + other.astype(F32)
        totals.append(total)

    columns, _ = lax.optimization_barrier((columns, chunks[-1][0]))
    parts = columns.reshape(SLICES, n_expert // SLICES // groups, rank, share)
    parts = lax.dynamic_index_in_dim(parts, own % (n_expert // SLICES) // groups, 1, False)
    parts = [lax.dynamic_index_in_dim(parts, place ^ j, 0, False) for j in range(SLICES)]
    parts = jnp.stack(parts[:1] + [exchange(parts[j], j * line) for j in range(1, SLICES)])
    parts = [lax.dynamic_index_in_dim(parts, place ^ j, 0, False) for j in range(SLICES)]
    range_rows = jnp.concatenate(parts, axis=1).astype(F32)
    range_rows, _ = lax.optimization_barrier((range_rows, sums[0]))
    gram = lax.dot_general(range_rows, range_rows, (((1,), (1,)), ((), ())), precision=HIGH)
    lower = jnp.linalg.cholesky(gram)
    lower, _ = lax.optimization_barrier((lower, sums[-1]))
    inverse = jax.scipy.linalg.solve_triangular(lower, jnp.eye(rank, dtype=F32), lower=True)
    kept = lax.dynamic_slice_in_dim(range_rows, half * (width // n_dp), width // n_dp, axis=1)
    basis = jnp.dot(inverse * math.sqrt(width), kept, precision=HIGH)
    coeffs = [jnp.dot(inverse * scale, total, precision=HIGH) for total in totals]
    return basis[None], jnp.concatenate(coeffs, axis=1)[None]


def solution(mesh):
    in_specs = (
        P(("group", "expert", "dp"), None),
        P(("group", "expert", "dp"), None),
        P(("group", "expert", "dp"), None),
        P(("group", "expert", "dp"), None, None),
        P(),
    )
    out_specs = (P(("group", "expert"), None, "dp"), P(("group", "expert"), None, "dp"))
    return jax.shard_map(shards, mesh=mesh, in_specs=in_specs, out_specs=out_specs, check_vma=False)
```

```python
import functools
import math

import jax
import jax.numpy as jnp
from jax import lax
from jax.experimental import pallas as pl
from jax.experimental.pallas import tpu as pltpu
from jax.sharding import PartitionSpec as P

AXES = ("expert", "dp")
HIGH = lax.Precision.HIGHEST
CHUNKS = 2
SLICES = 4
LIMIT = 12 * 1024 * 1024
VMEM = pl.BlockSpec(memory_space=pltpu.VMEM)
SMEM = pl.BlockSpec(memory_space=pltpu.SMEM)
HBM = pl.BlockSpec(memory_space=pltpu.HBM)
BF16 = jnp.bfloat16
F32 = jnp.float32


def dot(left, right, left_dim, right_dim):
    dims = (((left_dim,), (right_dim,)), ((), ()))
    return lax.dot_general(left, right, dims, preferred_element_type=F32)


def iota(shape, dim):
    return lax.broadcasted_iota(jnp.int32, shape, dim)


def call(body, shapes, flops, size, spaces, scratch, *args):
    return pl.pallas_call(
        body,
        out_shape=shapes,
        in_specs=spaces,
        out_specs=[VMEM] * len(shapes),
        scratch_shapes=scratch,
        compiler_params=pltpu.CompilerParams(vmem_limit_bytes=LIMIT),
        cost_estimate=pl.CostEstimate(flops=flops, bytes_accessed=size, transcendentals=0),
    )(*args)


def pair_columns(ids, probs):
    top, tok = ids.shape
    rows = tok * top
    pick = (iota((rows, tok), 0) // top == iota((rows, tok), 1)).astype(BF16)
    here = iota((rows, top), 0) % top == iota((rows, top), 1)
    names = dot(pick, ids.astype(BF16), 1, 1)
    weights, rest = jnp.zeros((rows, top), F32), probs
    for _ in range(3):
        piece = rest.astype(BF16)
        weights = weights + dot(pick, piece, 1, 1)
        rest = rest - piece.astype(F32)
    names = jnp.sum(jnp.where(here, names, 0.0), axis=1, keepdims=True)
    weights = jnp.sum(jnp.where(here, weights, 0.0), axis=1, keepdims=True)
    return names, weights


def load(pairs, sems):
    copies = [pltpu.make_async_copy(src, dst, sems.at[i]) for i, (src, dst) in enumerate(pairs)]
    for copy in copies:
        copy.start()
    return copies


def y_kernel(groups, core, cot_at, sketch_at, ids_at, probs_at, *refs):
    outs, pairs, (cot, sketch, ids, probs, sems) = refs[:groups], refs[groups], refs[groups + 1 :]
    rows = cot.shape[0]
    tok = pairs.shape[1]
    top = rows // tok
    rank = sketch.shape[0]
    lanes = outs[0].shape[1]
    parts = 4
    piece = rows // parts
    sources = [(ids_at, ids), (probs_at, probs), (sketch_at, sketch)]
    for i in range(parts):
        cut = pl.ds(i * piece, piece)
        sources.append((cot_at.at[cut], cot.at[cut]))
    copies = load(sources, sems)
    copies[0].wait()
    copies[1].wait()
    pairs[:top] = ids[...].astype(F32)
    pairs[top:] = probs[...]
    names, weights = pair_columns(pairs[:top], pairs[top:])
    copies[2].wait()
    high = sketch[...].astype(BF16)
    low = (sketch[...] - high.astype(F32)).astype(BF16)
    lane = iota((rank, lanes), 1)
    tile = (iota((rank, lanes), 0) == lane % rank).astype(BF16)
    block = iota((1, lanes), 1) // rank * groups
    for i in range(parts):
        copies[3 + i].wait()
        here = slice(i * piece, (i + 1) * piece)
        there = slice(i * piece // top, (i + 1) * piece // top)
        pair = dot(cot[here], high, 1, 1) + dot(cot[here], low, 1, 1)
        tiled = dot((pair * weights[here]).astype(BF16), tile, 1, 0)
        for j, out in enumerate(outs):
            name = block + (core[0] ^ j) if groups == 2 else block
            y = jnp.where(names[here] == name.astype(F32), tiled, 0.0)
            out[there] = jnp.sum(y.reshape(piece // top, top, lanes), axis=1).astype(BF16)


def z_kernel(n, *refs):
    xs, ys, columns, zs = refs[: 2 * n], refs[2 * n : -8], refs[-8], refs[-7:-3]
    x, y, sems = refs[-3:]
    rows = xs[0].shape[0]
    tok = zs[0].shape[1]
    each = rows // tok
    sources = [(x_at, x.at[pl.ds(i * rows, rows)]) for i, x_at in enumerate(xs)]
    for b, y_at in enumerate(ys):
        for i in range(SLICES // each):
            for core in range(2):
                block = 2 * (b * (SLICES // each) + i) + core
                sources.append((y_at.at[pl.ds(i * each, each), core], y.at[block]))
    for copy in load(sources, sems):
        copy.wait()
    total = dot(y[...].reshape(x.shape[0], -1), x[...], 0, 0).astype(BF16)
    columns[...] = total
    part = dot(x[: 2 * SLICES * tok], total, 1, 1).astype(BF16)
    for j in range(SLICES):
        for core in range(2):
            start = ((j // each * 2 + core) * each + j % each) * tok
            zs[j][core] = part[start : start + tok]


def spread_rows(groups, at, zs, pairs, work, spread, low, rank):
    _, tok, lanes = zs[0].shape
    top = pairs[0].shape[0] // 2
    rows = tok * top
    block = iota((1, lanes), 1) // rank * groups + (at[0] if groups == 2 else 0)
    for core in range(2):
        z = zs[0][core].astype(F32)
        for other in zs[1:]:
            z = z + other[core].astype(F32)
        names, weights = pair_columns(pairs[core][:top], pairs[core][top:])
        z = jnp.broadcast_to(z[:, None], (tok, top, lanes)).reshape(rows, lanes)
        z = jnp.where(names == block.astype(F32), z * weights, 0.0).astype(BF16)
        work[:, core * rows : (core + 1) * rows] = z.T
    for r in range(low):
        for j in range(SLICES):
            start = pl.multiple_of((j * low + (at[1] ^ r)) * rank, rank)
            spread[(r * SLICES + j) * rank : (r * SLICES + j + 1) * rank] = work[
                pl.ds(start, rank)
            ]


def cot_copies(start, mine, other, cot, sems):
    rows, size = mine.shape[0], cot.shape[1]
    cut = pl.ds(start, size)
    sources = [(mine.at[:, cut], cot.at[pl.ds(0, rows)])]
    return load(sources + [(other.at[:, cut], cot.at[pl.ds(rows, rows)])], sems)


def terms(spread, cot, outs):
    size = outs[0].shape[0]
    part = dot(spread[...], cot[...], 1, 0).astype(BF16)
    for r, out in enumerate(outs):
        out[...] = part[r * size : (r + 1) * size]


def first_kernel(groups, at, z0, z1, z2, z3, own, pair, mine, other, spread, *refs):
    outs, (work, cot, sems) = refs[:-3], refs[-3:]
    copies = cot_copies(0, mine, other, cot, sems)
    rank = outs[0].shape[0] // SLICES
    spread_rows(groups, at, (z0, z1, z2, z3), (own, pair), work, spread, len(outs), rank)
    for copy in copies:
        copy.wait()
    terms(spread, cot, outs)


def next_kernel(start, spread, mine, other, *refs):
    outs, (cot, sems) = refs[:-2], refs[-2:]
    for copy in cot_copies(start, mine, other, cot, sems):
        copy.wait()
    terms(spread, cot, outs)


def shards(tokens, expert_ids, route_probs, cotangents, sketch):
    n_expert = lax.axis_size("expert")
    n_dp = lax.axis_size("dp")
    count = n_expert * n_dp
    line = count // SLICES
    low = line // 2
    groups = 2 // n_dp
    tok, width = tokens.shape
    top = expert_ids.shape[1]
    hidden, rank = sketch.shape
    rows = tok * top
    share = width // SLICES
    lanes = count // 2 * rank
    part = hidden // n_dp
    scale = 1.0 / math.sqrt(rows)
    own = lax.axis_index("expert")
    half = lax.axis_index("dp")
    me = lax.axis_index(AXES)
    core = me % 2
    place = me // line
    lower = me // 2 % low
    shape = jax.ShapeDtypeStruct

    def exchange(block, step):
        return lax.ppermute(block, AXES, [(i, i ^ step) for i in range(count)])

    cuts = [
        lax.dynamic_slice_in_dim(tokens, (place ^ j) * share, share, axis=1) for j in range(SLICES)
    ]
    cuts = cuts[:1] + [exchange(cuts[j], j * line) for j in range(1, SLICES)]
    xs = [jnp.concatenate(cuts[i : i + 2], axis=0) for i in range(0, SLICES, 2)]

    cot = cotangents.reshape(rows, hidden)
    if n_dp > 1:
        mine = lax.dynamic_slice_in_dim(cot, half * part, part, axis=1)
        other = exchange(lax.dynamic_slice_in_dim(cot, (1 - half) * part, part, axis=1), 1)
    else:
        mine, other = cot, exchange(cot, 1)

    *y, pairs = call(
        functools.partial(y_kernel, groups),
        [shape((tok, lanes), BF16)] * groups + [shape((2 * top, tok), F32)],
        4 * rows * hidden * rank,
        2 * rows * hidden,
        [SMEM] + [HBM] * 4,
        [
            pltpu.VMEM((rows, hidden), BF16),
            pltpu.VMEM((rank, hidden), F32),
            pltpu.VMEM((top, tok), jnp.int32),
            pltpu.VMEM((top, tok), F32),
            pltpu.SemaphoreType.DMA((7,)),
        ],
        core.reshape(1),
        cot,
        sketch.T,
        expert_ids.T,
        route_probs.T,
    )
    send, xs = lax.optimization_barrier((y[-1], xs))
    pairs = [pairs, exchange(pairs, 1)]
    y = jnp.stack([y[0], exchange(send, 1)])
    ys = [jnp.stack([y] + [exchange(y, j * line) for j in range(1, SLICES)])]
    step = 2
    while step < line:
        ys = ys + [exchange(b, step) for b in ys]
        xs = xs + [exchange(b, step) for b in xs]
        step *= 2
    xs = [b for x in xs for b in (x, exchange(x, 1))]

    if n_dp == 1:
        columns, *zs = call(
            functools.partial(z_kernel, len(xs) // 2),
            [shape((lanes, share), BF16)] + [shape((2, tok, lanes), BF16)] * SLICES,
            2 * count * tok * lanes * share * 3 // 2,
            2 * count * tok * (lanes + share),
            [HBM] * (len(xs) + len(ys)),
            [
                pltpu.VMEM((count * tok, share), BF16),
                pltpu.VMEM((len(xs), 2, tok, lanes), BF16),
                pltpu.SemaphoreType.DMA((2 * len(xs),)),
            ],
            *xs,
            *ys,
        )
    else:
        left = jnp.concatenate(ys, axis=0).reshape(-1, lanes)
        right = [jnp.stack([xs[i], xs[i + 1]]) for i in range(0, len(xs), 2)]
        right = jnp.stack(right).reshape(-1, 2, 2, tok, share).swapaxes(1, 2)
        columns = dot(left, right.reshape(-1, share), 0, 0).astype(BF16)
        zs = [
            jnp.stack([dot(x[i : i + tok], columns, 1, 1).astype(BF16) for x in xs[b : b + 2]])
            for b in (0, 2)
            for i in (0, tok)
        ]
    zs = zs[:1] + [exchange(zs[j], j * line) for j in range(1, SLICES)]
    columns, _ = lax.optimization_barrier((columns, zs[1]))

    piece = part // CHUNKS
    flops = 4 * rows * SLICES * rank * piece
    outs = [shape((SLICES * rank, piece), BF16)] * low
    work = [pltpu.VMEM((2 * rows, piece), BF16), pltpu.SemaphoreType.DMA((2,))]
    spread, *blocks = call(
        functools.partial(first_kernel, groups),
        [shape((lanes, 2 * rows), BF16)] + outs,
        flops,
        4 * rows * piece,
        [SMEM] + [VMEM] * (SLICES + 2) + [HBM] * 2,
        [pltpu.VMEM((lanes, 2 * rows), BF16)] + work,
        jnp.stack([core, lower]),
        *zs,
        *pairs,
        mine,
        other,
    )
    chunks = [blocks]
    for chunk in range(1, CHUNKS):
        chunks.append(
            call(
                functools.partial(next_kernel, chunk * piece),
                outs,
                flops,
                4 * rows * piece,
                [VMEM] + [HBM] * 2,
                work,
                spread,
                mine,
                other,
            )
        )
    sums = []
    for chunk in chunks:
        blocks = [term.reshape(SLICES, rank, piece) for term in chunk]
        step = 2
        while len(blocks) > 1:
            blocks = [
                (keep.astype(F32) + exchange(send, step).astype(F32)).astype(BF16)
                for keep, send in zip(blocks[::2], blocks[1::2])
            ]
            step *= 2
        sums.append(blocks[0])
    totals = []
    for block in sums:
        gone = [
            exchange(lax.dynamic_index_in_dim(block, place ^ j, 0, False), j * line)
            for j in range(1, SLICES)
        ]
        total = lax.dynamic_index_in_dim(block, place, 0, False).astype(F32)
        for other in gone:
            total = total + other.astype(F32)
        totals.append(total)

    parts = columns.reshape(SLICES, n_expert // SLICES // groups, rank, share)
    parts = lax.dynamic_index_in_dim(parts, own % (n_expert // SLICES) // groups, 1, False)
    parts = [lax.dynamic_index_in_dim(parts, place ^ j, 0, False) for j in range(SLICES)]
    parts = jnp.stack(parts[:1] + [exchange(parts[j], j * line) for j in range(1, SLICES)])
    parts = [lax.dynamic_index_in_dim(parts, place ^ j, 0, False) for j in range(SLICES)]
    range_rows = jnp.concatenate(parts, axis=1).astype(F32)
    gram = lax.dot_general(range_rows, range_rows, (((1,), (1,)), ((), ())), precision=HIGH)
    lower = jnp.linalg.cholesky(gram)
    inverse = jax.scipy.linalg.solve_triangular(lower, jnp.eye(rank, dtype=F32), lower=True)
    kept = lax.dynamic_slice_in_dim(range_rows, half * (width // n_dp), width // n_dp, axis=1)
    basis = jnp.dot(inverse * math.sqrt(width), kept, precision=HIGH)
    coeffs = [jnp.dot(inverse * scale, total, precision=HIGH) for total in totals]
    return basis[None], jnp.concatenate(coeffs, axis=1)[None]


def solution(mesh):
    in_specs = (
        P(("group", "expert", "dp"), None),
        P(("group", "expert", "dp"), None),
        P(("group", "expert", "dp"), None),
        P(("group", "expert", "dp"), None, None),
        P(),
    )
    out_specs = (P(("group", "expert"), None, "dp"), P(("group", "expert"), None, "dp"))
    return jax.shard_map(shards, mesh=mesh, in_specs=in_specs, out_specs=out_specs, check_vma=False)
```

```python
import functools
import math

import jax
import jax.numpy as jnp
from jax import lax
from jax.experimental import pallas as pl
from jax.experimental.pallas import tpu as pltpu
from jax.sharding import PartitionSpec as P

AXES = ("expert", "dp")
CHUNKS = 2
SLICES = 4
LIMIT = 12 * 1024 * 1024
LARGE = 56 * 1024 * 1024
VMEM = pl.BlockSpec(memory_space=pltpu.VMEM)
SMEM = pl.BlockSpec(memory_space=pltpu.SMEM)
HBM = pl.BlockSpec(memory_space=pltpu.HBM)
BF16 = jnp.bfloat16
F32 = jnp.float32


def dot(left, right, left_dim, right_dim):
    dims = (((left_dim,), (right_dim,)), ((), ()))
    return lax.dot_general(left, right, dims, preferred_element_type=F32)


def iota(shape, dim):
    return lax.broadcasted_iota(jnp.int32, shape, dim)


def call(body, shapes, spaces, scratch, *args, limit=LIMIT):
    return pl.pallas_call(
        body,
        out_shape=shapes,
        in_specs=spaces,
        out_specs=[VMEM] * len(shapes),
        scratch_shapes=scratch,
        compiler_params=pltpu.CompilerParams(vmem_limit_bytes=limit),
        cost_estimate=pl.CostEstimate(flops=1, bytes_accessed=1, transcendentals=0),
    )(*args)


def pieces(value, count):
    terms = []
    for _ in range(count):
        terms.append(value.astype(BF16))
        value = value - terms[-1].astype(F32)
    return terms


def pack(z, columns):
    tiles = [z[:, i : i + 128] for i in range(0, z.shape[1], 128)]
    tiles += [columns[:, i : i + 128] for i in range(0, columns.shape[1], 128)]
    return jnp.concatenate(tiles, axis=0)


def unpack_z(rows, size, lanes):
    tiles = [rows[i * size : (i + 1) * size] for i in range(lanes // 128)]
    return jnp.concatenate(tiles, axis=1)


def unpack_columns(rows, start, rank):
    tiles = [rows[i : i + rank] for i in range(start, rows.shape[0], rank)]
    return jnp.concatenate(tiles, axis=1)


def pair_columns(ids, probs):
    top, tok = ids.shape
    rows = tok * top
    pick = (iota((rows, tok), 0) // top == iota((rows, tok), 1)).astype(BF16)
    here = iota((rows, top), 0) % top == iota((rows, top), 1)
    names = dot(pick, ids.astype(BF16), 1, 1)
    weights, rest = jnp.zeros((rows, top), F32), probs
    for _ in range(3):
        piece = rest.astype(BF16)
        weights = weights + dot(pick, piece, 1, 1)
        rest = rest - piece.astype(F32)
    names = jnp.sum(jnp.where(here, names, 0.0), axis=1, keepdims=True)
    weights = jnp.sum(jnp.where(here, weights, 0.0), axis=1, keepdims=True)
    return names, weights


def load(pairs, sems):
    copies = [pltpu.make_async_copy(src, dst, sems.at[i]) for i, (src, dst) in enumerate(pairs)]
    for copy in copies:
        copy.start()
    return copies


def y_kernel(groups, core, cot_at, sketch_at, ids_at, probs_at, *refs):
    outs, pairs, (cot, sketch, ids, probs, sems) = refs[:groups], refs[groups], refs[groups + 1 :]
    rows = cot.shape[0]
    tok = pairs.shape[1]
    top = rows // tok
    rank = sketch.shape[0]
    lanes = outs[0].shape[1]
    parts = 4
    piece = rows // parts
    sources = [(ids_at, ids), (probs_at, probs), (sketch_at, sketch)]
    for i in range(parts):
        cut = pl.ds(i * piece, piece)
        sources.append((cot_at.at[cut], cot.at[cut]))
    copies = load(sources, sems)
    copies[0].wait()
    copies[1].wait()
    pairs[:top] = ids[...].astype(F32)
    pairs[top:] = probs[...]
    names, weights = pair_columns(pairs[:top], pairs[top:])
    copies[2].wait()
    high = sketch[...].astype(BF16)
    low = (sketch[...] - high.astype(F32)).astype(BF16)
    lane = iota((rank, lanes), 1)
    tile = (iota((rank, lanes), 0) == lane % rank).astype(BF16)
    block = iota((1, lanes), 1) // rank * groups
    for i in range(parts):
        copies[3 + i].wait()
        here = slice(i * piece, (i + 1) * piece)
        there = slice(i * piece // top, (i + 1) * piece // top)
        pair = dot(cot[here], high, 1, 1) + dot(cot[here], low, 1, 1)
        tiled = dot((pair * weights[here]).astype(BF16), tile, 1, 0)
        for j, out in enumerate(outs):
            name = block + (core[0] ^ j) if groups == 2 else block
            y = jnp.where(names[here] == name.astype(F32), tiled, 0.0)
            out[there] = jnp.sum(y.reshape(piece // top, top, lanes), axis=1).astype(BF16)


def z_kernel(n, low, at, *refs):
    xs, ys, outs = refs[: 2 * n], refs[2 * n : -8], refs[-8:-4]
    x, y, columns, sems = refs[-4:]
    rows = xs[0].shape[0]
    _, _, tok, lanes = y.shape
    rank = lanes // (SLICES * low)
    each = rows // tok
    sources = [(x_at, x.at[pl.ds(i * rows, rows)]) for i, x_at in enumerate(xs)]
    for b, y_at in enumerate(ys):
        for i in range(SLICES // each):
            for core in range(2):
                block = 2 * (b * (SLICES // each) + i) + core
                sources.append((y_at.at[pl.ds(i * each, each), core], y.at[block]))
    for copy in load(sources, sems):
        copy.wait()
    total = dot(y[...].reshape(x.shape[0], -1), x[...], 0, 0).astype(BF16)
    columns[...] = total
    part = dot(x[: 2 * SLICES * tok], total, 1, 1).astype(BF16)
    for j, out in enumerate(outs):
        starts = [((j // each * 2 + core) * each + j % each) * tok for core in range(2)]
        z = jnp.concatenate([part[start : start + tok] for start in starts], axis=0)
        expert = (at[2] ^ j) * low + at[1]
        out[...] = pack(z, columns[pl.ds(pl.multiple_of(expert * rank, rank), rank)])


def inverse_kernel(start, at, p0, p1, p2, p3, inverse, basis, columns):
    rank = inverse.shape[0]
    _, _, share = columns.shape
    gram = 0.0
    for j, packed in enumerate((p0, p1, p2, p3)):
        block = unpack_columns(packed[...], start, rank)
        columns[at[2] ^ j] = block
        gram = gram + dot(block, block, 1, 1)
    row = iota((rank, 128), 0)
    lane = iota((rank, 128), 1)
    eye = (row + rank == lane).astype(F32)
    work = jnp.concatenate([gram, jnp.zeros((rank, 128 - rank), F32)], axis=1) + eye
    for first in range(0, rank, 4):
        heads = [work[first + i : first + i + 1] for i in range(4)]
        sides = [
            jnp.broadcast_to(work[:, first + i : first + i + 1], (rank, 128)) for i in range(4)
        ]
        taken = 0.0
        for i in range(4):
            pivot = first + i
            factor = sides[i] / sides[i][pivot : pivot + 1]
            factor = jnp.where(row > pivot, factor, 0.0)
            taken = taken + factor * heads[i]
            for k in range(i + 1, 4):
                sides[k] = sides[k] - factor * sides[k][pivot : pivot + 1]
                heads[k] = heads[k] - factor[first + k : first + k + 1] * heads[i]
        work = work - taken
    diagonal = jnp.sum(jnp.where(row == lane, work, 0.0), axis=1, keepdims=True)
    result = work[:, rank : 2 * rank] * lax.rsqrt(diagonal)
    inverse[...] = result
    scaled = result * math.sqrt(SLICES * share)
    scaled = jnp.concatenate(pieces(scaled, 3), axis=0)
    count = basis.shape[1] // share
    for i in range(count):
        out = dot(scaled, columns[at[3] * count + i], 1, 0)
        out = out[:rank] + out[rank : 2 * rank] + out[2 * rank :]
        basis[:, i * share : (i + 1) * share] = out


def coeffs_kernel(scale, inverse, *refs):
    blocks, out = refs[:-1], refs[-1]
    rank, size = blocks[0].shape
    left = jnp.concatenate(pieces(inverse[...] * scale, 3), axis=0)
    left = jnp.concatenate([left] * SLICES, axis=1)
    for i in range(len(blocks) // SLICES):
        right = jnp.concatenate([b[...] for b in blocks[i * SLICES : (i + 1) * SLICES]], axis=0)
        part = dot(left, right, 1, 0)
        out[:, i * size : (i + 1) * size] = part[:rank] + part[rank : 2 * rank] + part[2 * rank :]


def spread_rows(groups, at, packed, pairs, work, spread, low, rank):
    lanes = work.shape[0]
    tok = pairs[0].shape[1]
    top = pairs[0].shape[0] // 2
    rows = tok * top
    size = 2 * tok * lanes // 128
    total = 0.0
    for block in packed:
        total = total + unpack_z(block[:size], 2 * tok, lanes).astype(F32)
    block = iota((1, lanes), 1) // rank * groups + (at[0] if groups == 2 else 0)
    for core in range(2):
        z = total[core * tok : (core + 1) * tok]
        names, weights = pair_columns(pairs[core][:top], pairs[core][top:])
        z = jnp.broadcast_to(z[:, None], (tok, top, lanes)).reshape(rows, lanes)
        z = jnp.where(names == block.astype(F32), z * weights, 0.0).astype(BF16)
        work[:, core * rows : (core + 1) * rows] = z.T
    for r in range(low):
        for j in range(SLICES):
            start = pl.multiple_of((j * low + (at[1] ^ r)) * rank, rank)
            spread[(r * SLICES + j) * rank : (r * SLICES + j + 1) * rank] = work[
                pl.ds(start, rank)
            ]


def cot_copies(start, mine, other, cot, sems):
    rows, size = mine.shape[0], cot.shape[1]
    cut = pl.ds(start, size)
    sources = [(mine.at[:, cut], cot.at[pl.ds(0, rows)])]
    return load(sources + [(other.at[:, cut], cot.at[pl.ds(rows, rows)])], sems)


def terms(spread, cot, outs):
    size = outs[0].shape[0]
    part = dot(spread[...], cot[...], 1, 0).astype(BF16)
    for r, out in enumerate(outs):
        out[...] = part[r * size : (r + 1) * size]


def first_kernel(groups, at, z0, z1, z2, z3, own, pair, mine, other, spread, *refs):
    outs, (work, cot, sems) = refs[:-3], refs[-3:]
    copies = cot_copies(0, mine, other, cot, sems)
    rank = outs[0].shape[0] // SLICES
    spread_rows(groups, at, (z0, z1, z2, z3), (own, pair), work, spread, len(outs), rank)
    for copy in copies:
        copy.wait()
    terms(spread, cot, outs)


def next_kernel(start, spread, mine, other, *refs):
    outs, (cot, sems) = refs[:-2], refs[-2:]
    for copy in cot_copies(start, mine, other, cot, sems):
        copy.wait()
    terms(spread, cot, outs)


def shards(tokens, expert_ids, route_probs, cotangents, sketch):
    n_expert = lax.axis_size("expert")
    n_dp = lax.axis_size("dp")
    count = n_expert * n_dp
    line = count // SLICES
    low = line // 2
    groups = 2 // n_dp
    tok, width = tokens.shape
    top = expert_ids.shape[1]
    hidden, rank = sketch.shape
    rows = tok * top
    share = width // SLICES
    lanes = count // 2 * rank
    part = hidden // n_dp
    scale = 1.0 / math.sqrt(rows)
    half = lax.axis_index("dp")
    me = lax.axis_index(AXES)
    core = me % 2
    place = me // line
    at = jnp.stack([core, me // 2 % low, place, half])
    shape = jax.ShapeDtypeStruct

    def exchange(block, step):
        return lax.ppermute(block, AXES, [(i, i ^ step) for i in range(count)])

    cuts = [
        lax.dynamic_slice_in_dim(tokens, (place ^ j) * share, share, axis=1) for j in range(SLICES)
    ]
    cuts = cuts[:1] + [exchange(cuts[j], j * line) for j in range(1, SLICES)]
    xs = [jnp.concatenate(cuts[i : i + 2], axis=0) for i in range(0, SLICES, 2)]

    cot = cotangents.reshape(rows, hidden)
    if n_dp > 1:
        mine = lax.dynamic_slice_in_dim(cot, half * part, part, axis=1)
        other = exchange(lax.dynamic_slice_in_dim(cot, (1 - half) * part, part, axis=1), 1)
    else:
        mine, other = cot, exchange(cot, 1)

    *y, pairs = call(
        functools.partial(y_kernel, groups),
        [shape((tok, lanes), BF16)] * groups + [shape((2 * top, tok), F32)],
        [SMEM] + [HBM] * 4,
        [
            pltpu.VMEM((rows, hidden), BF16),
            pltpu.VMEM((rank, hidden), F32),
            pltpu.VMEM((top, tok), jnp.int32),
            pltpu.VMEM((top, tok), F32),
            pltpu.SemaphoreType.DMA((7,)),
        ],
        at,
        cot,
        sketch.T,
        expert_ids.T,
        route_probs.T,
        limit=LARGE,
    )
    send, xs = lax.optimization_barrier((y[-1], xs))
    pairs = [pairs, exchange(pairs, 1)]
    y = jnp.stack([y[0], exchange(send, 1)])
    ys = [jnp.stack([y] + [exchange(y, j * line) for j in range(1, SLICES)])]
    step = 2
    while step < line:
        ys = ys + [exchange(b, step) for b in ys]
        xs = xs + [exchange(b, step) for b in xs]
        step *= 2
    xs = [b for x in xs for b in (x, exchange(x, 1))]

    size = 2 * tok * lanes // 128
    packed = size + rank * share // 128
    if n_dp == 1:
        zs = call(
            functools.partial(z_kernel, len(xs) // 2, low),
            [shape((packed, 128), BF16)] * SLICES,
            [SMEM] + [HBM] * (len(xs) + len(ys)),
            [
                pltpu.VMEM((count * tok, share), BF16),
                pltpu.VMEM((len(xs), 2, tok, lanes), BF16),
                pltpu.VMEM((lanes, share), BF16),
                pltpu.SemaphoreType.DMA((2 * len(xs),)),
            ],
            at,
            *xs,
            *ys,
        )
    else:
        left = jnp.concatenate(ys, axis=0).reshape(-1, lanes)
        right = [jnp.stack([xs[i], xs[i + 1]]) for i in range(0, len(xs), 2)]
        right = jnp.stack(right).reshape(-1, 2, 2, tok, share).swapaxes(1, 2)
        columns = dot(left, right.reshape(-1, share), 0, 0).astype(BF16)
        zs = [
            jnp.concatenate([dot(x[i : i + tok], columns, 1, 1) for x in xs[b : b + 2]], axis=0)
            for b in (0, 2)
            for i in (0, tok)
        ]
        zs = [
            pack(
                z.astype(BF16),
                lax.dynamic_slice_in_dim(columns, ((place ^ j) * low + at[1]) * rank, rank, axis=0),
            )
            for j, z in enumerate(zs)
        ]
    zs = list(zs[:1]) + [exchange(zs[j], j * line) for j in range(1, SLICES)]

    piece = part // CHUNKS
    outs = [shape((SLICES * rank, piece), BF16)] * low
    work = [pltpu.VMEM((2 * rows, piece), BF16), pltpu.SemaphoreType.DMA((2,))]
    spread, *blocks = call(
        functools.partial(first_kernel, groups),
        [shape((lanes, 2 * rows), BF16)] + outs,
        [SMEM] + [VMEM] * (SLICES + 2) + [HBM] * 2,
        [pltpu.VMEM((lanes, 2 * rows), BF16)] + work,
        at,
        *zs,
        *pairs,
        mine,
        other,
        limit=LARGE,
    )
    chunks = [blocks]
    for chunk in range(1, CHUNKS):
        chunks.append(
            call(
                functools.partial(next_kernel, chunk * piece),
                outs,
                [VMEM] + [HBM] * 2,
                work,
                spread,
                mine,
                other,
                limit=LARGE,
            )
        )
    zs, _ = lax.optimization_barrier((zs, chunks[-1][0]))
    inverse, basis = call(
        functools.partial(inverse_kernel, size),
        [shape((rank, rank), F32), shape((rank, width // n_dp), F32)],
        [SMEM] + [VMEM] * SLICES,
        [pltpu.VMEM((SLICES, rank, share), BF16)],
        at,
        *zs,
    )
    sums = []
    for chunk in chunks:
        blocks = [term.reshape(SLICES, rank, piece) for term in chunk]
        step = 2
        while len(blocks) > 1:
            blocks = [
                (keep.astype(F32) + exchange(send, step).astype(F32)).astype(BF16)
                for keep, send in zip(blocks[::2], blocks[1::2])
            ]
            step *= 2
        sums.append(blocks[0])
    sums[0], inverse = lax.optimization_barrier((sums[0], inverse))
    blocks = []
    for block in sums:
        own = [lax.dynamic_index_in_dim(block, place ^ j, 0, False) for j in range(SLICES)]
        blocks += own[:1] + [exchange(own[j], j * line) for j in range(1, SLICES)]
    [coeffs] = call(
        functools.partial(coeffs_kernel, scale),
        [shape((rank, part), F32)],
        [VMEM] * (1 + len(blocks)),
        [],
        inverse,
        *blocks,
    )
    return basis[None], coeffs[None]


def solution(mesh):
    in_specs = (
        P(("group", "expert", "dp"), None),
        P(("group", "expert", "dp"), None),
        P(("group", "expert", "dp"), None),
        P(("group", "expert", "dp"), None, None),
        P(),
    )
    out_specs = (P(("group", "expert"), None, "dp"), P(("group", "expert"), None, "dp"))
    return jax.shard_map(shards, mesh=mesh, in_specs=in_specs, out_specs=out_specs, check_vma=False)
```

```python
import functools
import math

import jax
import jax.numpy as jnp
from jax import lax
from jax.experimental import pallas as pl
from jax.experimental.pallas import tpu as pltpu
from jax.sharding import PartitionSpec as P

AXES = ("expert", "dp")
CHUNKS = 2
SLICES = 4
LIMIT = 12 * 1024 * 1024
LARGE = 56 * 1024 * 1024
VMEM = pl.BlockSpec(memory_space=pltpu.VMEM)
HBM = pl.BlockSpec(memory_space=pltpu.HBM)
BF16 = jnp.bfloat16
F32 = jnp.float32


def dot(left, right, left_dim, right_dim):
    dims = (((left_dim,), (right_dim,)), ((), ()))
    return lax.dot_general(left, right, dims, preferred_element_type=F32)


def iota(shape, dim):
    return lax.broadcasted_iota(jnp.int32, shape, dim)


def position():
    half = lax.axis_index("dp")
    me = lax.axis_index("expert") * lax.axis_size("dp") + half
    line = lax.axis_size("expert") * lax.axis_size("dp") // SLICES
    return me % 2, me // 2 % (line // 2), me // line, half


def call(body, shapes, spaces, scratch, *args, limit=LIMIT):
    return pl.pallas_call(
        body,
        out_shape=shapes,
        in_specs=spaces,
        out_specs=[VMEM] * len(shapes),
        scratch_shapes=scratch,
        compiler_params=pltpu.CompilerParams(vmem_limit_bytes=limit),
        cost_estimate=pl.CostEstimate(flops=1, bytes_accessed=1, transcendentals=0),
    )(*args)


def pieces(value, count):
    terms = []
    for _ in range(count):
        terms.append(value.astype(BF16))
        value = value - terms[-1].astype(F32)
    return terms


def pack(z, columns):
    tiles = [z[:, i : i + 128] for i in range(0, z.shape[1], 128)]
    tiles += [columns[:, i : i + 128] for i in range(0, columns.shape[1], 128)]
    return jnp.concatenate(tiles, axis=0)


def unpack_z(rows, size, lanes):
    tiles = [rows[i * size : (i + 1) * size] for i in range(lanes // 128)]
    return jnp.concatenate(tiles, axis=1)


def unpack_columns(rows, start, rank):
    tiles = [rows[i : i + rank] for i in range(start, rows.shape[0], rank)]
    return jnp.concatenate(tiles, axis=1)


def pair_columns(ids, probs):
    top, tok = ids.shape
    rows = tok * top
    pick = (iota((rows, tok), 0) // top == iota((rows, tok), 1)).astype(BF16)
    here = iota((rows, top), 0) % top == iota((rows, top), 1)
    names = dot(pick, ids.astype(BF16), 1, 1)
    weights, rest = jnp.zeros((rows, top), F32), probs
    for _ in range(3):
        piece = rest.astype(BF16)
        weights = weights + dot(pick, piece, 1, 1)
        rest = rest - piece.astype(F32)
    names = jnp.sum(jnp.where(here, names, 0.0), axis=1, keepdims=True)
    weights = jnp.sum(jnp.where(here, weights, 0.0), axis=1, keepdims=True)
    return names, weights


def load(pairs, sems):
    copies = [pltpu.make_async_copy(src, dst, sems.at[i]) for i, (src, dst) in enumerate(pairs)]
    for copy in copies:
        copy.start()
    return copies


def first_kernel(groups, tokens, cot_at, sketch_at, ids_at, probs_at, *refs):
    outs, pairs, (cot, sketch, ids, probs, sems, x_sems) = refs[:SLICES], refs[SLICES], refs[5:]
    core, _, place, _ = position()
    rows, hidden = cot.shape
    tok = pairs.shape[1]
    top = rows // tok
    rank = sketch.shape[0]
    share = tokens.shape[1] // SLICES
    lanes = (outs[0].shape[1] - share) // groups
    parts = 5
    piece = hidden // parts
    sources = [(ids_at, ids), (probs_at, probs), (sketch_at, sketch)]
    for i in range(parts):
        cut = pl.ds(i * piece, piece)
        sources.append((cot_at.at[:, cut], cot.at[:, cut]))
    copies = load(sources, sems)
    sources = []
    for j, out in enumerate(outs):
        cut = pl.ds(pl.multiple_of((place ^ j) * share, share), share)
        sources.append((tokens.at[:, cut], out.at[:, pl.ds(lanes, share)]))
    x_copies = load(sources, x_sems)
    copies[0].wait()
    copies[1].wait()
    pairs[:top] = ids[...].astype(F32)
    pairs[top:] = probs[...]
    names, weights = pair_columns(pairs[:top], pairs[top:])
    copies[2].wait()
    both = jnp.concatenate(pieces(sketch[...], 2), axis=0)
    pair = 0.0
    for i in range(parts):
        copies[3 + i].wait()
        here = slice(i * piece, (i + 1) * piece)
        pair = pair + dot(cot[:, here], both[:, here], 1, 1)
    pair = (pair[:, :rank] + pair[:, rank:]) * weights
    lane = iota((rank, lanes), 1)
    tiled = dot(pair.astype(BF16), (iota((rank, lanes), 0) == lane % rank).astype(BF16), 1, 0)
    block = iota((1, lanes), 1) // rank * groups
    for i in range(groups):
        name = block + (core ^ i) if groups == 2 else block
        y = jnp.where(names == name.astype(F32), tiled, 0.0)
        y = jnp.sum(y.reshape(tok, top, lanes), axis=1).astype(BF16)
        for out in outs:
            out[:, i * (lanes + share) : i * (lanes + share) + lanes] = y
    for copy in x_copies:
        copy.wait()


def gather(near, far, x, y, sems):
    share, lanes = x.shape[1], y.shape[1]
    rows = near[0].shape[0]
    sources = []
    for i, (a, b) in enumerate(zip(near, far)):
        cut = pl.ds(2 * i * rows, rows)
        sources.append((a.at[:, pl.ds(0, lanes)], y.at[cut]))
        sources.append((a.at[:, pl.ds(lanes, share)], x.at[cut]))
        cut = pl.ds((2 * i + 1) * rows, rows)
        sources.append((b.at[:, pl.ds(0, share)], x.at[cut]))
        sources.append((b.at[:, pl.ds(share, lanes)], y.at[cut]))
    for copy in load(sources, sems):
        copy.wait()


def columns_kernel(n, *refs):
    out, x, y, sems = refs[2 * n :]
    gather(refs[:n], refs[n : 2 * n], x, y, sems)
    out[...] = dot(y[...], x[...], 0, 0)


def z_kernel(n, low, part, near_x, far_x, *refs):
    outs, (x, y, columns, sems) = refs[2 * n : -4], refs[-4:]
    _, lower, place, _ = position()
    gather(refs[:n], refs[n : 2 * n], x, y, sems)
    rank = columns.shape[0] // (SLICES * low)
    share = x.shape[1]
    lanes = y.shape[1]
    rows = near_x.shape[0]
    tok = rows // 2
    total = (part[...] + dot(y[...], x[...], 0, 0)).astype(BF16)
    columns[...] = total
    own = jnp.concatenate([near_x[:, lanes : lanes + share], far_x[:, :share]], axis=0)
    halves = [dot(own, total, 1, 1), dot(x[: 2 * rows], total, 1, 1)]
    for j, out in enumerate(outs):
        half = halves[j // 2].astype(BF16)
        start = j % 2 * tok
        z = jnp.concatenate([half[start : start + tok], half[rows + start :][:tok]], axis=0)
        expert = (place ^ j) * low + lower
        out[...] = pack(z, columns[pl.ds(pl.multiple_of(expert * rank, rank), rank)])


def inverse_kernel(start, p0, p1, p2, p3, inverse, basis, columns):
    _, _, place, half = position()
    rank = inverse.shape[0]
    _, _, share = columns.shape
    gram = 0.0
    for j, packed in enumerate((p0, p1, p2, p3)):
        block = unpack_columns(packed[...], start, rank)
        columns[place ^ j] = block
        gram = gram + dot(block, block, 1, 1)
    row = iota((rank, 128), 0)
    lane = iota((rank, 128), 1)
    eye = (row + rank == lane).astype(F32)
    work = jnp.concatenate([gram, jnp.zeros((rank, 128 - rank), F32)], axis=1) + eye
    for first in range(0, rank, 4):
        heads = [work[first + i : first + i + 1] for i in range(4)]
        sides = [
            jnp.broadcast_to(work[:, first + i : first + i + 1], (rank, 128)) for i in range(4)
        ]
        taken = 0.0
        for i in range(4):
            pivot = first + i
            factor = sides[i] / sides[i][pivot : pivot + 1]
            factor = jnp.where(row > pivot, factor, 0.0)
            taken = taken + factor * heads[i]
            for k in range(i + 1, 4):
                sides[k] = sides[k] - factor * sides[k][pivot : pivot + 1]
                heads[k] = heads[k] - factor[first + k : first + k + 1] * heads[i]
        work = work - taken
    diagonal = jnp.sum(jnp.where(row == lane, work, 0.0), axis=1, keepdims=True)
    result = work[:, rank : 2 * rank] * lax.rsqrt(diagonal)
    inverse[...] = result
    scaled = result * math.sqrt(SLICES * share)
    scaled = jnp.concatenate(pieces(scaled, 3), axis=0)
    count = basis.shape[1] // share
    for i in range(count):
        out = dot(scaled, columns[half * count + i], 1, 0)
        out = out[:rank] + out[rank : 2 * rank] + out[2 * rank :]
        basis[:, i * share : (i + 1) * share] = out


def coeffs_kernel(scale, inverse, *refs):
    blocks, out = refs[:-1], refs[-1]
    rank, size = blocks[0].shape
    left = jnp.concatenate(pieces(inverse[...] * scale, 3), axis=0)
    left = jnp.concatenate([left] * SLICES, axis=1)
    for i in range(len(blocks) // SLICES):
        right = jnp.concatenate([b[...] for b in blocks[i * SLICES : (i + 1) * SLICES]], axis=0)
        part = dot(left, right, 1, 0)
        out[:, i * size : (i + 1) * size] = part[:rank] + part[rank : 2 * rank] + part[2 * rank :]


def mask_kernel(groups, own, pair, out):
    core = position()[0]
    lanes, rows = out.shape
    rows = rows // 2
    top, tok = own.shape[0] // 2, own.shape[1]
    rank = lanes // (lax.axis_size("expert") // groups)
    pick = (iota((tok, rows), 1) // top == iota((tok, rows), 0)).astype(BF16)
    here = iota((top, rows), 1) % top == iota((top, rows), 0)
    block = iota((lanes, 1), 0) // rank * groups + (core if groups == 2 else 0)
    for i, pairs in enumerate((own, pair)):
        names = dot(pairs[:top].astype(BF16), pick, 1, 0)
        weights = sum(dot(piece, pick, 1, 0) for piece in pieces(pairs[top:], 3))
        names = jnp.sum(jnp.where(here, names, 0.0), axis=0, keepdims=True)
        weights = jnp.sum(jnp.where(here, weights, 0.0), axis=0, keepdims=True)
        masked = jnp.where(names == block.astype(F32), weights, 0.0)
        out[:, i * rows : (i + 1) * rows] = masked


def terms_kernel(low, tok, z0, z1, z2, z3, mask, mine, other, *refs):
    outs, (work, spread) = refs[:-2], refs[-2:]
    lower = position()[1]
    lanes, rows = mask.shape
    rows = rows // 2
    rank = lanes // (SLICES * low)
    size = 2 * tok * lanes // 128
    z = 0.0
    for block in (z0, z1, z2, z3):
        z = z + unpack_z(block[:size], 2 * tok, lanes).astype(F32)
    repeat = iota((2 * tok, 2 * rows), 1) // (rows // tok) == iota((2 * tok, 2 * rows), 0)
    z = dot(z.astype(BF16), repeat.astype(BF16), 0, 0)
    work[...] = (z * mask[...]).astype(BF16)
    for r in range(low):
        for j in range(SLICES):
            start = pl.multiple_of((j * low + (lower ^ r)) * rank, rank)
            spread[(r * SLICES + j) * rank : (r * SLICES + j + 1) * rank] = work[
                pl.ds(start, rank)
            ]
    for chunk in range(len(outs) // low):
        block, width = outs[chunk * low].shape
        here = slice(chunk * width, (chunk + 1) * width)
        part = dot(spread[:, :rows], mine[:, here], 1, 0)
        part = (part + dot(spread[:, rows:], other[:, here], 1, 0)).astype(BF16)
        for r in range(low):
            outs[chunk * low + r][...] = part[r * block : (r + 1) * block]


def shards(tokens, expert_ids, route_probs, cotangents, sketch):
    n_expert = lax.axis_size("expert")
    n_dp = lax.axis_size("dp")
    count = n_expert * n_dp
    line = count // SLICES
    low = line // 2
    groups = 2 // n_dp
    tok, width = tokens.shape
    top = expert_ids.shape[1]
    hidden, rank = sketch.shape
    rows = tok * top
    share = width // SLICES
    lanes = count // 2 * rank
    part = hidden // n_dp
    scale = 1.0 / math.sqrt(rows)
    _, lower, place, half = position()
    limit = LIMIT if n_dp == 1 else LARGE
    shape = jax.ShapeDtypeStruct

    def exchange(block, step):
        return lax.ppermute(block, AXES, [(i, i ^ step) for i in range(count)])

    cot = cotangents.reshape(rows, hidden)
    if n_dp > 1:
        mine = lax.dynamic_slice_in_dim(cot, half * part, part, axis=1)
        other = exchange(lax.dynamic_slice_in_dim(cot, (1 - half) * part, part, axis=1), 1)
    else:
        mine, other = cot, exchange(cot, 1)

    *blocks, pairs = call(
        functools.partial(first_kernel, groups),
        [shape((tok, groups * lanes + share), BF16)] * SLICES + [shape((2 * top, tok), F32)],
        [HBM] * 5,
        [
            pltpu.VMEM((rows, hidden), BF16),
            pltpu.VMEM((rank, hidden), F32),
            pltpu.VMEM((top, tok), jnp.int32),
            pltpu.VMEM((top, tok), F32),
            pltpu.SemaphoreType.DMA((8,)),
            pltpu.SemaphoreType.DMA((SLICES,)),
        ],
        tokens,
        cot,
        sketch.T,
        expert_ids.T,
        route_probs.T,
        limit=LARGE,
    )
    blocks = blocks[:1] + [exchange(blocks[j], j * line) for j in range(1, SLICES)]
    pairs = [pairs, exchange(pairs, 1)]
    near = [[jnp.concatenate(blocks[i : i + 2], axis=0)] for i in range(0, SLICES, 2)]
    step = 2
    while step < line:
        near = [side + [exchange(b, step) for b in side] for side in near]
        step *= 2
    n = len(near[0])
    skip = lanes if groups == 2 else 0

    size = 2 * tok * lanes // 128
    far = [exchange(b[:, skip:], 1) for b in near[0]]
    if n_dp == 1:
        work = [
            pltpu.VMEM((4 * n * tok, share), BF16),
            pltpu.VMEM((4 * n * tok, lanes), BF16),
            pltpu.SemaphoreType.DMA((4 * n,)),
        ]
        [columns] = call(
            functools.partial(columns_kernel, n),
            [shape((lanes, share), F32)],
            [HBM] * (2 * n),
            work,
            *near[0],
            *far,
        )
        near[1], columns = lax.optimization_barrier((near[1], columns))
        zs = call(
            functools.partial(z_kernel, n, low),
            [shape((size + rank * share // 128, 128), BF16)] * SLICES,
            [VMEM] * 3 + [HBM] * (2 * n),
            work[:2] + [pltpu.VMEM((lanes, share), BF16)] + work[2:],
            columns,
            near[0][0],
            far[0],
            *near[1],
            *[exchange(b[:, skip:], 1) for b in near[1]],
        )
    else:
        far = [far, [exchange(b[:, skip:], 1) for b in near[1]]]
        rows_all = jnp.concatenate(near[0] + far[0] + near[1] + far[1], axis=0)
        columns = dot(rows_all[:, :lanes], rows_all[:, lanes:], 0, 0).astype(BF16)
        zs = []
        for j in range(SLICES):
            here = slice(j % 2 * tok, (j % 2 + 1) * tok)
            x = jnp.concatenate([near[j // 2][0][here], far[j // 2][0][here]], axis=0)
            start = ((place ^ j) * low + lower) * rank
            own = lax.dynamic_slice_in_dim(columns, start, rank, axis=0)
            zs.append(pack(dot(x[:, lanes:], columns, 1, 1).astype(BF16), own))
    zs = list(zs[:1]) + [exchange(zs[j], j * line) for j in range(1, SLICES)]

    [mask] = call(
        functools.partial(mask_kernel, groups),
        [shape((lanes, 2 * rows), F32)],
        [VMEM] * 2,
        [],
        *pairs,
        limit=limit,
    )
    piece = part // CHUNKS
    terms = call(
        functools.partial(terms_kernel, low, tok),
        [shape((SLICES * rank, piece), BF16)] * (low * CHUNKS),
        [VMEM] * (SLICES + 3),
        [pltpu.VMEM((lanes, 2 * rows), BF16)] * 2,
        *zs,
        mask,
        mine,
        other,
        limit=limit,
    )
    zs, _ = lax.optimization_barrier((zs, terms[-1]))
    inverse, basis = call(
        functools.partial(inverse_kernel, size),
        [shape((rank, rank), F32), shape((rank, width // n_dp), F32)],
        [VMEM] * SLICES,
        [pltpu.VMEM((SLICES, rank, share), BF16)],
        *zs,
    )
    sums = []
    for chunk in range(CHUNKS):
        blocks = terms[chunk * low : (chunk + 1) * low]
        blocks = [term.reshape(SLICES, rank, piece) for term in blocks]
        step = 2
        while len(blocks) > 1:
            blocks = [
                (keep.astype(F32) + exchange(send, step).astype(F32)).astype(BF16)
                for keep, send in zip(blocks[::2], blocks[1::2])
            ]
            step *= 2
        sums.append(blocks[0])
    sums[0], inverse = lax.optimization_barrier((sums[0], inverse))
    blocks = []
    for block in sums:
        own = [lax.dynamic_index_in_dim(block, place ^ j, 0, False) for j in range(SLICES)]
        blocks += own[:1] + [exchange(own[j], j * line) for j in range(1, SLICES)]
    [coeffs] = call(
        functools.partial(coeffs_kernel, scale),
        [shape((rank, part), F32)],
        [VMEM] * (1 + len(blocks)),
        [],
        inverse,
        *blocks,
    )
    return basis[None], coeffs[None]


def solution(mesh):
    in_specs = (
        P(("group", "expert", "dp"), None),
        P(("group", "expert", "dp"), None),
        P(("group", "expert", "dp"), None),
        P(("group", "expert", "dp"), None, None),
        P(),
    )
    out_specs = (P(("group", "expert"), None, "dp"), P(("group", "expert"), None, "dp"))
    return jax.shard_map(shards, mesh=mesh, in_specs=in_specs, out_specs=out_specs, check_vma=False)
```

```python
import functools
import math

import jax
import jax.numpy as jnp
from jax import lax
from jax.experimental import pallas as pl
from jax.experimental.pallas import tpu as pltpu
from jax.sharding import PartitionSpec as P

AXES = ("expert", "dp")
SLICES = 4
LIMIT = 12 * 1024 * 1024
LARGE = 56 * 1024 * 1024
VMEM = pl.BlockSpec(memory_space=pltpu.VMEM)
HBM = pl.BlockSpec(memory_space=pltpu.HBM)
BF16 = jnp.bfloat16
F32 = jnp.float32


def dot(left, right, left_dim, right_dim):
    dims = (((left_dim,), (right_dim,)), ((), ()))
    return lax.dot_general(left, right, dims, preferred_element_type=F32)


def iota(shape, dim):
    return lax.broadcasted_iota(jnp.int32, shape, dim)


def position():
    half = lax.axis_index("dp")
    me = lax.axis_index("expert") * lax.axis_size("dp") + half
    line = lax.axis_size("expert") * lax.axis_size("dp") // SLICES
    return me % 2, me // 2 % (line // 2), me // line, half


def call(body, shapes, spaces, scratch, *args, limit=LIMIT):
    return pl.pallas_call(
        body,
        out_shape=shapes,
        in_specs=spaces,
        out_specs=[VMEM] * len(shapes),
        scratch_shapes=scratch,
        compiler_params=pltpu.CompilerParams(vmem_limit_bytes=limit),
        cost_estimate=pl.CostEstimate(flops=1, bytes_accessed=1, transcendentals=0),
    )(*args)


def pieces(value, count):
    terms = []
    for _ in range(count):
        terms.append(value.astype(BF16))
        value = value - terms[-1].astype(F32)
    return terms


def pack(z, columns):
    tiles = [z[:, i : i + 128] for i in range(0, z.shape[1], 128)]
    tiles += [columns[:, i : i + 128] for i in range(0, columns.shape[1], 128)]
    return jnp.concatenate(tiles, axis=0)


def unpack_z(rows, size, lanes):
    tiles = [rows[i * size : (i + 1) * size] for i in range(lanes // 128)]
    return jnp.concatenate(tiles, axis=1)


def unpack_columns(rows, start, rank):
    tiles = [rows[i : i + rank] for i in range(start, rows.shape[0], rank)]
    return jnp.concatenate(tiles, axis=1)


def pair_columns(ids, probs):
    top, tok = ids.shape
    rows = tok * top
    pick = (iota((rows, tok), 0) // top == iota((rows, tok), 1)).astype(BF16)
    here = iota((rows, top), 0) % top == iota((rows, top), 1)
    names = dot(pick, ids.astype(BF16), 1, 1)
    weights, rest = jnp.zeros((rows, top), F32), probs
    for _ in range(3):
        piece = rest.astype(BF16)
        weights = weights + dot(pick, piece, 1, 1)
        rest = rest - piece.astype(F32)
    names = jnp.sum(jnp.where(here, names, 0.0), axis=1, keepdims=True)
    weights = jnp.sum(jnp.where(here, weights, 0.0), axis=1, keepdims=True)
    return names, weights


def load(pairs, sems):
    copies = [pltpu.make_async_copy(src, dst, sems.at[i]) for i, (src, dst) in enumerate(pairs)]
    for copy in copies:
        copy.start()
    return copies


def first_kernel(groups, tokens, cot_at, sketch_at, ids_at, probs_at, *refs):
    outs, pairs, (cot, sketch, ids, probs, sems, x_sems) = refs[:SLICES], refs[SLICES], refs[5:]
    core, _, place, _ = position()
    rows, hidden = cot.shape
    tok = pairs.shape[1]
    top = rows // tok
    rank = sketch.shape[0]
    share = tokens.shape[1] // SLICES
    lanes = (outs[0].shape[1] - share) // groups
    parts = 5
    piece = hidden // parts
    sources = [(ids_at, ids), (probs_at, probs), (sketch_at, sketch)]
    for i in range(parts):
        cut = pl.ds(i * piece, piece)
        sources.append((cot_at.at[:, cut], cot.at[:, cut]))
    copies = load(sources, sems)
    sources = []
    for j, out in enumerate(outs):
        cut = pl.ds(pl.multiple_of((place ^ j) * share, share), share)
        sources.append((tokens.at[:, cut], out.at[:, pl.ds(lanes, share)]))
    x_copies = load(sources, x_sems)
    copies[0].wait()
    copies[1].wait()
    pairs[:top] = ids[...].astype(F32)
    pairs[top:] = probs[...]
    names, weights = pair_columns(pairs[:top], pairs[top:])
    copies[2].wait()
    both = jnp.concatenate(pieces(sketch[...], 2), axis=0)
    pair = 0.0
    for i in range(parts):
        copies[3 + i].wait()
        here = slice(i * piece, (i + 1) * piece)
        pair = pair + dot(cot[:, here], both[:, here], 1, 1)
    pair = (pair[:, :rank] + pair[:, rank:]) * weights
    lane = iota((rank, lanes), 1)
    tiled = dot(pair.astype(BF16), (iota((rank, lanes), 0) == lane % rank).astype(BF16), 1, 0)
    block = iota((1, lanes), 1) // rank * groups
    for i in range(groups):
        name = block + (core ^ i) if groups == 2 else block
        y = jnp.where(names == name.astype(F32), tiled, 0.0)
        y = jnp.sum(y.reshape(tok, top, lanes), axis=1).astype(BF16)
        for out in outs:
            out[:, i * (lanes + share) : i * (lanes + share) + lanes] = y
    for copy in x_copies:
        copy.wait()


def gather(near, far, x, y, sems):
    share, lanes = x.shape[1], y.shape[1]
    rows = near[0].shape[0]
    sources = []
    for i, (a, b) in enumerate(zip(near, far)):
        cut = pl.ds(2 * i * rows, rows)
        sources.append((a.at[:, pl.ds(0, lanes)], y.at[cut]))
        sources.append((a.at[:, pl.ds(lanes, share)], x.at[cut]))
        cut = pl.ds((2 * i + 1) * rows, rows)
        sources.append((b.at[:, pl.ds(0, share)], x.at[cut]))
        sources.append((b.at[:, pl.ds(share, lanes)], y.at[cut]))
    for copy in load(sources, sems):
        copy.wait()


def columns_kernel(n, *refs):
    out, x, y, sems = refs[2 * n :]
    gather(refs[:n], refs[n : 2 * n], x, y, sems)
    out[...] = dot(y[...], x[...], 0, 0)


def z_kernel(n, low, part, near_x, far_x, *refs):
    outs, (x, y, columns, sems) = refs[2 * n : -4], refs[-4:]
    _, lower, place, _ = position()
    gather(refs[:n], refs[n : 2 * n], x, y, sems)
    rank = columns.shape[0] // (SLICES * low)
    share = x.shape[1]
    lanes = y.shape[1]
    tok = near_x.shape[0] // 2
    total = (part[...] + dot(y[...], x[...], 0, 0)).astype(BF16)
    columns[...] = total
    own = [near_x[:tok, lanes : lanes + share], far_x[:tok, :share]]
    own += [near_x[tok:, lanes : lanes + share], far_x[tok:, :share]]
    own += [x[: 2 * tok], x[n * tok : (n + 2) * tok]]
    z = dot(jnp.concatenate(own, axis=0), total, 1, 1).astype(BF16)
    for j, out in enumerate(outs):
        expert = (place ^ j) * low + lower
        own = columns[pl.ds(pl.multiple_of(expert * rank, rank), rank)]
        out[...] = pack(z[2 * j * tok : 2 * (j + 1) * tok], own)


def inverse_kernel(start, p0, p1, p2, p3, inverse, basis, columns):
    _, _, place, half = position()
    rank = inverse.shape[0]
    _, _, share = columns.shape
    gram = 0.0
    for j, packed in enumerate((p0, p1, p2, p3)):
        block = unpack_columns(packed[...], start, rank)
        columns[place ^ j] = block
        gram = gram + dot(block, block, 1, 1)
    row = iota((rank, 128), 0)
    lane = iota((rank, 128), 1)
    eye = (row + rank == lane).astype(F32)
    work = jnp.concatenate([gram, jnp.zeros((rank, 128 - rank), F32)], axis=1) + eye
    for first in range(0, rank, 4):
        heads = [work[first + i : first + i + 1] for i in range(4)]
        sides = [
            jnp.broadcast_to(work[:, first + i : first + i + 1], (rank, 128)) for i in range(4)
        ]
        taken = 0.0
        for i in range(4):
            pivot = first + i
            factor = sides[i] / sides[i][pivot : pivot + 1]
            factor = jnp.where(row > pivot, factor, 0.0)
            taken = taken + factor * heads[i]
            for k in range(i + 1, 4):
                sides[k] = sides[k] - factor * sides[k][pivot : pivot + 1]
                heads[k] = heads[k] - factor[first + k : first + k + 1] * heads[i]
        work = work - taken
    diagonal = jnp.sum(jnp.where(row == lane, work, 0.0), axis=1, keepdims=True)
    result = work[:, rank : 2 * rank] * lax.rsqrt(diagonal)
    inverse[...] = result
    scaled = result * math.sqrt(SLICES * share)
    scaled = jnp.concatenate(pieces(scaled, 3), axis=0)
    count = basis.shape[1] // share
    for i in range(count):
        out = dot(scaled, columns[half * count + i], 1, 0)
        out = out[:rank] + out[rank : 2 * rank] + out[2 * rank :]
        basis[:, i * share : (i + 1) * share] = out


def coeffs_kernel(scale, inverse, *refs):
    blocks, out = refs[:-1], refs[-1]
    rank = inverse.shape[0]
    left = jnp.concatenate(pieces(inverse[...] * scale, 3), axis=0)
    left = jnp.concatenate([left] * SLICES, axis=1)
    start = 0
    for i in range(0, len(blocks), SLICES):
        right = jnp.concatenate([b[...] for b in blocks[i : i + SLICES]], axis=0)
        part = dot(left, right, 1, 0)
        part = part[:rank] + part[rank : 2 * rank] + part[2 * rank :]
        out[:, start : start + right.shape[1]] = part
        start += right.shape[1]


def mask_kernel(groups, own, pair, out):
    core = position()[0]
    lanes, rows = out.shape
    rows = rows // 2
    top, tok = own.shape[0] // 2, own.shape[1]
    rank = lanes // (lax.axis_size("expert") // groups)
    pick = (iota((tok, rows), 1) // top == iota((tok, rows), 0)).astype(BF16)
    here = iota((top, rows), 1) % top == iota((top, rows), 0)
    block = iota((lanes, 1), 0) // rank * groups + (core if groups == 2 else 0)
    for i, pairs in enumerate((own, pair)):
        names = dot(pairs[:top].astype(BF16), pick, 1, 0)
        weights = sum(dot(piece, pick, 1, 0) for piece in pieces(pairs[top:], 3))
        names = jnp.sum(jnp.where(here, names, 0.0), axis=0, keepdims=True)
        weights = jnp.sum(jnp.where(here, weights, 0.0), axis=0, keepdims=True)
        masked = jnp.where(names == block.astype(F32), weights, 0.0)
        out[:, i * rows : (i + 1) * rows] = masked


def terms_kernel(low, tok, z0, z1, z2, z3, mask, mine, other, *refs):
    outs, (work, spread) = refs[:-2], refs[-2:]
    lower = position()[1]
    lanes, rows = mask.shape
    rows = rows // 2
    rank = lanes // (SLICES * low)
    size = 2 * tok * lanes // 128
    z = 0.0
    for block in (z0, z1, z2, z3):
        z = z + unpack_z(block[:size], 2 * tok, lanes).astype(F32)
    repeat = iota((2 * tok, 2 * rows), 1) // (rows // tok) == iota((2 * tok, 2 * rows), 0)
    z = dot(z.astype(BF16), repeat.astype(BF16), 0, 0)
    work[...] = (z * mask[...]).astype(BF16)
    for r in range(low):
        for j in range(SLICES):
            start = pl.multiple_of((j * low + (lower ^ r)) * rank, rank)
            spread[(r * SLICES + j) * rank : (r * SLICES + j + 1) * rank] = work[
                pl.ds(start, rank)
            ]
    start = 0
    for chunk in range(0, len(outs), low):
        block, width = outs[chunk].shape
        here = slice(start, start + width)
        part = dot(spread[:, :rows], mine[:, here], 1, 0)
        part = (part + dot(spread[:, rows:], other[:, here], 1, 0)).astype(BF16)
        for r in range(low):
            outs[chunk + r][...] = part[r * block : (r + 1) * block]
        start += width


def shards(tokens, expert_ids, route_probs, cotangents, sketch):
    n_expert = lax.axis_size("expert")
    n_dp = lax.axis_size("dp")
    count = n_expert * n_dp
    line = count // SLICES
    low = line // 2
    groups = 2 // n_dp
    tok, width = tokens.shape
    top = expert_ids.shape[1]
    hidden, rank = sketch.shape
    rows = tok * top
    share = width // SLICES
    lanes = count // 2 * rank
    part = hidden // n_dp
    scale = 1.0 / math.sqrt(rows)
    _, lower, place, half = position()
    limit = LIMIT if n_dp == 1 else LARGE
    shape = jax.ShapeDtypeStruct

    def exchange(block, step):
        return lax.ppermute(block, AXES, [(i, i ^ step) for i in range(count)])

    cot = cotangents.reshape(rows, hidden)
    if n_dp > 1:
        mine = lax.dynamic_slice_in_dim(cot, half * part, part, axis=1)
        other = exchange(lax.dynamic_slice_in_dim(cot, (1 - half) * part, part, axis=1), 1)
    else:
        mine, other = cot, exchange(cot, 1)

    *blocks, pairs = call(
        functools.partial(first_kernel, groups),
        [shape((tok, groups * lanes + share), BF16)] * SLICES + [shape((2 * top, tok), F32)],
        [HBM] * 5,
        [
            pltpu.VMEM((rows, hidden), BF16),
            pltpu.VMEM((rank, hidden), F32),
            pltpu.VMEM((top, tok), jnp.int32),
            pltpu.VMEM((top, tok), F32),
            pltpu.SemaphoreType.DMA((8,)),
            pltpu.SemaphoreType.DMA((SLICES,)),
        ],
        tokens,
        cot,
        sketch.T,
        expert_ids.T,
        route_probs.T,
        limit=LARGE,
    )
    blocks = blocks[:1] + [exchange(blocks[j], j * line) for j in range(1, SLICES)]
    pairs = [pairs, exchange(pairs, 1)]
    near = [[jnp.concatenate(blocks[:2], axis=0)], [blocks[2]], [blocks[3]]]
    step = 2
    while step < line:
        near = [side + [exchange(b, step) for b in side] for side in near]
        step *= 2
    n = len(near[0])
    late = near[1] + near[2]
    skip = lanes if groups == 2 else 0

    size = 2 * tok * lanes // 128
    far = [exchange(b[:, skip:], 1) for b in near[0]]
    if n_dp == 1:
        work = [
            pltpu.VMEM((4 * n * tok, share), BF16),
            pltpu.VMEM((4 * n * tok, lanes), BF16),
            pltpu.SemaphoreType.DMA((4 * n,)),
        ]
        [columns] = call(
            functools.partial(columns_kernel, n),
            [shape((lanes, share), F32)],
            [HBM] * (2 * n),
            work,
            *near[0],
            *far,
        )
        late[-1], columns = lax.optimization_barrier((late[-1], columns))
        zs = call(
            functools.partial(z_kernel, 2 * n, low),
            [shape((size + rank * share // 128, 128), BF16)] * SLICES,
            [VMEM] * 3 + [HBM] * (4 * n),
            work[:2]
            + [pltpu.VMEM((lanes, share), BF16), pltpu.SemaphoreType.DMA((8 * n,))],
            columns,
            near[0][0],
            far[0],
            *late,
            *[exchange(b[:, skip:], 1) for b in late],
        )
    else:
        far += [exchange(b[:, skip:], 1) for b in late]
        rows_all = jnp.concatenate(near[0] + late + far, axis=0)
        columns = dot(rows_all[:, :lanes], rows_all[:, lanes:], 0, 0).astype(BF16)
        zs = []
        for j, (b, i) in enumerate([(0, 0), (0, tok), (n, 0), (2 * n, 0)]):
            x = [side[b][i : i + tok, lanes:] for side in (near[0] + late, far)]
            start = ((place ^ j) * low + lower) * rank
            own = lax.dynamic_slice_in_dim(columns, start, rank, axis=0)
            zs.append(pack(dot(jnp.concatenate(x, axis=0), columns, 1, 1).astype(BF16), own))
    zs = list(zs[:1]) + [exchange(zs[j], j * line) for j in range(1, SLICES)]

    [mask] = call(
        functools.partial(mask_kernel, groups),
        [shape((lanes, 2 * rows), F32)],
        [VMEM] * 2,
        [],
        *pairs,
        limit=limit,
    )
    piece = part // 128 * 3 // 10 * 128
    chunks = [part - 2 * piece, piece, piece]
    terms = call(
        functools.partial(terms_kernel, low, tok),
        [shape((SLICES * rank, chunk), BF16) for chunk in chunks for _ in range(low)],
        [VMEM] * (SLICES + 3),
        [pltpu.VMEM((lanes, 2 * rows), BF16)] * 2,
        *zs,
        mask,
        mine,
        other,
        limit=limit,
    )
    zs, _ = lax.optimization_barrier((zs, terms[-1]))
    inverse, basis = call(
        functools.partial(inverse_kernel, size),
        [shape((rank, rank), F32), shape((rank, width // n_dp), F32)],
        [VMEM] * SLICES,
        [pltpu.VMEM((SLICES, rank, share), BF16)],
        *zs,
    )
    sums = []
    for i in range(len(chunks)):
        blocks = terms[i * low : (i + 1) * low]
        blocks = [term.reshape(SLICES, rank, chunks[i]) for term in blocks]
        step = 2
        while len(blocks) > 1:
            blocks = [
                (keep.astype(F32) + exchange(send, step).astype(F32)).astype(BF16)
                for keep, send in zip(blocks[::2], blocks[1::2])
            ]
            step *= 2
        sums.append(blocks[0])
    sums[0], inverse = lax.optimization_barrier((sums[0], inverse))
    blocks = []
    for block in sums:
        own = [lax.dynamic_index_in_dim(block, place ^ j, 0, False) for j in range(SLICES)]
        blocks += own[:1] + [exchange(own[j], j * line) for j in range(1, SLICES)]
    [coeffs] = call(
        functools.partial(coeffs_kernel, scale),
        [shape((rank, part), F32)],
        [VMEM] * (1 + len(blocks)),
        [],
        inverse,
        *blocks,
    )
    return basis[None], coeffs[None]


def solution(mesh):
    in_specs = (
        P(("group", "expert", "dp"), None),
        P(("group", "expert", "dp"), None),
        P(("group", "expert", "dp"), None),
        P(("group", "expert", "dp"), None, None),
        P(),
    )
    out_specs = (P(("group", "expert"), None, "dp"), P(("group", "expert"), None, "dp"))
    return jax.shard_map(shards, mesh=mesh, in_specs=in_specs, out_specs=out_specs, check_vma=False)
```

```python
import functools
import math

import jax
import jax.numpy as jnp
from jax import lax
from jax.experimental import pallas as pl
from jax.experimental.pallas import tpu as pltpu
from jax.sharding import PartitionSpec as P

AXES = ("expert", "dp")
CHUNKS = 2
SLICES = 4
LIMIT = 12 * 1024 * 1024
LARGE = 56 * 1024 * 1024
VMEM = pl.BlockSpec(memory_space=pltpu.VMEM)
HBM = pl.BlockSpec(memory_space=pltpu.HBM)
BF16 = jnp.bfloat16
F32 = jnp.float32


def dot(left, right, left_dim, right_dim):
    dims = (((left_dim,), (right_dim,)), ((), ()))
    return lax.dot_general(left, right, dims, preferred_element_type=F32)


def iota(shape, dim):
    return lax.broadcasted_iota(jnp.int32, shape, dim)


def position():
    half = lax.axis_index("dp")
    me = lax.axis_index("expert") * lax.axis_size("dp") + half
    line = lax.axis_size("expert") * lax.axis_size("dp") // SLICES
    return me % 2, me // 2 % (line // 2), me // line, half


def call(body, shapes, spaces, scratch, *args, limit=LIMIT):
    return pl.pallas_call(
        body,
        out_shape=shapes,
        in_specs=spaces,
        out_specs=[VMEM] * len(shapes),
        scratch_shapes=scratch,
        compiler_params=pltpu.CompilerParams(vmem_limit_bytes=limit),
        cost_estimate=pl.CostEstimate(flops=1, bytes_accessed=1, transcendentals=0),
    )(*args)


def pieces(value, count):
    terms = []
    for _ in range(count):
        terms.append(value.astype(BF16))
        value = value - terms[-1].astype(F32)
    return terms


def pair_columns(ids, probs):
    top, tok = ids.shape
    rows = tok * top
    pick = (iota((rows, tok), 0) // top == iota((rows, tok), 1)).astype(BF16)
    here = iota((rows, top), 0) % top == iota((rows, top), 1)
    names = dot(pick, ids.astype(BF16), 1, 1)
    weights, rest = jnp.zeros((rows, top), F32), probs
    for _ in range(3):
        piece = rest.astype(BF16)
        weights = weights + dot(pick, piece, 1, 1)
        rest = rest - piece.astype(F32)
    names = jnp.sum(jnp.where(here, names, 0.0), axis=1, keepdims=True)
    weights = jnp.sum(jnp.where(here, weights, 0.0), axis=1, keepdims=True)
    return names, weights


def load(pairs, sems):
    copies = [pltpu.make_async_copy(src, dst, sems.at[i]) for i, (src, dst) in enumerate(pairs)]
    for copy in copies:
        copy.start()
    return copies


def first_kernel(groups, tokens, cot_at, sketch_at, ids_at, probs_at, *refs):
    outs, pairs, (cot, sketch, ids, probs, sems, x_sems) = refs[:SLICES], refs[SLICES], refs[5:]
    core, _, place, _ = position()
    rows, hidden = cot.shape
    tok = pairs.shape[1]
    top = rows // tok
    rank = sketch.shape[0]
    share = tokens.shape[1] // SLICES
    lanes = (outs[0].shape[1] - share) // groups
    parts = 5
    piece = hidden // parts
    sources = [(ids_at, ids), (probs_at, probs), (sketch_at, sketch)]
    for i in range(parts):
        cut = pl.ds(i * piece, piece)
        sources.append((cot_at.at[:, cut], cot.at[:, cut]))
    copies = load(sources, sems)
    sources = []
    for j, out in enumerate(outs):
        cut = pl.ds(pl.multiple_of((place ^ j) * share, share), share)
        sources.append((tokens.at[:, cut], out.at[:, pl.ds(lanes, share)]))
    x_copies = load(sources, x_sems)
    copies[0].wait()
    copies[1].wait()
    pairs[:top] = ids[...].astype(F32)
    pairs[top:] = probs[...]
    names, weights = pair_columns(pairs[:top], pairs[top:])
    copies[2].wait()
    both = jnp.concatenate(pieces(sketch[...], 2), axis=0)
    pair = 0.0
    for i in range(parts):
        copies[3 + i].wait()
        here = slice(i * piece, (i + 1) * piece)
        pair = pair + dot(cot[:, here], both[:, here], 1, 1)
    pair = (pair[:, :rank] + pair[:, rank:]) * weights
    lane = iota((rank, lanes), 1)
    tiled = dot(pair.astype(BF16), (iota((rank, lanes), 0) == lane % rank).astype(BF16), 1, 0)
    block = iota((1, lanes), 1) // rank * groups
    pick = (iota((rows, tok), 0) // top == iota((rows, tok), 1)).astype(BF16)
    for i in range(groups):
        name = block + (core ^ i) if groups == 2 else block
        y = jnp.where(names == name.astype(F32), tiled, 0.0).astype(BF16)
        y = dot(pick, y, 0, 0).astype(BF16)
        for out in outs:
            out[:, i * (lanes + share) : i * (lanes + share) + lanes] = y
    for copy in x_copies:
        copy.wait()


def gather(near, far, x, y, sems):
    share, lanes = x.shape[1], y.shape[1]
    rows = near[0].shape[0]
    sources = []
    for i, (a, b) in enumerate(zip(near, far)):
        cut = pl.ds(2 * i * rows, rows)
        sources.append((a.at[:, pl.ds(0, lanes)], y.at[cut]))
        sources.append((a.at[:, pl.ds(lanes, share)], x.at[cut]))
        cut = pl.ds((2 * i + 1) * rows, rows)
        sources.append((b.at[:, pl.ds(0, share)], x.at[cut]))
        sources.append((b.at[:, pl.ds(share, lanes)], y.at[cut]))
    for copy in load(sources, sems):
        copy.wait()


def columns_kernel(n, *refs):
    out, x, y, sems = refs[2 * n :]
    gather(refs[:n], refs[n : 2 * n], x, y, sems)
    out[...] = dot(y[...], x[...], 0, 0)


def z_kernel(n, low, part, near_x, far_x, *refs):
    outs, (x, y, columns, sems) = refs[2 * n : -4], refs[-4:]
    _, lower, place, _ = position()
    gather(refs[:n], refs[n : 2 * n], x, y, sems)
    rank = columns.shape[0] // (SLICES * low)
    share = x.shape[1]
    lanes = y.shape[1]
    rows = near_x.shape[0]
    tok = rows // 2
    total = (part[...] + dot(y[...], x[...], 0, 0)).astype(BF16)
    columns[...] = total
    own = jnp.concatenate([near_x[:, lanes : lanes + share], far_x[:, :share]], axis=0)
    halves = [dot(own, total, 1, 1), dot(x[: 2 * rows], total, 1, 1)]
    for j in range(SLICES):
        half = halves[j // 2].astype(BF16)
        start = j % 2 * tok
        outs[j][:tok] = half[start : start + tok]
        outs[j][tok:] = half[rows + start : rows + start + tok]
        expert = (place ^ j) * low + lower
        outs[SLICES + j][...] = columns[pl.ds(pl.multiple_of(expert * rank, rank), rank)]


def inverse_kernel(c0, c1, c2, c3, inverse, basis, columns):
    _, _, place, half = position()
    rank = inverse.shape[0]
    _, _, share = columns.shape
    gram = 0.0
    for j, block in enumerate((c0, c1, c2, c3)):
        columns[place ^ j] = block[...]
        gram = gram + dot(block[...], block[...], 1, 1)
    row = iota((rank, 128), 0)
    lane = iota((rank, 128), 1)
    eye = (row + rank == lane).astype(F32)
    work = jnp.concatenate([gram, jnp.zeros((rank, 128 - rank), F32)], axis=1) + eye
    for first in range(0, rank, 4):
        heads = [work[first + i : first + i + 1] for i in range(4)]
        sides = [
            jnp.broadcast_to(work[:, first + i : first + i + 1], (rank, 128)) for i in range(4)
        ]
        taken = 0.0
        for i in range(4):
            pivot = first + i
            factor = sides[i] / sides[i][pivot : pivot + 1]
            factor = jnp.where(row > pivot, factor, 0.0)
            taken = taken + factor * heads[i]
            for k in range(i + 1, 4):
                sides[k] = sides[k] - factor * sides[k][pivot : pivot + 1]
                heads[k] = heads[k] - factor[first + k : first + k + 1] * heads[i]
        work = work - taken
    diagonal = jnp.sum(jnp.where(row == lane, work, 0.0), axis=1, keepdims=True)
    result = work[:, rank : 2 * rank] * lax.rsqrt(diagonal)
    inverse[...] = result
    scaled = result * math.sqrt(SLICES * share)
    scaled = jnp.concatenate(pieces(scaled, 3), axis=0)
    count = basis.shape[1] // share
    for i in range(count):
        out = dot(scaled, columns[half * count + i], 1, 0)
        out = out[:rank] + out[rank : 2 * rank] + out[2 * rank :]
        basis[:, i * share : (i + 1) * share] = out


def coeffs_kernel(scale, inverse, *refs):
    blocks, out = refs[:-1], refs[-1]
    rank, size = blocks[0].shape
    left = jnp.concatenate(pieces(inverse[...] * scale, 3), axis=0)
    left = jnp.concatenate([left] * SLICES, axis=1)
    for i in range(len(blocks) // SLICES):
        right = jnp.concatenate([b[...] for b in blocks[i * SLICES : (i + 1) * SLICES]], axis=0)
        part = dot(left, right, 1, 0)
        out[:, i * size : (i + 1) * size] = part[:rank] + part[rank : 2 * rank] + part[2 * rank :]


def mask_kernel(groups, own, pair, out):
    core = position()[0]
    lanes, rows = out.shape
    rows = rows // 2
    top, tok = own.shape[0] // 2, own.shape[1]
    rank = lanes // (lax.axis_size("expert") // groups)
    pick = (iota((tok, rows), 1) // top == iota((tok, rows), 0)).astype(BF16)
    here = iota((top, rows), 1) % top == iota((top, rows), 0)
    block = iota((lanes, 1), 0) // rank * groups + (core if groups == 2 else 0)
    for i, pairs in enumerate((own, pair)):
        names = dot(pairs[:top].astype(BF16), pick, 1, 0)
        weights = sum(dot(piece, pick, 1, 0) for piece in pieces(pairs[top:], 3))
        names = jnp.sum(jnp.where(here, names, 0.0), axis=0, keepdims=True)
        weights = jnp.sum(jnp.where(here, weights, 0.0), axis=0, keepdims=True)
        masked = jnp.where(names == block.astype(F32), weights, 0.0)
        out[:, i * rows : (i + 1) * rows] = masked


def terms_kernel(low, tok, z0, z1, z2, z3, mask, mine, other, *refs):
    outs, (work, spread) = refs[:-2], refs[-2:]
    lower = position()[1]
    lanes, rows = mask.shape
    rows = rows // 2
    rank = lanes // (SLICES * low)
    z = 0.0
    for block in (z0, z1, z2, z3):
        z = z + block[...].astype(F32)
    repeat = iota((2 * tok, 2 * rows), 1) // (rows // tok) == iota((2 * tok, 2 * rows), 0)
    z = dot(z.astype(BF16), repeat.astype(BF16), 0, 0)
    work[...] = (z * mask[...]).astype(BF16)
    for r in range(low):
        for j in range(SLICES):
            start = pl.multiple_of((j * low + (lower ^ r)) * rank, rank)
            spread[(r * SLICES + j) * rank : (r * SLICES + j + 1) * rank] = work[
                pl.ds(start, rank)
            ]
    for chunk in range(len(outs) // low):
        block, width = outs[chunk * low].shape
        here = slice(chunk * width, (chunk + 1) * width)
        part = dot(spread[:, :rows], mine[:, here], 1, 0)
        part = (part + dot(spread[:, rows:], other[:, here], 1, 0)).astype(BF16)
        for r in range(low):
            outs[chunk * low + r][...] = part[r * block : (r + 1) * block]


def shards(tokens, expert_ids, route_probs, cotangents, sketch):
    n_expert = lax.axis_size("expert")
    n_dp = lax.axis_size("dp")
    count = n_expert * n_dp
    line = count // SLICES
    low = line // 2
    groups = 2 // n_dp
    tok, width = tokens.shape
    top = expert_ids.shape[1]
    hidden, rank = sketch.shape
    rows = tok * top
    share = width // SLICES
    lanes = count // 2 * rank
    part = hidden // n_dp
    scale = 1.0 / math.sqrt(rows)
    _, lower, place, half = position()
    limit = LIMIT if n_dp == 1 else LARGE
    shape = jax.ShapeDtypeStruct

    def exchange(block, step):
        return lax.ppermute(block, AXES, [(i, i ^ step) for i in range(count)])

    cot = cotangents.reshape(rows, hidden)

    *blocks, pairs = call(
        functools.partial(first_kernel, groups),
        [shape((tok, groups * lanes + share), BF16)] * SLICES + [shape((2 * top, tok), F32)],
        [HBM] * 5,
        [
            pltpu.VMEM((rows, hidden), BF16),
            pltpu.VMEM((rank, hidden), F32),
            pltpu.VMEM((top, tok), jnp.int32),
            pltpu.VMEM((top, tok), F32),
            pltpu.SemaphoreType.DMA((8,)),
            pltpu.SemaphoreType.DMA((SLICES,)),
        ],
        tokens,
        cot,
        sketch.T,
        expert_ids.T,
        route_probs.T,
        limit=LARGE,
    )
    blocks = blocks[:1] + [exchange(blocks[j], j * line) for j in range(1, SLICES)]

    pairs, send = lax.optimization_barrier((pairs, cot))
    pairs = [pairs, exchange(pairs, 1)]
    mine = cot
    if n_dp > 1:
        mine = lax.dynamic_slice_in_dim(cot, half * part, part, axis=1)
        send = lax.dynamic_slice_in_dim(send, (1 - half) * part, part, axis=1)
    other = exchange(send, 1)

    near = [[jnp.concatenate(blocks[i : i + 2], axis=0)] for i in range(0, SLICES, 2)]
    step = 2
    while step < line:
        near = [side + [exchange(b, step) for b in side] for side in near]
        step *= 2
    n = len(near[0])
    skip = lanes if groups == 2 else 0

    far = [exchange(b[:, skip:], 1) for b in near[0]]
    if n_dp == 1:
        work = [
            pltpu.VMEM((4 * n * tok, share), BF16),
            pltpu.VMEM((4 * n * tok, lanes), BF16),
            pltpu.SemaphoreType.DMA((4 * n,)),
        ]
        [columns] = call(
            functools.partial(columns_kernel, n),
            [shape((lanes, share), F32)],
            [HBM] * (2 * n),
            work,
            *near[0],
            *far,
        )
        near[1], columns = lax.optimization_barrier((near[1], columns))
        zs = call(
            functools.partial(z_kernel, n, low),
            [shape((2 * tok, lanes), BF16)] * SLICES + [shape((rank, share), BF16)] * SLICES,
            [VMEM] * 3 + [HBM] * (2 * n),
            work[:2] + [pltpu.VMEM((lanes, share), BF16)] + work[2:],
            columns,
            near[0][0],
            far[0],
            *near[1],
            *[exchange(b[:, skip:], 1) for b in near[1]],
        )
    else:
        far = [far, [exchange(b[:, skip:], 1) for b in near[1]]]
        rows_all = jnp.concatenate(near[0] + far[0] + near[1] + far[1], axis=0)
        columns = dot(rows_all[:, :lanes], rows_all[:, lanes:], 0, 0).astype(BF16)
        zs, own = [], []
        for j in range(SLICES):
            here = slice(j % 2 * tok, (j % 2 + 1) * tok)
            x = jnp.concatenate([near[j // 2][0][here], far[j // 2][0][here]], axis=0)
            start = ((place ^ j) * low + lower) * rank
            own.append(lax.dynamic_slice_in_dim(columns, start, rank, axis=0))
            zs.append(dot(x[:, lanes:], columns, 1, 1).astype(BF16))
        zs = zs + own
    columns = zs[SLICES:]
    zs = list(zs[:1]) + [exchange(zs[j], j * line) for j in range(1, SLICES)]

    [mask] = call(
        functools.partial(mask_kernel, groups),
        [shape((lanes, 2 * rows), F32)],
        [VMEM] * 2,
        [],
        *pairs,
        limit=limit,
    )
    piece = part // CHUNKS
    terms = call(
        functools.partial(terms_kernel, low, tok),
        [shape((SLICES * rank, piece), BF16)] * (low * CHUNKS),
        [VMEM] * (SLICES + 3),
        [pltpu.VMEM((lanes, 2 * rows), BF16)] * 2,
        *zs,
        mask,
        mine,
        other,
        limit=limit,
    )
    columns, _ = lax.optimization_barrier((columns, exchange(terms[0][:16, :128], 1)))
    columns = list(columns[:1]) + [exchange(columns[j], j * line) for j in range(1, SLICES)]
    inverse, basis = call(
        inverse_kernel,
        [shape((rank, rank), F32), shape((rank, width // n_dp), F32)],
        [VMEM] * SLICES,
        [pltpu.VMEM((SLICES, rank, share), BF16)],
        *columns,
    )
    sums = []
    for chunk in range(CHUNKS):
        blocks = terms[chunk * low : (chunk + 1) * low]
        blocks = [term.reshape(SLICES, rank, piece) for term in blocks]
        step = 2
        while len(blocks) > 1:
            blocks = [
                (keep.astype(F32) + exchange(send, step).astype(F32)).astype(BF16)
                for keep, send in zip(blocks[::2], blocks[1::2])
            ]
            step *= 2
        sums.append(blocks[0])
    sums[-1], inverse = lax.optimization_barrier((sums[-1], inverse))
    blocks = []
    for block in sums:
        own = [lax.dynamic_index_in_dim(block, place ^ j, 0, False) for j in range(SLICES)]
        blocks += own[:1] + [exchange(own[j], j * line) for j in range(1, SLICES)]
    [coeffs] = call(
        functools.partial(coeffs_kernel, scale),
        [shape((rank, part), F32)],
        [VMEM] * (1 + len(blocks)),
        [],
        inverse,
        *blocks,
    )
    return basis[None], coeffs[None]


def solution(mesh):
    in_specs = (
        P(("group", "expert", "dp"), None),
        P(("group", "expert", "dp"), None),
        P(("group", "expert", "dp"), None),
        P(("group", "expert", "dp"), None, None),
        P(),
    )
    out_specs = (P(("group", "expert"), None, "dp"), P(("group", "expert"), None, "dp"))
    return jax.shard_map(shards, mesh=mesh, in_specs=in_specs, out_specs=out_specs, check_vma=False)
```

```python
import functools
import math

import jax
import jax.numpy as jnp
from jax import lax
from jax.experimental import pallas as pl
from jax.experimental.pallas import tpu as pltpu
from jax.sharding import PartitionSpec as P

AXES = ("expert", "dp")
CHUNKS = 2
SLICES = 4
LIMIT = 12 * 1024 * 1024
LARGE = 56 * 1024 * 1024
VMEM = pl.BlockSpec(memory_space=pltpu.VMEM)
HBM = pl.BlockSpec(memory_space=pltpu.HBM)
BF16 = jnp.bfloat16
F32 = jnp.float32


def dot(left, right, left_dim, right_dim):
    dims = (((left_dim,), (right_dim,)), ((), ()))
    return lax.dot_general(left, right, dims, preferred_element_type=F32)


def iota(shape, dim):
    return lax.broadcasted_iota(jnp.int32, shape, dim)


def position():
    half = lax.axis_index("dp")
    me = lax.axis_index("expert") * lax.axis_size("dp") + half
    line = lax.axis_size("expert") * lax.axis_size("dp") // SLICES
    return me % 2, me // 2 % (line // 2), me // line, half


def call(body, shapes, spaces, scratch, *args, limit=LIMIT, cost=1):
    return pl.pallas_call(
        body,
        out_shape=shapes,
        in_specs=spaces,
        out_specs=[VMEM] * len(shapes),
        scratch_shapes=scratch,
        compiler_params=pltpu.CompilerParams(vmem_limit_bytes=limit),
        cost_estimate=pl.CostEstimate(flops=cost, bytes_accessed=cost, transcendentals=0),
    )(*args)


def pieces(value, count):
    terms = []
    for _ in range(count):
        terms.append(value.astype(BF16))
        value = value - terms[-1].astype(F32)
    return terms


def pair_columns(ids, probs):
    top, tok = ids.shape
    rows = tok * top
    pick = (iota((rows, tok), 0) // top == iota((rows, tok), 1)).astype(BF16)
    here = iota((rows, top), 0) % top == iota((rows, top), 1)
    names = dot(pick, ids.astype(BF16), 1, 1)
    weights, rest = jnp.zeros((rows, top), F32), probs
    for _ in range(3):
        piece = rest.astype(BF16)
        weights = weights + dot(pick, piece, 1, 1)
        rest = rest - piece.astype(F32)
    names = jnp.sum(jnp.where(here, names, 0.0), axis=1, keepdims=True)
    weights = jnp.sum(jnp.where(here, weights, 0.0), axis=1, keepdims=True)
    return names, weights


def load(pairs, sems):
    copies = [pltpu.make_async_copy(src, dst, sems.at[i]) for i, (src, dst) in enumerate(pairs)]
    for copy in copies:
        copy.start()
    return copies


def first_kernel(groups, tokens, cot_at, sketch_at, ids_at, probs_at, *refs):
    outs, pairs, (cot, sketch, ids, probs, sems, x_sems) = refs[:SLICES], refs[SLICES], refs[5:]
    core, _, place, _ = position()
    rows, hidden = cot.shape
    tok = pairs.shape[1]
    top = rows // tok
    rank = sketch.shape[0]
    share = tokens.shape[1] // SLICES
    lanes = (outs[0].shape[1] - share) // groups
    parts = 5
    piece = hidden // parts
    sources = [(ids_at, ids), (probs_at, probs), (sketch_at, sketch)]
    for i in range(parts):
        cut = pl.ds(i * piece, piece)
        sources.append((cot_at.at[:, cut], cot.at[:, cut]))
    copies = load(sources, sems)
    sources = []
    for j, out in enumerate(outs):
        cut = pl.ds(pl.multiple_of((place ^ j) * share, share), share)
        sources.append((tokens.at[:, cut], out.at[:, pl.ds(lanes, share)]))
    x_copies = load(sources, x_sems)
    copies[0].wait()
    copies[1].wait()
    pairs[:top] = ids[...].astype(F32)
    pairs[top:] = probs[...]
    names, weights = pair_columns(pairs[:top], pairs[top:])
    copies[2].wait()
    both = jnp.concatenate(pieces(sketch[...], 2), axis=0)
    pair = 0.0
    for i in range(parts):
        copies[3 + i].wait()
        here = slice(i * piece, (i + 1) * piece)
        pair = pair + dot(cot[:, here], both[:, here], 1, 1)
    pair = (pair[:, :rank] + pair[:, rank:]) * weights
    lane = iota((rank, lanes), 1)
    tiled = dot(pair.astype(BF16), (iota((rank, lanes), 0) == lane % rank).astype(BF16), 1, 0)
    block = iota((1, lanes), 1) // rank * groups
    pick = (iota((rows, tok), 0) // top == iota((rows, tok), 1)).astype(BF16)
    for i in range(groups):
        name = block + (core ^ i) if groups == 2 else block
        y = jnp.where(names == name.astype(F32), tiled, 0.0).astype(BF16)
        y = dot(pick, y, 0, 0).astype(BF16)
        for out in outs:
            out[:, i * (lanes + share) : i * (lanes + share) + lanes] = y
    for copy in x_copies:
        copy.wait()


def gather(near, far, x, y, sems):
    share, lanes = x.shape[1], y.shape[1]
    rows = near[0].shape[0]
    sources = []
    for i, (a, b) in enumerate(zip(near, far)):
        cut = pl.ds(2 * i * rows, rows)
        sources.append((a.at[:, pl.ds(0, lanes)], y.at[cut]))
        sources.append((a.at[:, pl.ds(lanes, share)], x.at[cut]))
        cut = pl.ds((2 * i + 1) * rows, rows)
        sources.append((b.at[:, pl.ds(0, share)], x.at[cut]))
        sources.append((b.at[:, pl.ds(share, lanes)], y.at[cut]))
    for copy in load(sources, sems):
        copy.wait()


def columns_kernel(n, *refs):
    out, x, y, sems = refs[2 * n :]
    gather(refs[:n], refs[n : 2 * n], x, y, sems)
    out[...] = dot(y[...], x[...], 0, 0)


def z_kernel(n, low, part, near_x, far_x, *refs):
    outs, (x, y, columns, sems) = refs[2 * n : -4], refs[-4:]
    _, lower, place, _ = position()
    gather(refs[:n], refs[n : 2 * n], x, y, sems)
    rank = columns.shape[0] // (SLICES * low)
    share = x.shape[1]
    lanes = y.shape[1]
    rows = near_x.shape[0]
    tok = rows // 2
    total = (part[...] + dot(y[...], x[...], 0, 0)).astype(BF16)
    columns[...] = total
    own = jnp.concatenate([near_x[:, lanes : lanes + share], far_x[:, :share]], axis=0)
    halves = [dot(own, total, 1, 1), dot(x[: 2 * rows], total, 1, 1)]
    for j in range(SLICES):
        half = halves[j // 2].astype(BF16)
        start = j % 2 * tok
        outs[j][:tok] = half[start : start + tok]
        outs[j][tok:] = half[rows + start : rows + start + tok]
        expert = (place ^ j) * low + lower
        outs[SLICES + j][...] = columns[pl.ds(pl.multiple_of(expert * rank, rank), rank)]


def inverse_kernel(c0, c1, c2, c3, inverse, basis, columns):
    _, _, place, half = position()
    rank = inverse.shape[0]
    _, _, share = columns.shape
    gram = 0.0
    for j, block in enumerate((c0, c1, c2, c3)):
        columns[place ^ j] = block[...]
        gram = gram + dot(block[...], block[...], 1, 1)
    row = iota((rank, 128), 0)
    lane = iota((rank, 128), 1)
    eye = (row + rank == lane).astype(F32)
    work = jnp.concatenate([gram, jnp.zeros((rank, 128 - rank), F32)], axis=1) + eye
    for first in range(0, rank, 4):
        heads = [work[first + i : first + i + 1] for i in range(4)]
        sides = [
            jnp.broadcast_to(work[:, first + i : first + i + 1], (rank, 128)) for i in range(4)
        ]
        taken = 0.0
        for i in range(4):
            pivot = first + i
            factor = sides[i] / sides[i][pivot : pivot + 1]
            factor = jnp.where(row > pivot, factor, 0.0)
            taken = taken + factor * heads[i]
            for k in range(i + 1, 4):
                sides[k] = sides[k] - factor * sides[k][pivot : pivot + 1]
                heads[k] = heads[k] - factor[first + k : first + k + 1] * heads[i]
        work = work - taken
    diagonal = jnp.sum(jnp.where(row == lane, work, 0.0), axis=1, keepdims=True)
    result = work[:, rank : 2 * rank] * lax.rsqrt(diagonal)
    inverse[...] = result
    scaled = result * math.sqrt(SLICES * share)
    scaled = jnp.concatenate(pieces(scaled, 3), axis=0)
    count = basis.shape[1] // share
    for i in range(count):
        out = dot(scaled, columns[half * count + i], 1, 0)
        out = out[:rank] + out[rank : 2 * rank] + out[2 * rank :]
        basis[:, i * share : (i + 1) * share] = out


def coeffs_kernel(scale, inverse, *refs):
    blocks, out = refs[:-1], refs[-1]
    rank, size = blocks[0].shape
    left = jnp.concatenate(pieces(inverse[...] * scale, 3), axis=0)
    left = jnp.concatenate([left] * SLICES, axis=1)
    for i in range(len(blocks) // SLICES):
        right = jnp.concatenate([b[...] for b in blocks[i * SLICES : (i + 1) * SLICES]], axis=0)
        part = dot(left, right, 1, 0)
        out[:, i * size : (i + 1) * size] = part[:rank] + part[rank : 2 * rank] + part[2 * rank :]


def mask_kernel(groups, own, pair, out):
    core = position()[0]
    lanes, rows = out.shape
    rows = rows // 2
    top, tok = own.shape[0] // 2, own.shape[1]
    rank = lanes // (lax.axis_size("expert") // groups)
    pick = (iota((tok, rows), 1) // top == iota((tok, rows), 0)).astype(BF16)
    here = iota((top, rows), 1) % top == iota((top, rows), 0)
    block = iota((lanes, 1), 0) // rank * groups + (core if groups == 2 else 0)
    for i, pairs in enumerate((own, pair)):
        names = dot(pairs[:top].astype(BF16), pick, 1, 0)
        weights = sum(dot(piece, pick, 1, 0) for piece in pieces(pairs[top:], 3))
        names = jnp.sum(jnp.where(here, names, 0.0), axis=0, keepdims=True)
        weights = jnp.sum(jnp.where(here, weights, 0.0), axis=0, keepdims=True)
        masked = jnp.where(names == block.astype(F32), weights, 0.0)
        out[:, i * rows : (i + 1) * rows] = masked


def terms_kernel(low, tok, z0, z1, z2, z3, mask, mine, other, *refs):
    outs, (work, spread) = refs[:-2], refs[-2:]
    lower = position()[1]
    lanes, rows = mask.shape
    rows = rows // 2
    rank = lanes // (SLICES * low)
    z = 0.0
    for block in (z0, z1, z2, z3):
        z = z + block[...].astype(F32)
    repeat = iota((2 * tok, 2 * rows), 1) // (rows // tok) == iota((2 * tok, 2 * rows), 0)
    z = dot(z.astype(BF16), repeat.astype(BF16), 0, 0)
    work[...] = (z * mask[...]).astype(BF16)
    for r in range(low):
        for j in range(SLICES):
            start = pl.multiple_of((j * low + (lower ^ r)) * rank, rank)
            spread[(r * SLICES + j) * rank : (r * SLICES + j + 1) * rank] = work[
                pl.ds(start, rank)
            ]
    for chunk in range(len(outs) // low):
        block, width = outs[chunk * low].shape
        here = slice(chunk * width, (chunk + 1) * width)
        part = dot(spread[:, :rows], mine[:, here], 1, 0)
        part = (part + dot(spread[:, rows:], other[:, here], 1, 0)).astype(BF16)
        for r in range(low):
            outs[chunk * low + r][...] = part[r * block : (r + 1) * block]


def shards(tokens, expert_ids, route_probs, cotangents, sketch):
    n_expert = lax.axis_size("expert")
    n_dp = lax.axis_size("dp")
    count = n_expert * n_dp
    line = count // SLICES
    low = line // 2
    groups = 2 // n_dp
    tok, width = tokens.shape
    top = expert_ids.shape[1]
    hidden, rank = sketch.shape
    rows = tok * top
    share = width // SLICES
    lanes = count // 2 * rank
    part = hidden // n_dp
    scale = 1.0 / math.sqrt(rows)
    _, lower, place, half = position()
    limit = LIMIT if n_dp == 1 else LARGE
    shape = jax.ShapeDtypeStruct

    def exchange(block, step):
        return lax.ppermute(block, AXES, [(i, i ^ step) for i in range(count)])

    cot = cotangents.reshape(rows, hidden)

    *blocks, pairs = call(
        functools.partial(first_kernel, groups),
        [shape((tok, groups * lanes + share), BF16)] * SLICES + [shape((2 * top, tok), F32)],
        [HBM] * 5,
        [
            pltpu.VMEM((rows, hidden), BF16),
            pltpu.VMEM((rank, hidden), F32),
            pltpu.VMEM((top, tok), jnp.int32),
            pltpu.VMEM((top, tok), F32),
            pltpu.SemaphoreType.DMA((8,)),
            pltpu.SemaphoreType.DMA((SLICES,)),
        ],
        tokens,
        cot,
        sketch.T,
        expert_ids.T,
        route_probs.T,
        limit=LARGE,
    )
    blocks = blocks[:1] + [exchange(blocks[j], j * line) for j in range(1, SLICES)]

    pairs, send = lax.optimization_barrier((pairs, cot))
    pairs = [pairs, exchange(pairs, 1)]
    mine = cot
    if n_dp > 1:
        mine = lax.dynamic_slice_in_dim(cot, half * part, part, axis=1)
        send = lax.dynamic_slice_in_dim(send, (1 - half) * part, part, axis=1)
    other = exchange(send, 1)

    near = [[jnp.concatenate(blocks[i : i + 2], axis=0)] for i in range(0, SLICES, 2)]
    step = 2
    while step < line:
        near = [side + [exchange(b, step) for b in side] for side in near]
        step *= 2
    n = len(near[0])
    skip = lanes if groups == 2 else 0

    far = [exchange(b[:, skip:], 1) for b in near[0]]
    if n_dp == 1:
        work = [
            pltpu.VMEM((4 * n * tok, share), BF16),
            pltpu.VMEM((4 * n * tok, lanes), BF16),
            pltpu.SemaphoreType.DMA((4 * n,)),
        ]
        [columns] = call(
            functools.partial(columns_kernel, n),
            [shape((lanes, share), F32)],
            [HBM] * (2 * n),
            work,
            *near[0],
            *far,
        )
        near[1], columns = lax.optimization_barrier((near[1], columns))
        zs = call(
            functools.partial(z_kernel, n, low),
            [shape((2 * tok, lanes), BF16)] * SLICES + [shape((rank, share), BF16)] * SLICES,
            [VMEM] * 3 + [HBM] * (2 * n),
            work[:2] + [pltpu.VMEM((lanes, share), BF16)] + work[2:],
            columns,
            near[0][0],
            far[0],
            *near[1],
            *[exchange(b[:, skip:], 1) for b in near[1]],
        )
    else:
        far = [far, [exchange(b[:, skip:], 1) for b in near[1]]]
        rows_all = jnp.concatenate(near[0] + far[0] + near[1] + far[1], axis=0)
        columns = dot(rows_all[:, :lanes], rows_all[:, lanes:], 0, 0).astype(BF16)
        zs, own = [], []
        for j in range(SLICES):
            here = slice(j % 2 * tok, (j % 2 + 1) * tok)
            x = jnp.concatenate([near[j // 2][0][here], far[j // 2][0][here]], axis=0)
            start = ((place ^ j) * low + lower) * rank
            own.append(lax.dynamic_slice_in_dim(columns, start, rank, axis=0))
            zs.append(dot(x[:, lanes:], columns, 1, 1).astype(BF16))
        zs = zs + own
    columns = zs[SLICES:]
    zs = list(zs[:1]) + [exchange(zs[j], j * line) for j in range(1, SLICES)]

    [mask] = call(
        functools.partial(mask_kernel, groups),
        [shape((lanes, 2 * rows), F32)],
        [VMEM] * 2,
        [],
        *pairs,
        limit=limit,
    )
    piece = part // CHUNKS
    terms = call(
        functools.partial(terms_kernel, low, tok),
        [shape((SLICES * rank, piece), BF16)] * (low * CHUNKS),
        [VMEM] * (SLICES + 3),
        [pltpu.VMEM((lanes, 2 * rows), BF16)] * 2,
        *zs,
        mask,
        mine,
        other,
        limit=limit,
    )
    columns = list(columns[:1]) + [exchange(columns[j], j * line) for j in range(1, SLICES)]
    inverse, basis = call(
        inverse_kernel,
        [shape((rank, rank), F32), shape((rank, width // n_dp), F32)],
        [VMEM] * SLICES,
        [pltpu.VMEM((SLICES, rank, share), BF16)],
        *columns,
        cost=10_000_000,
    )
    sums = []
    for chunk in range(CHUNKS):
        blocks = terms[chunk * low : (chunk + 1) * low]
        blocks = [term.reshape(SLICES, rank, piece) for term in blocks]
        step = 2
        while len(blocks) > 1:
            blocks = [
                (keep.astype(F32) + exchange(send, step).astype(F32)).astype(BF16)
                for keep, send in zip(blocks[::2], blocks[1::2])
            ]
            step *= 2
        sums.append(blocks[0])
    sums[-1], inverse = lax.optimization_barrier((sums[-1], inverse))
    blocks = []
    for block in sums:
        own = [lax.dynamic_index_in_dim(block, place ^ j, 0, False) for j in range(SLICES)]
        blocks += own[:1] + [exchange(own[j], j * line) for j in range(1, SLICES)]
    [coeffs] = call(
        functools.partial(coeffs_kernel, scale),
        [shape((rank, part), F32)],
        [VMEM] * (1 + len(blocks)),
        [],
        inverse,
        *blocks,
    )
    return basis[None], coeffs[None]


def solution(mesh):
    in_specs = (
        P(("group", "expert", "dp"), None),
        P(("group", "expert", "dp"), None),
        P(("group", "expert", "dp"), None),
        P(("group", "expert", "dp"), None, None),
        P(),
    )
    out_specs = (P(("group", "expert"), None, "dp"), P(("group", "expert"), None, "dp"))
    return jax.shard_map(shards, mesh=mesh, in_specs=in_specs, out_specs=out_specs, check_vma=False)
```

```python
import functools
import math

import jax
import jax.numpy as jnp
from jax import lax
from jax.experimental import pallas as pl
from jax.experimental.pallas import tpu as pltpu
from jax.sharding import PartitionSpec as P

AXES = ("expert", "dp")
CHUNKS = 2
SLICES = 4
LIMIT = 12 * 1024 * 1024
LARGE = 56 * 1024 * 1024
VMEM = pl.BlockSpec(memory_space=pltpu.VMEM)
HBM = pl.BlockSpec(memory_space=pltpu.HBM)
BF16 = jnp.bfloat16
F32 = jnp.float32


def dot(left, right, left_dim, right_dim):
    dims = (((left_dim,), (right_dim,)), ((), ()))
    return lax.dot_general(left, right, dims, preferred_element_type=F32)


def iota(shape, dim):
    return lax.broadcasted_iota(jnp.int32, shape, dim)


def position():
    half = lax.axis_index("dp")
    me = lax.axis_index("expert") * lax.axis_size("dp") + half
    line = lax.axis_size("expert") * lax.axis_size("dp") // SLICES
    return me % 2, me // 2 % (line // 2), me // line, half


def call(body, shapes, spaces, scratch, *args, limit=LIMIT):
    return pl.pallas_call(
        body,
        out_shape=shapes,
        in_specs=spaces,
        out_specs=[VMEM] * len(shapes),
        scratch_shapes=scratch,
        compiler_params=pltpu.CompilerParams(vmem_limit_bytes=limit),
        cost_estimate=pl.CostEstimate(flops=1, bytes_accessed=1, transcendentals=0),
    )(*args)


def pieces(value, count):
    terms = []
    for _ in range(count):
        terms.append(value.astype(BF16))
        value = value - terms[-1].astype(F32)
    return terms


def pair_columns(ids, probs):
    top, tok = ids.shape
    rows = tok * top
    pick = (iota((rows, tok), 0) // top == iota((rows, tok), 1)).astype(BF16)
    here = iota((rows, top), 0) % top == iota((rows, top), 1)
    names = dot(pick, ids.astype(BF16), 1, 1)
    weights, rest = jnp.zeros((rows, top), F32), probs
    for _ in range(3):
        piece = rest.astype(BF16)
        weights = weights + dot(pick, piece, 1, 1)
        rest = rest - piece.astype(F32)
    names = jnp.sum(jnp.where(here, names, 0.0), axis=1, keepdims=True)
    weights = jnp.sum(jnp.where(here, weights, 0.0), axis=1, keepdims=True)
    return names, weights


def load(pairs, sems):
    copies = [pltpu.make_async_copy(src, dst, sems.at[i]) for i, (src, dst) in enumerate(pairs)]
    for copy in copies:
        copy.start()
    return copies


def first_kernel(groups, tokens, cot_at, sketch_at, ids_at, probs_at, *refs):
    outs, pairs, (cot, sketch, ids, probs, sems, x_sems) = refs[:SLICES], refs[SLICES], refs[5:]
    core, _, place, _ = position()
    rows, hidden = cot.shape
    tok = pairs.shape[1]
    top = rows // tok
    rank = sketch.shape[0]
    share = tokens.shape[1] // SLICES
    lanes = (outs[0].shape[1] - share) // groups
    parts = 5
    piece = hidden // parts
    sources = [(ids_at, ids), (probs_at, probs), (sketch_at, sketch)]
    for i in range(parts):
        cut = pl.ds(i * piece, piece)
        sources.append((cot_at.at[:, cut], cot.at[:, cut]))
    copies = load(sources, sems)
    sources = []
    for j, out in enumerate(outs):
        cut = pl.ds(pl.multiple_of((place ^ j) * share, share), share)
        sources.append((tokens.at[:, cut], out.at[:, pl.ds(lanes, share)]))
    x_copies = load(sources, x_sems)
    copies[0].wait()
    copies[1].wait()
    pairs[:top] = ids[...].astype(F32)
    pairs[top:] = probs[...]
    names, weights = pair_columns(pairs[:top], pairs[top:])
    copies[2].wait()
    both = jnp.concatenate(pieces(sketch[...], 2), axis=0)
    pair = 0.0
    for i in range(parts):
        copies[3 + i].wait()
        here = slice(i * piece, (i + 1) * piece)
        pair = pair + dot(cot[:, here], both[:, here], 1, 1)
    pair = (pair[:, :rank] + pair[:, rank:]) * weights
    lane = iota((rank, lanes), 1)
    tiled = dot(pair.astype(BF16), (iota((rank, lanes), 0) == lane % rank).astype(BF16), 1, 0)
    block = iota((1, lanes), 1) // rank * groups
    pick = (iota((rows, tok), 0) // top == iota((rows, tok), 1)).astype(BF16)
    for i in range(groups):
        name = block + (core ^ i) if groups == 2 else block
        y = jnp.where(names == name.astype(F32), tiled, 0.0).astype(BF16)
        y = dot(pick, y, 0, 0).astype(BF16)
        for out in outs:
            out[:, i * (lanes + share) : i * (lanes + share) + lanes] = y
    for copy in x_copies:
        copy.wait()


def gather(near, far, x, y, sems):
    share, lanes = x.shape[1], y.shape[1]
    rows = near[0].shape[0]
    sources = []
    for i, (a, b) in enumerate(zip(near, far)):
        cut = pl.ds(2 * i * rows, rows)
        sources.append((a.at[:, pl.ds(0, lanes)], y.at[cut]))
        sources.append((a.at[:, pl.ds(lanes, share)], x.at[cut]))
        cut = pl.ds((2 * i + 1) * rows, rows)
        sources.append((b.at[:, pl.ds(0, share)], x.at[cut]))
        sources.append((b.at[:, pl.ds(share, lanes)], y.at[cut]))
    for copy in load(sources, sems):
        copy.wait()


def columns_kernel(n, *refs):
    out, x, y, sems = refs[2 * n :]
    gather(refs[:n], refs[n : 2 * n], x, y, sems)
    out[...] = dot(y[...], x[...], 0, 0)


def z_kernel(n, low, part, near_x, far_x, *refs):
    outs, (x, y, columns, sems) = refs[2 * n : -4], refs[-4:]
    _, lower, place, _ = position()
    gather(refs[:n], refs[n : 2 * n], x, y, sems)
    rank = columns.shape[0] // (SLICES * low)
    share = x.shape[1]
    lanes = y.shape[1]
    rows = near_x.shape[0]
    tok = rows // 2
    total = (part[...] + dot(y[...], x[...], 0, 0)).astype(BF16)
    columns[...] = total
    own = jnp.concatenate([near_x[:, lanes : lanes + share], far_x[:, :share]], axis=0)
    halves = [dot(own, total, 1, 1), dot(x[: 2 * rows], total, 1, 1)]
    for j in range(SLICES):
        half = halves[j // 2].astype(BF16)
        start = j % 2 * tok
        outs[j][:tok] = half[start : start + tok]
        outs[j][tok:] = half[rows + start : rows + start + tok]
        expert = (place ^ j) * low + lower
        outs[SLICES + j][...] = columns[pl.ds(pl.multiple_of(expert * rank, rank), rank)]


def inverse_kernel(c0, c1, c2, c3, inverse, basis, columns):
    _, _, place, half = position()
    rank = inverse.shape[0]
    _, _, share = columns.shape
    gram = 0.0
    for j, block in enumerate((c0, c1, c2, c3)):
        columns[place ^ j] = block[...]
        gram = gram + dot(block[...], block[...], 1, 1)
    row = iota((rank, 128), 0)
    lane = iota((rank, 128), 1)
    eye = (row + rank == lane).astype(F32)
    work = jnp.concatenate([gram, jnp.zeros((rank, 128 - rank), F32)], axis=1) + eye
    for first in range(0, rank, 4):
        heads = [work[first + i : first + i + 1] for i in range(4)]
        sides = [
            jnp.broadcast_to(work[:, first + i : first + i + 1], (rank, 128)) for i in range(4)
        ]
        taken = 0.0
        for i in range(4):
            pivot = first + i
            factor = sides[i] / sides[i][pivot : pivot + 1]
            factor = jnp.where(row > pivot, factor, 0.0)
            taken = taken + factor * heads[i]
            for k in range(i + 1, 4):
                sides[k] = sides[k] - factor * sides[k][pivot : pivot + 1]
                heads[k] = heads[k] - factor[first + k : first + k + 1] * heads[i]
        work = work - taken
    diagonal = jnp.sum(jnp.where(row == lane, work, 0.0), axis=1, keepdims=True)
    result = work[:, rank : 2 * rank] * lax.rsqrt(diagonal)
    inverse[...] = result
    scaled = result * math.sqrt(SLICES * share)
    scaled = jnp.concatenate(pieces(scaled, 3), axis=0)
    count = basis.shape[1] // share
    for i in range(count):
        out = dot(scaled, columns[half * count + i], 1, 0)
        out = out[:rank] + out[rank : 2 * rank] + out[2 * rank :]
        basis[:, i * share : (i + 1) * share] = out


def coeffs_kernel(scale, inverse, *refs):
    blocks, out = refs[:-1], refs[-1]
    rank, size = blocks[0].shape
    left = jnp.concatenate(pieces(inverse[...] * scale, 3), axis=0)
    left = jnp.concatenate([left] * SLICES, axis=1)
    for i in range(len(blocks) // SLICES):
        right = jnp.concatenate([b[...] for b in blocks[i * SLICES : (i + 1) * SLICES]], axis=0)
        part = dot(left, right, 1, 0)
        out[:, i * size : (i + 1) * size] = part[:rank] + part[rank : 2 * rank] + part[2 * rank :]


def mask_kernel(groups, own, pair, out):
    core = position()[0]
    lanes, rows = out.shape
    rows = rows // 2
    top, tok = own.shape[0] // 2, own.shape[1]
    rank = lanes // (lax.axis_size("expert") // groups)
    pick = (iota((tok, rows), 1) // top == iota((tok, rows), 0)).astype(BF16)
    here = iota((top, rows), 1) % top == iota((top, rows), 0)
    block = iota((lanes, 1), 0) // rank * groups + (core if groups == 2 else 0)
    for i, pairs in enumerate((own, pair)):
        names = dot(pairs[:top].astype(BF16), pick, 1, 0)
        weights = sum(dot(piece, pick, 1, 0) for piece in pieces(pairs[top:], 3))
        names = jnp.sum(jnp.where(here, names, 0.0), axis=0, keepdims=True)
        weights = jnp.sum(jnp.where(here, weights, 0.0), axis=0, keepdims=True)
        masked = jnp.where(names == block.astype(F32), weights, 0.0)
        out[:, i * rows : (i + 1) * rows] = masked


def terms_kernel(low, tok, z0, z1, z2, z3, mask, mine, other, *refs):
    outs, (work, spread) = refs[:-2], refs[-2:]
    lower = position()[1]
    lanes, rows = mask.shape
    rows = rows // 2
    rank = lanes // (SLICES * low)
    z = 0.0
    for block in (z0, z1, z2, z3):
        z = z + block[...].astype(F32)
    repeat = iota((2 * tok, 2 * rows), 1) // (rows // tok) == iota((2 * tok, 2 * rows), 0)
    z = dot(z.astype(BF16), repeat.astype(BF16), 0, 0)
    work[...] = (z * mask[...]).astype(BF16)
    for r in range(low):
        for j in range(SLICES):
            start = pl.multiple_of((j * low + (lower ^ r)) * rank, rank)
            spread[(r * SLICES + j) * rank : (r * SLICES + j + 1) * rank] = work[
                pl.ds(start, rank)
            ]
    for chunk in range(len(outs) // low):
        block, width = outs[chunk * low].shape
        here = slice(chunk * width, (chunk + 1) * width)
        part = dot(spread[:, :rows], mine[:, here], 1, 0)
        part = (part + dot(spread[:, rows:], other[:, here], 1, 0)).astype(BF16)
        for r in range(low):
            outs[chunk * low + r][...] = part[r * block : (r + 1) * block]


def shards(tokens, expert_ids, route_probs, cotangents, sketch):
    n_expert = lax.axis_size("expert")
    n_dp = lax.axis_size("dp")
    count = n_expert * n_dp
    line = count // SLICES
    low = line // 2
    groups = 2 // n_dp
    tok, width = tokens.shape
    top = expert_ids.shape[1]
    hidden, rank = sketch.shape
    rows = tok * top
    share = width // SLICES
    lanes = count // 2 * rank
    part = hidden // n_dp
    scale = 1.0 / math.sqrt(rows)
    _, lower, place, half = position()
    limit = LIMIT if n_dp == 1 else LARGE
    shape = jax.ShapeDtypeStruct

    def exchange(block, step):
        return lax.ppermute(block, AXES, [(i, i ^ step) for i in range(count)])

    cot = cotangents.reshape(rows, hidden)

    *blocks, pairs = call(
        functools.partial(first_kernel, groups),
        [shape((tok, groups * lanes + share), BF16)] * SLICES + [shape((2 * top, tok), F32)],
        [HBM] * 5,
        [
            pltpu.VMEM((rows, hidden), BF16),
            pltpu.VMEM((rank, hidden), F32),
            pltpu.VMEM((top, tok), jnp.int32),
            pltpu.VMEM((top, tok), F32),
            pltpu.SemaphoreType.DMA((8,)),
            pltpu.SemaphoreType.DMA((SLICES,)),
        ],
        tokens,
        cot,
        sketch.T,
        expert_ids.T,
        route_probs.T,
        limit=LARGE,
    )
    blocks = blocks[:1] + [exchange(blocks[j], j * line) for j in range(1, SLICES)]

    pairs, send = lax.optimization_barrier((pairs, cot))
    pairs = [pairs, exchange(pairs, 1)]
    mine = cot
    if n_dp > 1:
        mine = lax.dynamic_slice_in_dim(cot, half * part, part, axis=1)
        send = lax.dynamic_slice_in_dim(send, (1 - half) * part, part, axis=1)
    other = exchange(send, 1)

    near = [[jnp.concatenate(blocks[i : i + 2], axis=0)] for i in range(0, SLICES, 2)]
    step = 2
    while step < line:
        near = [side + [exchange(b, step) for b in side] for side in near]
        step *= 2
    n = len(near[0])
    skip = lanes if groups == 2 else 0

    far = [exchange(b[:, skip:], 1) for b in near[0]]
    if n_dp == 1:
        work = [
            pltpu.VMEM((4 * n * tok, share), BF16),
            pltpu.VMEM((4 * n * tok, lanes), BF16),
            pltpu.SemaphoreType.DMA((4 * n,)),
        ]
        [columns] = call(
            functools.partial(columns_kernel, n),
            [shape((lanes, share), F32)],
            [HBM] * (2 * n),
            work,
            *near[0],
            *far,
        )
        near[1], columns = lax.optimization_barrier((near[1], columns))
        zs = call(
            functools.partial(z_kernel, n, low),
            [shape((2 * tok, lanes), BF16)] * SLICES + [shape((rank, share), BF16)] * SLICES,
            [VMEM] * 3 + [HBM] * (2 * n),
            work[:2] + [pltpu.VMEM((lanes, share), BF16)] + work[2:],
            columns,
            near[0][0],
            far[0],
            *near[1],
            *[exchange(b[:, skip:], 1) for b in near[1]],
        )
    else:
        far = [far, [exchange(b[:, skip:], 1) for b in near[1]]]
        rows_all = jnp.concatenate(near[0] + far[0] + near[1] + far[1], axis=0)
        columns = dot(rows_all[:, :lanes], rows_all[:, lanes:], 0, 0).astype(BF16)
        zs, own = [], []
        for j in range(SLICES):
            here = slice(j % 2 * tok, (j % 2 + 1) * tok)
            x = jnp.concatenate([near[j // 2][0][here], far[j // 2][0][here]], axis=0)
            start = ((place ^ j) * low + lower) * rank
            own.append(lax.dynamic_slice_in_dim(columns, start, rank, axis=0))
            zs.append(dot(x[:, lanes:], columns, 1, 1).astype(BF16))
        zs = zs + own
    columns = zs[SLICES:]
    zs = list(zs[:1]) + [exchange(zs[j], j * line) for j in range(1, SLICES)]

    [mask] = call(
        functools.partial(mask_kernel, groups),
        [shape((lanes, 2 * rows), F32)],
        [VMEM] * 2,
        [],
        *pairs,
        limit=limit,
    )
    piece = part // CHUNKS
    terms = call(
        functools.partial(terms_kernel, low, tok),
        [shape((SLICES * rank, piece), BF16)] * (low * CHUNKS),
        [VMEM] * (SLICES + 3),
        [pltpu.VMEM((lanes, 2 * rows), BF16)] * 2,
        *zs,
        mask,
        mine,
        other,
        limit=limit,
    )
    sums = []
    for chunk in range(CHUNKS):
        blocks = terms[chunk * low : (chunk + 1) * low]
        blocks = [term.reshape(SLICES, rank, piece) for term in blocks]
        step = 2
        while len(blocks) > 1:
            blocks = [
                (keep.astype(F32) + exchange(send, step).astype(F32)).astype(BF16)
                for keep, send in zip(blocks[::2], blocks[1::2])
            ]
            step *= 2
        sums.append(blocks[0])
    columns = list(columns[:1]) + [exchange(columns[j], j * line) for j in range(1, SLICES)]
    blocks = []
    for i, block in enumerate(sums):
        if i == len(sums) - 1:
            block, inverse = lax.optimization_barrier((block, inverse))
        own = [lax.dynamic_index_in_dim(block, place ^ j, 0, False) for j in range(SLICES)]
        gone = [exchange(own[j], j * line) for j in range(1, SLICES)]
        if i == 0:
            gone[0], *columns = lax.optimization_barrier((gone[0], *columns))
            inverse, basis = call(
                inverse_kernel,
                [shape((rank, rank), F32), shape((rank, width // n_dp), F32)],
                [VMEM] * SLICES,
                [pltpu.VMEM((SLICES, rank, share), BF16)],
                *columns,
            )
        blocks += own[:1] + gone
    [coeffs] = call(
        functools.partial(coeffs_kernel, scale),
        [shape((rank, part), F32)],
        [VMEM] * (1 + len(blocks)),
        [],
        inverse,
        *blocks,
    )
    return basis[None], coeffs[None]


def solution(mesh):
    in_specs = (
        P(("group", "expert", "dp"), None),
        P(("group", "expert", "dp"), None),
        P(("group", "expert", "dp"), None),
        P(("group", "expert", "dp"), None, None),
        P(),
    )
    out_specs = (P(("group", "expert"), None, "dp"), P(("group", "expert"), None, "dp"))
    return jax.shard_map(shards, mesh=mesh, in_specs=in_specs, out_specs=out_specs, check_vma=False)
```

```python
import functools
import math

import jax
import jax.numpy as jnp
from jax import lax
from jax.experimental import pallas as pl
from jax.experimental.pallas import tpu as pltpu
from jax.sharding import PartitionSpec as P

AXES = ("expert", "dp")
CHUNKS = 2
SLICES = 4
LIMIT = 12 * 1024 * 1024
LARGE = 56 * 1024 * 1024
VMEM = pl.BlockSpec(memory_space=pltpu.VMEM)
HBM = pl.BlockSpec(memory_space=pltpu.HBM)
BF16 = jnp.bfloat16
F32 = jnp.float32


def dot(left, right, left_dim, right_dim):
    dims = (((left_dim,), (right_dim,)), ((), ()))
    return lax.dot_general(left, right, dims, preferred_element_type=F32)


def iota(shape, dim):
    return lax.broadcasted_iota(jnp.int32, shape, dim)


def position():
    half = lax.axis_index("dp")
    me = lax.axis_index("expert") * lax.axis_size("dp") + half
    line = lax.axis_size("expert") * lax.axis_size("dp") // SLICES
    return me % 2, me // 2 % (line // 2), me // line, half


def call(body, shapes, spaces, scratch, *args, limit=LIMIT):
    return pl.pallas_call(
        body,
        out_shape=shapes,
        in_specs=spaces,
        out_specs=[VMEM] * len(shapes),
        scratch_shapes=scratch,
        compiler_params=pltpu.CompilerParams(vmem_limit_bytes=limit),
        cost_estimate=pl.CostEstimate(flops=1, bytes_accessed=1, transcendentals=0),
    )(*args)


def pieces(value, count):
    terms = []
    for _ in range(count):
        terms.append(value.astype(BF16))
        value = value - terms[-1].astype(F32)
    return terms


def pair_columns(ids, probs):
    top, tok = ids.shape
    rows = tok * top
    pick = (iota((rows, tok), 0) // top == iota((rows, tok), 1)).astype(BF16)
    here = iota((rows, top), 0) % top == iota((rows, top), 1)
    names = dot(pick, ids.astype(BF16), 1, 1)
    weights, rest = jnp.zeros((rows, top), F32), probs
    for _ in range(3):
        piece = rest.astype(BF16)
        weights = weights + dot(pick, piece, 1, 1)
        rest = rest - piece.astype(F32)
    names = jnp.sum(jnp.where(here, names, 0.0), axis=1, keepdims=True)
    weights = jnp.sum(jnp.where(here, weights, 0.0), axis=1, keepdims=True)
    return names, weights


def load(pairs, sems):
    copies = [pltpu.make_async_copy(src, dst, sems.at[i]) for i, (src, dst) in enumerate(pairs)]
    for copy in copies:
        copy.start()
    return copies


def first_kernel(groups, tokens, cot_at, sketch_at, ids_at, probs_at, *refs):
    outs, pairs, (cot, sketch, ids, probs, sems, x_sems) = refs[:SLICES], refs[SLICES], refs[5:]
    core, _, place, _ = position()
    rows, hidden = cot.shape
    tok = pairs.shape[1]
    top = rows // tok
    rank = sketch.shape[0]
    share = tokens.shape[1] // SLICES
    lanes = (outs[0].shape[1] - share) // groups
    parts = 5
    piece = hidden // parts
    sources = [(ids_at, ids), (probs_at, probs), (sketch_at, sketch)]
    for i in range(parts):
        cut = pl.ds(i * piece, piece)
        sources.append((cot_at.at[:, cut], cot.at[:, cut]))
    copies = load(sources, sems)
    sources = []
    for j, out in enumerate(outs):
        cut = pl.ds(pl.multiple_of((place ^ j) * share, share), share)
        sources.append((tokens.at[:, cut], out.at[:, pl.ds(lanes, share)]))
    x_copies = load(sources, x_sems)
    copies[0].wait()
    copies[1].wait()
    pairs[:top] = ids[...].astype(F32)
    pairs[top:] = probs[...]
    names, weights = pair_columns(pairs[:top], pairs[top:])
    copies[2].wait()
    both = jnp.concatenate(pieces(sketch[...], 2), axis=0)
    pair = 0.0
    for i in range(parts):
        copies[3 + i].wait()
        here = slice(i * piece, (i + 1) * piece)
        pair = pair + dot(cot[:, here], both[:, here], 1, 1)
    pair = (pair[:, :rank] + pair[:, rank:]) * weights
    lane = iota((rank, lanes), 1)
    tiled = dot(pair.astype(BF16), (iota((rank, lanes), 0) == lane % rank).astype(BF16), 1, 0)
    block = iota((1, lanes), 1) // rank * groups
    pick = (iota((rows, tok), 0) // top == iota((rows, tok), 1)).astype(BF16)
    for i in range(groups):
        name = block + (core ^ i) if groups == 2 else block
        y = jnp.where(names == name.astype(F32), tiled, 0.0).astype(BF16)
        y = dot(pick, y, 0, 0).astype(BF16)
        for out in outs:
            out[:, i * (lanes + share) : i * (lanes + share) + lanes] = y
    for copy in x_copies:
        copy.wait()


def gather(near, far, x, y, sems):
    share, lanes = x.shape[1], y.shape[1]
    rows = near[0].shape[0]
    sources = []
    for i, (a, b) in enumerate(zip(near, far)):
        cut = pl.ds(2 * i * rows, rows)
        sources.append((a.at[:, pl.ds(0, lanes)], y.at[cut]))
        sources.append((a.at[:, pl.ds(lanes, share)], x.at[cut]))
        cut = pl.ds((2 * i + 1) * rows, rows)
        sources.append((b.at[:, pl.ds(0, share)], x.at[cut]))
        sources.append((b.at[:, pl.ds(share, lanes)], y.at[cut]))
    for copy in load(sources, sems):
        copy.wait()


def columns_kernel(n, *refs):
    out, x, y, sems = refs[2 * n :]
    gather(refs[:n], refs[n : 2 * n], x, y, sems)
    out[...] = dot(y[...], x[...], 0, 0)


def z_kernel(n, low, part, near_x, far_x, *refs):
    outs, (x, y, columns, sems) = refs[2 * n : -4], refs[-4:]
    _, lower, place, _ = position()
    gather(refs[:n], refs[n : 2 * n], x, y, sems)
    rank = columns.shape[0] // (SLICES * low)
    share = x.shape[1]
    lanes = y.shape[1]
    rows = near_x.shape[0]
    tok = rows // 2
    total = (part[...] + dot(y[...], x[...], 0, 0)).astype(BF16)
    columns[...] = total
    own = jnp.concatenate([near_x[:, lanes : lanes + share], far_x[:, :share]], axis=0)
    halves = [dot(own, total, 1, 1), dot(x[: 2 * rows], total, 1, 1)]
    for j in range(SLICES):
        half = halves[j // 2].astype(BF16)
        start = j % 2 * tok
        outs[j][:tok] = half[start : start + tok]
        outs[j][tok:] = half[rows + start : rows + start + tok]
        expert = (place ^ j) * low + lower
        outs[SLICES + j][...] = columns[pl.ds(pl.multiple_of(expert * rank, rank), rank)]


def inverse_kernel(c0, c1, c2, c3, inverse, basis, columns):
    _, _, place, half = position()
    rank = inverse.shape[0]
    _, _, share = columns.shape
    gram = 0.0
    for j, block in enumerate((c0, c1, c2, c3)):
        columns[place ^ j] = block[...]
        gram = gram + dot(block[...], block[...], 1, 1)
    row = iota((rank, 128), 0)
    lane = iota((rank, 128), 1)
    eye = (row + rank == lane).astype(F32)
    work = jnp.concatenate([gram, jnp.zeros((rank, 128 - rank), F32)], axis=1) + eye
    for first in range(0, rank, 4):
        heads = [work[first + i : first + i + 1] for i in range(4)]
        sides = [
            jnp.broadcast_to(work[:, first + i : first + i + 1], (rank, 128)) for i in range(4)
        ]
        taken = 0.0
        for i in range(4):
            pivot = first + i
            factor = sides[i] / sides[i][pivot : pivot + 1]
            factor = jnp.where(row > pivot, factor, 0.0)
            taken = taken + factor * heads[i]
            for k in range(i + 1, 4):
                sides[k] = sides[k] - factor * sides[k][pivot : pivot + 1]
                heads[k] = heads[k] - factor[first + k : first + k + 1] * heads[i]
        work = work - taken
    diagonal = jnp.sum(jnp.where(row == lane, work, 0.0), axis=1, keepdims=True)
    result = work[:, rank : 2 * rank] * lax.rsqrt(diagonal)
    inverse[...] = result
    scaled = result * math.sqrt(SLICES * share)
    scaled = jnp.concatenate(pieces(scaled, 3), axis=0)
    count = basis.shape[1] // share
    for i in range(count):
        out = dot(scaled, columns[half * count + i], 1, 0)
        out = out[:rank] + out[rank : 2 * rank] + out[2 * rank :]
        basis[:, i * share : (i + 1) * share] = out


def coeffs_kernel(scale, inverse, *refs):
    blocks, out = refs[:-1], refs[-1]
    rank, size = blocks[0].shape
    left = jnp.concatenate(pieces(inverse[...] * scale, 3), axis=0)
    left = jnp.concatenate([left] * SLICES, axis=1)
    for i in range(len(blocks) // SLICES):
        right = jnp.concatenate([b[...] for b in blocks[i * SLICES : (i + 1) * SLICES]], axis=0)
        part = dot(left, right, 1, 0)
        out[:, i * size : (i + 1) * size] = part[:rank] + part[rank : 2 * rank] + part[2 * rank :]


def mask_kernel(groups, own, pair, out):
    core = position()[0]
    lanes, rows = out.shape
    rows = rows // 2
    top, tok = own.shape[0] // 2, own.shape[1]
    rank = lanes // (lax.axis_size("expert") // groups)
    pick = (iota((tok, rows), 1) // top == iota((tok, rows), 0)).astype(BF16)
    here = iota((top, rows), 1) % top == iota((top, rows), 0)
    block = iota((lanes, 1), 0) // rank * groups + (core if groups == 2 else 0)
    for i, pairs in enumerate((own, pair)):
        names = dot(pairs[:top].astype(BF16), pick, 1, 0)
        weights = sum(dot(piece, pick, 1, 0) for piece in pieces(pairs[top:], 3))
        names = jnp.sum(jnp.where(here, names, 0.0), axis=0, keepdims=True)
        weights = jnp.sum(jnp.where(here, weights, 0.0), axis=0, keepdims=True)
        masked = jnp.where(names == block.astype(F32), weights, 0.0)
        out[:, i * rows : (i + 1) * rows] = masked


def terms_kernel(low, tok, z0, z1, z2, z3, mask, mine, other, *refs):
    outs, (work, spread) = refs[:-2], refs[-2:]
    lower = position()[1]
    lanes, rows = mask.shape
    rows = rows // 2
    rank = lanes // (SLICES * low)
    z = 0.0
    for block in (z0, z1, z2, z3):
        z = z + block[...].astype(F32)
    repeat = iota((2 * tok, 2 * rows), 1) // (rows // tok) == iota((2 * tok, 2 * rows), 0)
    z = dot(z.astype(BF16), repeat.astype(BF16), 0, 0)
    work[...] = (z * mask[...]).astype(BF16)
    for r in range(low):
        for j in range(SLICES):
            start = pl.multiple_of((j * low + (lower ^ r)) * rank, rank)
            spread[(r * SLICES + j) * rank : (r * SLICES + j + 1) * rank] = work[
                pl.ds(start, rank)
            ]
    for chunk in range(len(outs) // low):
        block, width = outs[chunk * low].shape
        here = slice(chunk * width, (chunk + 1) * width)
        part = dot(spread[:, :rows], mine[:, here], 1, 0)
        part = (part + dot(spread[:, rows:], other[:, here], 1, 0)).astype(BF16)
        for r in range(low):
            outs[chunk * low + r][...] = part[r * block : (r + 1) * block]


def shards(tokens, expert_ids, route_probs, cotangents, sketch):
    n_expert = lax.axis_size("expert")
    n_dp = lax.axis_size("dp")
    count = n_expert * n_dp
    line = count // SLICES
    low = line // 2
    groups = 2 // n_dp
    tok, width = tokens.shape
    top = expert_ids.shape[1]
    hidden, rank = sketch.shape
    rows = tok * top
    share = width // SLICES
    lanes = count // 2 * rank
    part = hidden // n_dp
    scale = 1.0 / math.sqrt(rows)
    _, lower, place, half = position()
    limit = LIMIT if n_dp == 1 else LARGE
    shape = jax.ShapeDtypeStruct

    def exchange(block, step):
        return lax.ppermute(block, AXES, [(i, i ^ step) for i in range(count)])

    cot = cotangents.reshape(rows, hidden)

    *blocks, pairs = call(
        functools.partial(first_kernel, groups),
        [shape((tok, groups * lanes + share), BF16)] * SLICES + [shape((2 * top, tok), F32)],
        [HBM] * 5,
        [
            pltpu.VMEM((rows, hidden), BF16),
            pltpu.VMEM((rank, hidden), F32),
            pltpu.VMEM((top, tok), jnp.int32),
            pltpu.VMEM((top, tok), F32),
            pltpu.SemaphoreType.DMA((8,)),
            pltpu.SemaphoreType.DMA((SLICES,)),
        ],
        tokens,
        cot,
        sketch.T,
        expert_ids.T,
        route_probs.T,
        limit=LARGE,
    )
    blocks = blocks[:1] + [exchange(blocks[j], j * line) for j in range(1, SLICES)]

    pairs, send = lax.optimization_barrier((pairs, cot))
    pairs = [pairs, exchange(pairs, 1)]
    mine = cot
    if n_dp > 1:
        mine = lax.dynamic_slice_in_dim(cot, half * part, part, axis=1)
        send = lax.dynamic_slice_in_dim(send, (1 - half) * part, part, axis=1)
    other = exchange(send, 1)

    near = [[jnp.concatenate(blocks[i : i + 2], axis=0)] for i in range(0, SLICES, 2)]
    step = 2
    while step < line:
        near = [side + [exchange(b, step) for b in side] for side in near]
        step *= 2
    n = len(near[0])
    skip = lanes if groups == 2 else 0

    far = [exchange(b[:, skip:], 1) for b in near[0]]
    if n_dp == 1:
        work = [
            pltpu.VMEM((4 * n * tok, share), BF16),
            pltpu.VMEM((4 * n * tok, lanes), BF16),
            pltpu.SemaphoreType.DMA((4 * n,)),
        ]
        [columns] = call(
            functools.partial(columns_kernel, n),
            [shape((lanes, share), F32)],
            [HBM] * (2 * n),
            work,
            *near[0],
            *far,
        )
        near[1], columns = lax.optimization_barrier((near[1], columns))
        zs = call(
            functools.partial(z_kernel, n, low),
            [shape((2 * tok, lanes), BF16)] * SLICES + [shape((rank, share), BF16)] * SLICES,
            [VMEM] * 3 + [HBM] * (2 * n),
            work[:2] + [pltpu.VMEM((lanes, share), BF16)] + work[2:],
            columns,
            near[0][0],
            far[0],
            *near[1],
            *[exchange(b[:, skip:], 1) for b in near[1]],
        )
    else:
        far = [far, [exchange(b[:, skip:], 1) for b in near[1]]]
        rows_all = jnp.concatenate(near[0] + far[0] + near[1] + far[1], axis=0)
        columns = dot(rows_all[:, :lanes], rows_all[:, lanes:], 0, 0).astype(BF16)
        zs, own = [], []
        for j in range(SLICES):
            here = slice(j % 2 * tok, (j % 2 + 1) * tok)
            x = jnp.concatenate([near[j // 2][0][here], far[j // 2][0][here]], axis=0)
            start = ((place ^ j) * low + lower) * rank
            own.append(lax.dynamic_slice_in_dim(columns, start, rank, axis=0))
            zs.append(dot(x[:, lanes:], columns, 1, 1).astype(BF16))
        zs = zs + own
    columns = zs[SLICES:]
    zs = list(zs[:1]) + [exchange(zs[j], j * line) for j in range(1, SLICES)]

    [mask] = call(
        functools.partial(mask_kernel, groups),
        [shape((lanes, 2 * rows), F32)],
        [VMEM] * 2,
        [],
        *pairs,
        limit=limit,
    )
    piece = part // CHUNKS
    terms = call(
        functools.partial(terms_kernel, low, tok),
        [shape((SLICES * rank, piece), BF16)] * (low * CHUNKS),
        [VMEM] * (SLICES + 3),
        [pltpu.VMEM((lanes, 2 * rows), BF16)] * 2,
        *zs,
        mask,
        mine,
        other,
        limit=limit,
    )
    columns = list(columns[:1]) + [exchange(columns[j], j * line) for j in range(1, SLICES)]
    blocks = []
    for i in range(CHUNKS):
        parts = terms[i * low : (i + 1) * low]
        parts = [term.reshape(SLICES, rank, piece) for term in parts]
        step = 2
        while len(parts) > 1:
            got = [exchange(send, step) for send in parts[1::2]]
            if i and step == 2:
                got[0], blocks[2] = lax.optimization_barrier((got[0], blocks[2]))
            parts = [
                (keep.astype(F32) + other.astype(F32)).astype(BF16)
                for keep, other in zip(parts[::2], got)
            ]
            step *= 2
        own = [lax.dynamic_index_in_dim(parts[0], place ^ j, 0, False) for j in range(SLICES)]
        blocks += own[:1] + [exchange(own[j], j * line) for j in range(1, SLICES)]
    blocks[-3], *columns = lax.optimization_barrier((blocks[-3], *columns))
    inverse, basis = call(
        inverse_kernel,
        [shape((rank, rank), F32), shape((rank, width // n_dp), F32)],
        [VMEM] * SLICES,
        [pltpu.VMEM((SLICES, rank, share), BF16)],
        *columns,
    )
    [coeffs] = call(
        functools.partial(coeffs_kernel, scale),
        [shape((rank, part), F32)],
        [VMEM] * (1 + len(blocks)),
        [],
        inverse,
        *blocks,
    )
    return basis[None], coeffs[None]


def solution(mesh):
    in_specs = (
        P(("group", "expert", "dp"), None),
        P(("group", "expert", "dp"), None),
        P(("group", "expert", "dp"), None),
        P(("group", "expert", "dp"), None, None),
        P(),
    )
    out_specs = (P(("group", "expert"), None, "dp"), P(("group", "expert"), None, "dp"))
    return jax.shard_map(shards, mesh=mesh, in_specs=in_specs, out_specs=out_specs, check_vma=False)
```

```python
import functools
import math

import jax
import jax.numpy as jnp
from jax import lax
from jax.experimental import pallas as pl
from jax.experimental.pallas import tpu as pltpu
from jax.sharding import PartitionSpec as P

AXES = ("expert", "dp")
CHUNKS = 2
SLICES = 4
LIMIT = 12 * 1024 * 1024
LARGE = 56 * 1024 * 1024
VMEM = pl.BlockSpec(memory_space=pltpu.VMEM)
HBM = pl.BlockSpec(memory_space=pltpu.HBM)
BF16 = jnp.bfloat16
F32 = jnp.float32


def dot(left, right, left_dim, right_dim):
    dims = (((left_dim,), (right_dim,)), ((), ()))
    return lax.dot_general(left, right, dims, preferred_element_type=F32)


def iota(shape, dim):
    return lax.broadcasted_iota(jnp.int32, shape, dim)


def position():
    half = lax.axis_index("dp")
    me = lax.axis_index("expert") * lax.axis_size("dp") + half
    line = lax.axis_size("expert") * lax.axis_size("dp") // SLICES
    return me % 2, me // 2 % (line // 2), me // line, half


def call(body, shapes, spaces, scratch, *args, limit=LIMIT):
    return pl.pallas_call(
        body,
        out_shape=shapes,
        in_specs=spaces,
        out_specs=[VMEM] * len(shapes),
        scratch_shapes=scratch,
        compiler_params=pltpu.CompilerParams(vmem_limit_bytes=limit),
        cost_estimate=pl.CostEstimate(flops=1, bytes_accessed=1, transcendentals=0),
    )(*args)


def pieces(value, count):
    terms = []
    for _ in range(count):
        terms.append(value.astype(BF16))
        value = value - terms[-1].astype(F32)
    return terms


def pair_columns(ids, probs):
    top, tok = ids.shape
    rows = tok * top
    pick = (iota((rows, tok), 0) // top == iota((rows, tok), 1)).astype(BF16)
    here = iota((rows, top), 0) % top == iota((rows, top), 1)
    names = dot(pick, ids.astype(BF16), 1, 1)
    weights, rest = jnp.zeros((rows, top), F32), probs
    for _ in range(3):
        piece = rest.astype(BF16)
        weights = weights + dot(pick, piece, 1, 1)
        rest = rest - piece.astype(F32)
    names = jnp.sum(jnp.where(here, names, 0.0), axis=1, keepdims=True)
    weights = jnp.sum(jnp.where(here, weights, 0.0), axis=1, keepdims=True)
    return names, weights


def load(pairs, sems):
    copies = [pltpu.make_async_copy(src, dst, sems.at[i]) for i, (src, dst) in enumerate(pairs)]
    for copy in copies:
        copy.start()
    return copies


def first_kernel(groups, tokens, cot_at, sketch_at, ids_at, probs_at, *refs):
    outs, pairs, (cot, sketch, ids, probs, sems, x_sems) = refs[:SLICES], refs[SLICES], refs[5:]
    core, _, place, _ = position()
    rows, hidden = cot.shape
    tok = pairs.shape[1]
    top = rows // tok
    rank = sketch.shape[0]
    share = tokens.shape[1] // SLICES
    lanes = (outs[0].shape[1] - share) // groups
    parts = 5
    piece = hidden // parts
    sources = [(ids_at, ids), (probs_at, probs), (sketch_at, sketch)]
    for i in range(parts):
        cut = pl.ds(i * piece, piece)
        sources.append((cot_at.at[:, cut], cot.at[:, cut]))
    copies = load(sources, sems)
    sources = []
    for j, out in enumerate(outs):
        cut = pl.ds(pl.multiple_of((place ^ j) * share, share), share)
        sources.append((tokens.at[:, cut], out.at[:, pl.ds(lanes, share)]))
    x_copies = load(sources, x_sems)
    copies[0].wait()
    copies[1].wait()
    pairs[:top] = ids[...].astype(F32)
    pairs[top:] = probs[...]
    names, weights = pair_columns(pairs[:top], pairs[top:])
    copies[2].wait()
    both = jnp.concatenate(pieces(sketch[...], 2), axis=0)
    pair = 0.0
    for i in range(parts):
        copies[3 + i].wait()
        here = slice(i * piece, (i + 1) * piece)
        pair = pair + dot(cot[:, here], both[:, here], 1, 1)
    pair = (pair[:, :rank] + pair[:, rank:]) * weights
    lane = iota((rank, lanes), 1)
    tiled = dot(pair.astype(BF16), (iota((rank, lanes), 0) == lane % rank).astype(BF16), 1, 0)
    block = iota((1, lanes), 1) // rank * groups
    pick = (iota((rows, tok), 0) // top == iota((rows, tok), 1)).astype(BF16)
    for i in range(groups):
        name = block + (core ^ i) if groups == 2 else block
        y = jnp.where(names == name.astype(F32), tiled, 0.0).astype(BF16)
        y = dot(pick, y, 0, 0).astype(BF16)
        for out in outs:
            out[:, i * (lanes + share) : i * (lanes + share) + lanes] = y
    for copy in x_copies:
        copy.wait()


def gather(near, far, x, y, sems):
    share, lanes = x.shape[1], y.shape[1]
    rows = near[0].shape[0]
    sources = []
    for i, (a, b) in enumerate(zip(near, far)):
        cut = pl.ds(2 * i * rows, rows)
        sources.append((a.at[:, pl.ds(0, lanes)], y.at[cut]))
        sources.append((a.at[:, pl.ds(lanes, share)], x.at[cut]))
        cut = pl.ds((2 * i + 1) * rows, rows)
        sources.append((b.at[:, pl.ds(0, share)], x.at[cut]))
        sources.append((b.at[:, pl.ds(share, lanes)], y.at[cut]))
    for copy in load(sources, sems):
        copy.wait()


def columns_kernel(n, *refs):
    out, x, y, sems = refs[2 * n :]
    gather(refs[:n], refs[n : 2 * n], x, y, sems)
    out[...] = dot(y[...], x[...], 0, 0)


def z_kernel(n, low, part, near_x, far_x, *refs):
    outs, (x, y, columns, sems) = refs[2 * n : -4], refs[-4:]
    _, lower, place, _ = position()
    gather(refs[:n], refs[n : 2 * n], x, y, sems)
    rank = columns.shape[0] // (SLICES * low)
    share = x.shape[1]
    lanes = y.shape[1]
    rows = near_x.shape[0]
    tok = rows // 2
    total = (part[...] + dot(y[...], x[...], 0, 0)).astype(BF16)
    columns[...] = total
    own = jnp.concatenate([near_x[:, lanes : lanes + share], far_x[:, :share]], axis=0)
    halves = [dot(own, total, 1, 1), dot(x[: 2 * rows], total, 1, 1)]
    for j in range(SLICES):
        half = halves[j // 2].astype(BF16)
        start = j % 2 * tok
        outs[j][:tok] = half[start : start + tok]
        outs[j][tok:] = half[rows + start : rows + start + tok]
        expert = (place ^ j) * low + lower
        outs[SLICES + j][...] = columns[pl.ds(pl.multiple_of(expert * rank, rank), rank)]


def inverse_kernel(c0, c1, c2, c3, inverse, basis, columns):
    _, _, place, half = position()
    rank = inverse.shape[0]
    _, _, share = columns.shape
    gram = 0.0
    for j, block in enumerate((c0, c1, c2, c3)):
        columns[place ^ j] = block[...]
        gram = gram + dot(block[...], block[...], 1, 1)
    row = iota((rank, 128), 0)
    lane = iota((rank, 128), 1)
    eye = (row + rank == lane).astype(F32)
    work = jnp.concatenate([gram, jnp.zeros((rank, 128 - rank), F32)], axis=1) + eye
    for first in range(0, rank, 4):
        heads = [work[first + i : first + i + 1] for i in range(4)]
        sides = [
            jnp.broadcast_to(work[:, first + i : first + i + 1], (rank, 128)) for i in range(4)
        ]
        taken = 0.0
        for i in range(4):
            pivot = first + i
            factor = sides[i] / sides[i][pivot : pivot + 1]
            factor = jnp.where(row > pivot, factor, 0.0)
            taken = taken + factor * heads[i]
            for k in range(i + 1, 4):
                sides[k] = sides[k] - factor * sides[k][pivot : pivot + 1]
                heads[k] = heads[k] - factor[first + k : first + k + 1] * heads[i]
        work = work - taken
    diagonal = jnp.sum(jnp.where(row == lane, work, 0.0), axis=1, keepdims=True)
    result = work[:, rank : 2 * rank] * lax.rsqrt(diagonal)
    inverse[...] = result
    scaled = result * math.sqrt(SLICES * share)
    scaled = jnp.concatenate(pieces(scaled, 3), axis=0)
    count = basis.shape[1] // share
    for i in range(count):
        out = dot(scaled, columns[half * count + i], 1, 0)
        out = out[:rank] + out[rank : 2 * rank] + out[2 * rank :]
        basis[:, i * share : (i + 1) * share] = out


def coeffs_kernel(scale, inverse, *refs):
    blocks, out = refs[:-1], refs[-1]
    rank, size = blocks[0].shape
    left = jnp.concatenate(pieces(inverse[...] * scale, 3), axis=0)
    left = jnp.concatenate([left] * SLICES, axis=1)
    for i in range(len(blocks) // SLICES):
        right = jnp.concatenate([b[...] for b in blocks[i * SLICES : (i + 1) * SLICES]], axis=0)
        part = dot(left, right, 1, 0)
        out[:, i * size : (i + 1) * size] = part[:rank] + part[rank : 2 * rank] + part[2 * rank :]


def mask_kernel(groups, own, pair, out):
    core = position()[0]
    lanes, rows = out.shape
    rows = rows // 2
    top, tok = own.shape[0] // 2, own.shape[1]
    rank = lanes // (lax.axis_size("expert") // groups)
    pick = (iota((tok, rows), 1) // top == iota((tok, rows), 0)).astype(BF16)
    here = iota((top, rows), 1) % top == iota((top, rows), 0)
    block = iota((lanes, 1), 0) // rank * groups + (core if groups == 2 else 0)
    for i, pairs in enumerate((own, pair)):
        names = dot(pairs[:top].astype(BF16), pick, 1, 0)
        weights = sum(dot(piece, pick, 1, 0) for piece in pieces(pairs[top:], 3))
        names = jnp.sum(jnp.where(here, names, 0.0), axis=0, keepdims=True)
        weights = jnp.sum(jnp.where(here, weights, 0.0), axis=0, keepdims=True)
        masked = jnp.where(names == block.astype(F32), weights, 0.0)
        out[:, i * rows : (i + 1) * rows] = masked


def terms_kernel(low, tok, z0, z1, z2, z3, mask, mine, other, *refs):
    outs, (work, spread) = refs[:-2], refs[-2:]
    lower = position()[1]
    lanes, rows = mask.shape
    rows = rows // 2
    rank = lanes // (SLICES * low)
    z = 0.0
    for block in (z0, z1, z2, z3):
        z = z + block[...].astype(F32)
    repeat = iota((2 * tok, 2 * rows), 1) // (rows // tok) == iota((2 * tok, 2 * rows), 0)
    z = dot(z.astype(BF16), repeat.astype(BF16), 0, 0)
    work[...] = (z * mask[...]).astype(BF16)
    for r in range(low):
        for j in range(SLICES):
            start = pl.multiple_of((j * low + (lower ^ r)) * rank, rank)
            spread[(r * SLICES + j) * rank : (r * SLICES + j + 1) * rank] = work[
                pl.ds(start, rank)
            ]
    for chunk in range(len(outs) // low):
        block, width = outs[chunk * low].shape
        here = slice(chunk * width, (chunk + 1) * width)
        part = dot(spread[:, :rows], mine[:, here], 1, 0)
        part = (part + dot(spread[:, rows:], other[:, here], 1, 0)).astype(BF16)
        for r in range(low):
            outs[chunk * low + r][...] = part[r * block : (r + 1) * block]


def shards(tokens, expert_ids, route_probs, cotangents, sketch):
    n_expert = lax.axis_size("expert")
    n_dp = lax.axis_size("dp")
    count = n_expert * n_dp
    line = count // SLICES
    low = line // 2
    groups = 2 // n_dp
    tok, width = tokens.shape
    top = expert_ids.shape[1]
    hidden, rank = sketch.shape
    rows = tok * top
    share = width // SLICES
    lanes = count // 2 * rank
    part = hidden // n_dp
    scale = 1.0 / math.sqrt(rows)
    _, lower, place, half = position()
    limit = LIMIT if n_dp == 1 else LARGE
    shape = jax.ShapeDtypeStruct

    def exchange(block, step):
        return lax.ppermute(block, AXES, [(i, i ^ step) for i in range(count)])

    cot = cotangents.reshape(rows, hidden)

    *blocks, pairs = call(
        functools.partial(first_kernel, groups),
        [shape((tok, groups * lanes + share), BF16)] * SLICES + [shape((2 * top, tok), F32)],
        [HBM] * 5,
        [
            pltpu.VMEM((rows, hidden), BF16),
            pltpu.VMEM((rank, hidden), F32),
            pltpu.VMEM((top, tok), jnp.int32),
            pltpu.VMEM((top, tok), F32),
            pltpu.SemaphoreType.DMA((8,)),
            pltpu.SemaphoreType.DMA((SLICES,)),
        ],
        tokens,
        cot,
        sketch.T,
        expert_ids.T,
        route_probs.T,
        limit=LARGE,
    )
    blocks = blocks[:1] + [exchange(blocks[j], j * line) for j in range(1, SLICES)]

    pairs, send = lax.optimization_barrier((pairs, cot))
    pairs = [pairs, exchange(pairs, 1)]
    mine = cot
    if n_dp > 1:
        mine = lax.dynamic_slice_in_dim(cot, half * part, part, axis=1)
        send = lax.dynamic_slice_in_dim(send, (1 - half) * part, part, axis=1)
    other = exchange(send, 1)

    near = [[jnp.concatenate(blocks[i : i + 2], axis=0)] for i in range(0, SLICES, 2)]
    step = 2
    while step < line:
        near = [side + [exchange(b, step) for b in side] for side in near]
        step *= 2
    n = len(near[0])
    skip = lanes if groups == 2 else 0

    far = [exchange(b[:, skip:], 1) for b in near[0]]
    if n_dp == 1:
        work = [
            pltpu.VMEM((4 * n * tok, share), BF16),
            pltpu.VMEM((4 * n * tok, lanes), BF16),
            pltpu.SemaphoreType.DMA((4 * n,)),
        ]
        [columns] = call(
            functools.partial(columns_kernel, n),
            [shape((lanes, share), F32)],
            [HBM] * (2 * n),
            work,
            *near[0],
            *far,
        )
        near[1], columns = lax.optimization_barrier((near[1], columns))
        zs = call(
            functools.partial(z_kernel, n, low),
            [shape((2 * tok, lanes), BF16)] * SLICES + [shape((rank, share), BF16)] * SLICES,
            [VMEM] * 3 + [HBM] * (2 * n),
            work[:2] + [pltpu.VMEM((lanes, share), BF16)] + work[2:],
            columns,
            near[0][0],
            far[0],
            *near[1],
            *[exchange(b[:, skip:], 1) for b in near[1]],
        )
    else:
        far = [far, [exchange(b[:, skip:], 1) for b in near[1]]]
        rows_all = jnp.concatenate(near[0] + far[0] + near[1] + far[1], axis=0)
        columns = dot(rows_all[:, :lanes], rows_all[:, lanes:], 0, 0).astype(BF16)
        zs, own = [], []
        for j in range(SLICES):
            here = slice(j % 2 * tok, (j % 2 + 1) * tok)
            x = jnp.concatenate([near[j // 2][0][here], far[j // 2][0][here]], axis=0)
            start = ((place ^ j) * low + lower) * rank
            own.append(lax.dynamic_slice_in_dim(columns, start, rank, axis=0))
            zs.append(dot(x[:, lanes:], columns, 1, 1).astype(BF16))
        zs = zs + own
    columns = zs[SLICES:]
    zs = list(zs[:1]) + [exchange(zs[j], j * line) for j in range(1, SLICES)]

    [mask] = call(
        functools.partial(mask_kernel, groups),
        [shape((lanes, 2 * rows), F32)],
        [VMEM] * 2,
        [],
        *pairs,
        limit=limit,
    )
    piece = part // CHUNKS
    terms = call(
        functools.partial(terms_kernel, low, tok),
        [shape((SLICES * rank, piece), BF16)] * (low * CHUNKS),
        [VMEM] * (SLICES + 3),
        [pltpu.VMEM((lanes, 2 * rows), BF16)] * 2,
        *zs,
        mask,
        mine,
        other,
        limit=limit,
    )
    columns = list(columns[:1]) + [exchange(columns[j], j * line) for j in range(1, SLICES)]
    blocks = []
    for i in range(CHUNKS):
        parts = terms[i * low : (i + 1) * low]
        parts = [term.reshape(SLICES, rank, piece) for term in parts]
        step = 2
        while len(parts) > 1:
            got = [exchange(send, step) for send in parts[1::2]]
            if step == 2:
                if i:
                    got[0], blocks[2] = lax.optimization_barrier((got[0], blocks[2]))
                else:
                    got[0], *columns = lax.optimization_barrier((got[0], *columns))
            parts = [
                (keep.astype(F32) + other.astype(F32)).astype(BF16)
                for keep, other in zip(parts[::2], got)
            ]
            step *= 2
        own = [lax.dynamic_index_in_dim(parts[0], place ^ j, 0, False) for j in range(SLICES)]
        blocks += own[:1] + [exchange(own[j], j * line) for j in range(1, SLICES)]
    blocks[-3], *columns = lax.optimization_barrier((blocks[-3], *columns))
    inverse, basis = call(
        inverse_kernel,
        [shape((rank, rank), F32), shape((rank, width // n_dp), F32)],
        [VMEM] * SLICES,
        [pltpu.VMEM((SLICES, rank, share), BF16)],
        *columns,
    )
    [coeffs] = call(
        functools.partial(coeffs_kernel, scale),
        [shape((rank, part), F32)],
        [VMEM] * (1 + len(blocks)),
        [],
        inverse,
        *blocks,
    )
    return basis[None], coeffs[None]


def solution(mesh):
    in_specs = (
        P(("group", "expert", "dp"), None),
        P(("group", "expert", "dp"), None),
        P(("group", "expert", "dp"), None),
        P(("group", "expert", "dp"), None, None),
        P(),
    )
    out_specs = (P(("group", "expert"), None, "dp"), P(("group", "expert"), None, "dp"))
    return jax.shard_map(shards, mesh=mesh, in_specs=in_specs, out_specs=out_specs, check_vma=False)
```

```python
import functools
import math

import jax
import jax.numpy as jnp
from jax import lax
from jax.experimental import pallas as pl
from jax.experimental.pallas import tpu as pltpu
from jax.sharding import PartitionSpec as P

AXES = ("expert", "dp")
CHUNKS = 2
SLICES = 4
LIMIT = 12 * 1024 * 1024
LARGE = 56 * 1024 * 1024
VMEM = pl.BlockSpec(memory_space=pltpu.VMEM)
HBM = pl.BlockSpec(memory_space=pltpu.HBM)
BF16 = jnp.bfloat16
F32 = jnp.float32


def dot(left, right, left_dim, right_dim):
    dims = (((left_dim,), (right_dim,)), ((), ()))
    return lax.dot_general(left, right, dims, preferred_element_type=F32)


def iota(shape, dim):
    return lax.broadcasted_iota(jnp.int32, shape, dim)


def position():
    half = lax.axis_index("dp")
    me = lax.axis_index("expert") * lax.axis_size("dp") + half
    line = lax.axis_size("expert") * lax.axis_size("dp") // SLICES
    return me % 2, me // 2 % (line // 2), me // line, half


def call(body, shapes, spaces, scratch, *args, limit=LIMIT):
    return pl.pallas_call(
        body,
        out_shape=shapes,
        in_specs=spaces,
        out_specs=[VMEM] * len(shapes),
        scratch_shapes=scratch,
        compiler_params=pltpu.CompilerParams(vmem_limit_bytes=limit),
        cost_estimate=pl.CostEstimate(flops=1, bytes_accessed=1, transcendentals=0),
    )(*args)


def pieces(value, count):
    terms = []
    for _ in range(count):
        terms.append(value.astype(BF16))
        value = value - terms[-1].astype(F32)
    return terms


def pair_columns(ids, probs):
    top, tok = ids.shape
    rows = tok * top
    pick = (iota((rows, tok), 0) // top == iota((rows, tok), 1)).astype(BF16)
    here = iota((rows, top), 0) % top == iota((rows, top), 1)
    names = dot(pick, ids.astype(BF16), 1, 1)
    weights, rest = jnp.zeros((rows, top), F32), probs
    for _ in range(3):
        piece = rest.astype(BF16)
        weights = weights + dot(pick, piece, 1, 1)
        rest = rest - piece.astype(F32)
    names = jnp.sum(jnp.where(here, names, 0.0), axis=1, keepdims=True)
    weights = jnp.sum(jnp.where(here, weights, 0.0), axis=1, keepdims=True)
    return names, weights


def load(pairs, sems):
    copies = [pltpu.make_async_copy(src, dst, sems.at[i]) for i, (src, dst) in enumerate(pairs)]
    for copy in copies:
        copy.start()
    return copies


def first_kernel(groups, tokens, cot_at, sketch_at, ids_at, probs_at, *refs):
    outs, pairs, (cot, sketch, ids, probs, sems, x_sems) = refs[:SLICES], refs[SLICES], refs[5:]
    core, _, place, _ = position()
    rows, hidden = cot.shape
    tok = pairs.shape[1]
    top = rows // tok
    rank = sketch.shape[0]
    share = tokens.shape[1] // SLICES
    lanes = (outs[0].shape[1] - share) // groups
    parts = 5
    piece = hidden // parts
    sources = [(ids_at, ids), (probs_at, probs), (sketch_at, sketch)]
    for i in range(parts):
        cut = pl.ds(i * piece, piece)
        sources.append((cot_at.at[:, cut], cot.at[:, cut]))
    copies = load(sources, sems)
    sources = []
    for j, out in enumerate(outs):
        cut = pl.ds(pl.multiple_of((place ^ j) * share, share), share)
        sources.append((tokens.at[:, cut], out.at[:, pl.ds(lanes, share)]))
    x_copies = load(sources, x_sems)
    copies[0].wait()
    copies[1].wait()
    pairs[:top] = ids[...].astype(F32)
    pairs[top:] = probs[...]
    names, weights = pair_columns(pairs[:top], pairs[top:])
    copies[2].wait()
    both = jnp.concatenate(pieces(sketch[...], 2), axis=0)
    pair = 0.0
    for i in range(parts):
        copies[3 + i].wait()
        here = slice(i * piece, (i + 1) * piece)
        pair = pair + dot(cot[:, here], both[:, here], 1, 1)
    pair = (pair[:, :rank] + pair[:, rank:]) * weights
    lane = iota((rank, lanes), 1)
    tiled = dot(pair.astype(BF16), (iota((rank, lanes), 0) == lane % rank).astype(BF16), 1, 0)
    block = iota((1, lanes), 1) // rank * groups
    pick = (iota((rows, tok), 0) // top == iota((rows, tok), 1)).astype(BF16)
    for i in range(groups):
        name = block + (core ^ i) if groups == 2 else block
        y = jnp.where(names == name.astype(F32), tiled, 0.0).astype(BF16)
        y = dot(pick, y, 0, 0).astype(BF16)
        for out in outs:
            out[:, i * (lanes + share) : i * (lanes + share) + lanes] = y
    for copy in x_copies:
        copy.wait()


def gather(near, far, x, y, sems):
    share, lanes = x.shape[1], y.shape[1]
    rows = near[0].shape[0]
    sources = []
    for i, (a, b) in enumerate(zip(near, far)):
        cut = pl.ds(2 * i * rows, rows)
        sources.append((a.at[:, pl.ds(0, lanes)], y.at[cut]))
        sources.append((a.at[:, pl.ds(lanes, share)], x.at[cut]))
        cut = pl.ds((2 * i + 1) * rows, rows)
        sources.append((b.at[:, pl.ds(0, share)], x.at[cut]))
        sources.append((b.at[:, pl.ds(share, lanes)], y.at[cut]))
    for copy in load(sources, sems):
        copy.wait()


def columns_kernel(n, *refs):
    out, x, y, sems = refs[2 * n :]
    gather(refs[:n], refs[n : 2 * n], x, y, sems)
    out[...] = dot(y[...], x[...], 0, 0)


def z_kernel(n, low, part, near_x, far_x, *refs):
    outs, (x, y, columns, sems) = refs[2 * n : -4], refs[-4:]
    _, lower, place, _ = position()
    gather(refs[:n], refs[n : 2 * n], x, y, sems)
    rank = columns.shape[0] // (SLICES * low)
    share = x.shape[1]
    lanes = y.shape[1]
    rows = near_x.shape[0]
    tok = rows // 2
    total = (part[...] + dot(y[...], x[...], 0, 0)).astype(BF16)
    columns[...] = total
    own = jnp.concatenate([near_x[:, lanes : lanes + share], far_x[:, :share]], axis=0)
    halves = [dot(own, total, 1, 1), dot(x[: 2 * rows], total, 1, 1)]
    for j in range(SLICES):
        half = halves[j // 2].astype(BF16)
        start = j % 2 * tok
        outs[j][:tok] = half[start : start + tok]
        outs[j][tok:] = half[rows + start : rows + start + tok]
        expert = (place ^ j) * low + lower
        outs[SLICES + j][...] = columns[pl.ds(pl.multiple_of(expert * rank, rank), rank)]


def inverse_kernel(c0, c1, c2, c3, inverse, basis, columns):
    _, _, place, half = position()
    rank = inverse.shape[0]
    _, _, share = columns.shape
    gram = 0.0
    for j, block in enumerate((c0, c1, c2, c3)):
        columns[place ^ j] = block[...]
        gram = gram + dot(block[...], block[...], 1, 1)
    row = iota((rank, 128), 0)
    lane = iota((rank, 128), 1)
    eye = (row + rank == lane).astype(F32)
    work = jnp.concatenate([gram, jnp.zeros((rank, 128 - rank), F32)], axis=1) + eye
    for first in range(0, rank, 4):
        heads = [work[first + i : first + i + 1] for i in range(4)]
        sides = [
            jnp.broadcast_to(work[:, first + i : first + i + 1], (rank, 128)) for i in range(4)
        ]
        taken = 0.0
        for i in range(4):
            pivot = first + i
            factor = sides[i] / sides[i][pivot : pivot + 1]
            factor = jnp.where(row > pivot, factor, 0.0)
            taken = taken + factor * heads[i]
            for k in range(i + 1, 4):
                sides[k] = sides[k] - factor * sides[k][pivot : pivot + 1]
                heads[k] = heads[k] - factor[first + k : first + k + 1] * heads[i]
        work = work - taken
    diagonal = jnp.sum(jnp.where(row == lane, work, 0.0), axis=1, keepdims=True)
    result = work[:, rank : 2 * rank] * lax.rsqrt(diagonal)
    inverse[...] = result
    scaled = result * math.sqrt(SLICES * share)
    scaled = jnp.concatenate(pieces(scaled, 3), axis=0)
    count = basis.shape[1] // share
    for i in range(count):
        out = dot(scaled, columns[half * count + i], 1, 0)
        out = out[:rank] + out[rank : 2 * rank] + out[2 * rank :]
        basis[:, i * share : (i + 1) * share] = out


def coeffs_kernel(scale, inverse, *refs):
    blocks, out = refs[:-1], refs[-1]
    rank, size = blocks[0].shape
    left = jnp.concatenate(pieces(inverse[...] * scale, 3), axis=0)
    left = jnp.concatenate([left] * SLICES, axis=1)
    for i in range(len(blocks) // SLICES):
        right = jnp.concatenate([b[...] for b in blocks[i * SLICES : (i + 1) * SLICES]], axis=0)
        part = dot(left, right, 1, 0)
        out[:, i * size : (i + 1) * size] = part[:rank] + part[rank : 2 * rank] + part[2 * rank :]


def mask_kernel(groups, own, pair, out):
    core = position()[0]
    lanes, rows = out.shape
    rows = rows // 2
    top, tok = own.shape[0] // 2, own.shape[1]
    rank = lanes // (lax.axis_size("expert") // groups)
    pick = (iota((tok, rows), 1) // top == iota((tok, rows), 0)).astype(BF16)
    here = iota((top, rows), 1) % top == iota((top, rows), 0)
    block = iota((lanes, 1), 0) // rank * groups + (core if groups == 2 else 0)
    for i, pairs in enumerate((own, pair)):
        names = dot(pairs[:top].astype(BF16), pick, 1, 0)
        weights = sum(dot(piece, pick, 1, 0) for piece in pieces(pairs[top:], 3))
        names = jnp.sum(jnp.where(here, names, 0.0), axis=0, keepdims=True)
        weights = jnp.sum(jnp.where(here, weights, 0.0), axis=0, keepdims=True)
        masked = jnp.where(names == block.astype(F32), weights, 0.0)
        out[:, i * rows : (i + 1) * rows] = masked


def terms_kernel(low, tok, z0, z1, z2, z3, mask, mine, other, *refs):
    outs, (work, spread) = refs[:-2], refs[-2:]
    lower = position()[1]
    lanes, rows = mask.shape
    rows = rows // 2
    rank = lanes // (SLICES * low)
    z = 0.0
    for block in (z0, z1, z2, z3):
        z = z + block[...].astype(F32)
    repeat = iota((2 * tok, 2 * rows), 1) // (rows // tok) == iota((2 * tok, 2 * rows), 0)
    z = dot(z.astype(BF16), repeat.astype(BF16), 0, 0)
    work[...] = (z * mask[...]).astype(BF16)
    for r in range(low):
        for j in range(SLICES):
            start = pl.multiple_of((j * low + (lower ^ r)) * rank, rank)
            spread[(r * SLICES + j) * rank : (r * SLICES + j + 1) * rank] = work[
                pl.ds(start, rank)
            ]
    for chunk in range(len(outs) // low):
        block, width = outs[chunk * low].shape
        here = slice(chunk * width, (chunk + 1) * width)
        part = dot(spread[:, :rows], mine[:, here], 1, 0)
        part = (part + dot(spread[:, rows:], other[:, here], 1, 0)).astype(BF16)
        for r in range(low):
            outs[chunk * low + r][...] = part[r * block : (r + 1) * block]


def shards(tokens, expert_ids, route_probs, cotangents, sketch):
    n_expert = lax.axis_size("expert")
    n_dp = lax.axis_size("dp")
    count = n_expert * n_dp
    line = count // SLICES
    low = line // 2
    groups = 2 // n_dp
    tok, width = tokens.shape
    top = expert_ids.shape[1]
    hidden, rank = sketch.shape
    rows = tok * top
    share = width // SLICES
    lanes = count // 2 * rank
    part = hidden // n_dp
    scale = 1.0 / math.sqrt(rows)
    _, lower, place, half = position()
    limit = LIMIT if n_dp == 1 else LARGE
    shape = jax.ShapeDtypeStruct

    def exchange(block, step):
        return lax.ppermute(block, AXES, [(i, i ^ step) for i in range(count)])

    cot = cotangents.reshape(rows, hidden)

    *blocks, pairs = call(
        functools.partial(first_kernel, groups),
        [shape((tok, groups * lanes + share), BF16)] * SLICES + [shape((2 * top, tok), F32)],
        [HBM] * 5,
        [
            pltpu.VMEM((rows, hidden), BF16),
            pltpu.VMEM((rank, hidden), F32),
            pltpu.VMEM((top, tok), jnp.int32),
            pltpu.VMEM((top, tok), F32),
            pltpu.SemaphoreType.DMA((8,)),
            pltpu.SemaphoreType.DMA((SLICES,)),
        ],
        tokens,
        cot,
        sketch.T,
        expert_ids.T,
        route_probs.T,
        limit=LARGE,
    )
    blocks = blocks[:1] + [exchange(blocks[j], j * line) for j in range(1, SLICES)]

    pairs, send = lax.optimization_barrier((pairs, cot))
    pairs = [pairs, exchange(pairs, 1)]
    mine = cot
    if n_dp > 1:
        mine = lax.dynamic_slice_in_dim(cot, half * part, part, axis=1)
        send = lax.dynamic_slice_in_dim(send, (1 - half) * part, part, axis=1)
    other = exchange(send, 1)

    near = [[jnp.concatenate(blocks[i : i + 2], axis=0)] for i in range(0, SLICES, 2)]
    step = 2
    while step < line:
        near = [side + [exchange(b, step) for b in side] for side in near]
        step *= 2
    n = len(near[0])
    skip = lanes if groups == 2 else 0

    far = [exchange(b[:, skip:], 1) for b in near[0]]
    if n_dp == 1:
        work = [
            pltpu.VMEM((4 * n * tok, share), BF16),
            pltpu.VMEM((4 * n * tok, lanes), BF16),
            pltpu.SemaphoreType.DMA((4 * n,)),
        ]
        [columns] = call(
            functools.partial(columns_kernel, n),
            [shape((lanes, share), F32)],
            [HBM] * (2 * n),
            work,
            *near[0],
            *far,
        )
        near[1], columns = lax.optimization_barrier((near[1], columns))
        zs = call(
            functools.partial(z_kernel, n, low),
            [shape((2 * tok, lanes), BF16)] * SLICES + [shape((rank, share), BF16)] * SLICES,
            [VMEM] * 3 + [HBM] * (2 * n),
            work[:2] + [pltpu.VMEM((lanes, share), BF16)] + work[2:],
            columns,
            near[0][0],
            far[0],
            *near[1],
            *[exchange(b[:, skip:], 1) for b in near[1]],
        )
    else:
        far = [far, [exchange(b[:, skip:], 1) for b in near[1]]]
        rows_all = jnp.concatenate(near[0] + far[0] + near[1] + far[1], axis=0)
        columns = dot(rows_all[:, :lanes], rows_all[:, lanes:], 0, 0).astype(BF16)
        zs, own = [], []
        for j in range(SLICES):
            here = slice(j % 2 * tok, (j % 2 + 1) * tok)
            x = jnp.concatenate([near[j // 2][0][here], far[j // 2][0][here]], axis=0)
            start = ((place ^ j) * low + lower) * rank
            own.append(lax.dynamic_slice_in_dim(columns, start, rank, axis=0))
            zs.append(dot(x[:, lanes:], columns, 1, 1).astype(BF16))
        zs = zs + own
    columns = zs[SLICES:]
    zs = list(zs[:1]) + [exchange(zs[j], j * line) for j in range(1, SLICES)]

    [mask] = call(
        functools.partial(mask_kernel, groups),
        [shape((lanes, 2 * rows), F32)],
        [VMEM] * 2,
        [],
        *pairs,
        limit=limit,
    )
    piece = part // CHUNKS
    terms = call(
        functools.partial(terms_kernel, low, tok),
        [shape((SLICES * rank, piece), BF16)] * (low * CHUNKS),
        [VMEM] * (SLICES + 3),
        [pltpu.VMEM((lanes, 2 * rows), BF16)] * 2,
        *zs,
        mask,
        mine,
        other,
        limit=limit,
    )
    columns = list(columns[:1]) + [exchange(columns[j], j * line) for j in range(1, SLICES)]
    blocks = []
    for i in range(CHUNKS):
        parts = terms[i * low : (i + 1) * low]
        parts = [term.reshape(SLICES, rank, piece) for term in parts]
        step = 2
        while len(parts) > 1:
            got = [exchange(send, step) for send in parts[1::2]]
            if i == 0 and step == 2:
                got[0], *columns = lax.optimization_barrier((got[0], *columns))
            parts = [
                (keep.astype(F32) + other.astype(F32)).astype(BF16)
                for keep, other in zip(parts[::2], got)
            ]
            step *= 2
        own = [lax.dynamic_index_in_dim(parts[0], place ^ j, 0, False) for j in range(SLICES)]
        blocks += own[:1] + [exchange(own[j], j * line) for j in range(1, SLICES)]
    blocks[-3], *columns = lax.optimization_barrier((blocks[-3], *columns))
    inverse, basis = call(
        inverse_kernel,
        [shape((rank, rank), F32), shape((rank, width // n_dp), F32)],
        [VMEM] * SLICES,
        [pltpu.VMEM((SLICES, rank, share), BF16)],
        *columns,
    )
    [coeffs] = call(
        functools.partial(coeffs_kernel, scale),
        [shape((rank, part), F32)],
        [VMEM] * (1 + len(blocks)),
        [],
        inverse,
        *blocks,
    )
    return basis[None], coeffs[None]


def solution(mesh):
    in_specs = (
        P(("group", "expert", "dp"), None),
        P(("group", "expert", "dp"), None),
        P(("group", "expert", "dp"), None),
        P(("group", "expert", "dp"), None, None),
        P(),
    )
    out_specs = (P(("group", "expert"), None, "dp"), P(("group", "expert"), None, "dp"))
    return jax.shard_map(shards, mesh=mesh, in_specs=in_specs, out_specs=out_specs, check_vma=False)
```

```python
import functools
import math

import jax
import jax.numpy as jnp
from jax import lax
from jax.experimental import pallas as pl
from jax.experimental.pallas import tpu as pltpu
from jax.sharding import PartitionSpec as P

AXES = ("expert", "dp")
CHUNKS = 2
SLICES = 4
LIMIT = 12 * 1024 * 1024
LARGE = 56 * 1024 * 1024
VMEM = pl.BlockSpec(memory_space=pltpu.VMEM)
HBM = pl.BlockSpec(memory_space=pltpu.HBM)
BF16 = jnp.bfloat16
F32 = jnp.float32


def dot(left, right, left_dim, right_dim):
    dims = (((left_dim,), (right_dim,)), ((), ()))
    return lax.dot_general(left, right, dims, preferred_element_type=F32)


def add(left, right):
    return (left.astype(F32) + right.astype(F32)).astype(BF16)


def iota(shape, dim):
    return lax.broadcasted_iota(jnp.int32, shape, dim)


def position():
    half = lax.axis_index("dp")
    me = lax.axis_index("expert") * lax.axis_size("dp") + half
    line = lax.axis_size("expert") * lax.axis_size("dp") // SLICES
    return me % 2, me // 2 % (line // 2), me // line, half


def call(body, shapes, spaces, scratch, *args, limit=LIMIT):
    return pl.pallas_call(
        body,
        out_shape=shapes,
        in_specs=spaces,
        out_specs=[VMEM] * len(shapes),
        scratch_shapes=scratch,
        compiler_params=pltpu.CompilerParams(vmem_limit_bytes=limit),
        cost_estimate=pl.CostEstimate(flops=1, bytes_accessed=1, transcendentals=0),
    )(*args)


def pieces(value, count):
    terms = []
    for _ in range(count):
        terms.append(value.astype(BF16))
        value = value - terms[-1].astype(F32)
    return terms


def pair_columns(ids, probs):
    top, tok = ids.shape
    rows = tok * top
    pick = (iota((rows, tok), 0) // top == iota((rows, tok), 1)).astype(BF16)
    here = iota((rows, top), 0) % top == iota((rows, top), 1)
    names = dot(pick, ids.astype(BF16), 1, 1)
    weights, rest = jnp.zeros((rows, top), F32), probs
    for _ in range(3):
        piece = rest.astype(BF16)
        weights = weights + dot(pick, piece, 1, 1)
        rest = rest - piece.astype(F32)
    names = jnp.sum(jnp.where(here, names, 0.0), axis=1, keepdims=True)
    weights = jnp.sum(jnp.where(here, weights, 0.0), axis=1, keepdims=True)
    return names, weights


def load(pairs, sems):
    copies = [pltpu.make_async_copy(src, dst, sems.at[i]) for i, (src, dst) in enumerate(pairs)]
    for copy in copies:
        copy.start()
    return copies


def first_kernel(groups, tokens, cot_at, sketch_at, ids_at, probs_at, *refs):
    outs, pairs, (cot, sketch, ids, probs, sems, x_sems) = refs[:SLICES], refs[SLICES], refs[5:]
    core, _, place, _ = position()
    rows, hidden = cot.shape
    tok = pairs.shape[1]
    top = rows // tok
    rank = sketch.shape[0]
    share = tokens.shape[1] // SLICES
    lanes = (outs[0].shape[1] - share) // groups
    parts = 5
    piece = hidden // parts
    sources = [(ids_at, ids), (probs_at, probs), (sketch_at, sketch)]
    for i in range(parts):
        cut = pl.ds(i * piece, piece)
        sources.append((cot_at.at[:, cut], cot.at[:, cut]))
    copies = load(sources, sems)
    sources = []
    for j, out in enumerate(outs):
        cut = pl.ds(pl.multiple_of((place ^ j) * share, share), share)
        sources.append((tokens.at[:, cut], out.at[:, pl.ds(lanes, share)]))
    x_copies = load(sources, x_sems)
    copies[0].wait()
    copies[1].wait()
    pairs[:top] = ids[...].astype(F32)
    pairs[top:] = probs[...]
    names, weights = pair_columns(pairs[:top], pairs[top:])
    copies[2].wait()
    both = jnp.concatenate(pieces(sketch[...], 2), axis=0)
    pair = 0.0
    for i in range(parts):
        copies[3 + i].wait()
        here = slice(i * piece, (i + 1) * piece)
        pair = pair + dot(cot[:, here], both[:, here], 1, 1)
    pair = (pair[:, :rank] + pair[:, rank:]) * weights
    lane = iota((rank, lanes), 1)
    tiled = dot(pair.astype(BF16), (iota((rank, lanes), 0) == lane % rank).astype(BF16), 1, 0)
    block = iota((1, lanes), 1) // rank * groups
    pick = (iota((rows, tok), 0) // top == iota((rows, tok), 1)).astype(BF16)
    for i in range(groups):
        name = block + (core ^ i) if groups == 2 else block
        y = jnp.where(names == name.astype(F32), tiled, 0.0).astype(BF16)
        y = dot(pick, y, 0, 0).astype(BF16)
        for out in outs:
            out[:, i * (lanes + share) : i * (lanes + share) + lanes] = y
    for copy in x_copies:
        copy.wait()


def gather(near, far, x, y, sems):
    share, lanes = x.shape[1], y.shape[1]
    rows = near[0].shape[0]
    sources = []
    for i, (a, b) in enumerate(zip(near, far)):
        cut = pl.ds(2 * i * rows, rows)
        sources.append((a.at[:, pl.ds(0, lanes)], y.at[cut]))
        sources.append((a.at[:, pl.ds(lanes, share)], x.at[cut]))
        cut = pl.ds((2 * i + 1) * rows, rows)
        sources.append((b.at[:, pl.ds(0, share)], x.at[cut]))
        sources.append((b.at[:, pl.ds(share, lanes)], y.at[cut]))
    for copy in load(sources, sems):
        copy.wait()


def columns_kernel(n, *refs):
    out, x, y, sems = refs[2 * n :]
    gather(refs[:n], refs[n : 2 * n], x, y, sems)
    out[...] = dot(y[...], x[...], 0, 0)


def z_kernel(n, low, part, near_x, far_x, *refs):
    outs, (x, y, columns, sems) = refs[2 * n : -4], refs[-4:]
    _, lower, place, _ = position()
    gather(refs[:n], refs[n : 2 * n], x, y, sems)
    rank = columns.shape[0] // (SLICES * low)
    share = x.shape[1]
    lanes = y.shape[1]
    rows = near_x.shape[0]
    tok = rows // 2
    total = (part[...] + dot(y[...], x[...], 0, 0)).astype(BF16)
    columns[...] = total
    own = jnp.concatenate([near_x[:, lanes : lanes + share], far_x[:, :share]], axis=0)
    halves = [dot(own, total, 1, 1), dot(x[: 2 * rows], total, 1, 1)]
    for j in range(SLICES):
        half = halves[j // 2].astype(BF16)
        start = j % 2 * tok
        outs[j][:tok] = half[start : start + tok]
        outs[j][tok:] = half[rows + start : rows + start + tok]
        expert = (place ^ j) * low + lower
        outs[SLICES + j][...] = columns[pl.ds(pl.multiple_of(expert * rank, rank), rank)]


def inverse_kernel(c0, c1, c2, c3, inverse, basis, columns):
    _, _, place, half = position()
    rank = inverse.shape[0]
    _, _, share = columns.shape
    gram = 0.0
    for j, block in enumerate((c0, c1, c2, c3)):
        columns[place ^ j] = block[...]
        gram = gram + dot(block[...], block[...], 1, 1)
    row = iota((rank, 128), 0)
    lane = iota((rank, 128), 1)
    eye = (row + rank == lane).astype(F32)
    work = jnp.concatenate([gram, jnp.zeros((rank, 128 - rank), F32)], axis=1) + eye
    for first in range(0, rank, 4):
        heads = [work[first + i : first + i + 1] for i in range(4)]
        sides = [
            jnp.broadcast_to(work[:, first + i : first + i + 1], (rank, 128)) for i in range(4)
        ]
        taken = 0.0
        for i in range(4):
            pivot = first + i
            factor = sides[i] / sides[i][pivot : pivot + 1]
            factor = jnp.where(row > pivot, factor, 0.0)
            taken = taken + factor * heads[i]
            for k in range(i + 1, 4):
                sides[k] = sides[k] - factor * sides[k][pivot : pivot + 1]
                heads[k] = heads[k] - factor[first + k : first + k + 1] * heads[i]
        work = work - taken
    diagonal = jnp.sum(jnp.where(row == lane, work, 0.0), axis=1, keepdims=True)
    result = work[:, rank : 2 * rank] * lax.rsqrt(diagonal)
    inverse[...] = result
    scaled = result * math.sqrt(SLICES * share)
    scaled = jnp.concatenate(pieces(scaled, 3), axis=0)
    count = basis.shape[1] // share
    for i in range(count):
        out = dot(scaled, columns[half * count + i], 1, 0)
        out = out[:rank] + out[rank : 2 * rank] + out[2 * rank :]
        basis[:, i * share : (i + 1) * share] = out


def coeffs_kernel(scale, inverse, *refs):
    blocks, out = refs[:-1], refs[-1]
    rank, size = blocks[0].shape
    left = jnp.concatenate(pieces(inverse[...] * scale, 3), axis=0)
    left = jnp.concatenate([left] * 2, axis=1)
    for i in range(len(blocks) // 2):
        right = jnp.concatenate([b[...] for b in blocks[2 * i : 2 * i + 2]], axis=0)
        part = dot(left, right, 1, 0)
        out[:, i * size : (i + 1) * size] = part[:rank] + part[rank : 2 * rank] + part[2 * rank :]


def mask_kernel(groups, own, pair, out):
    core = position()[0]
    lanes, rows = out.shape
    rows = rows // 2
    top, tok = own.shape[0] // 2, own.shape[1]
    rank = lanes // (lax.axis_size("expert") // groups)
    pick = (iota((tok, rows), 1) // top == iota((tok, rows), 0)).astype(BF16)
    here = iota((top, rows), 1) % top == iota((top, rows), 0)
    block = iota((lanes, 1), 0) // rank * groups + (core if groups == 2 else 0)
    for i, pairs in enumerate((own, pair)):
        names = dot(pairs[:top].astype(BF16), pick, 1, 0)
        weights = sum(dot(piece, pick, 1, 0) for piece in pieces(pairs[top:], 3))
        names = jnp.sum(jnp.where(here, names, 0.0), axis=0, keepdims=True)
        weights = jnp.sum(jnp.where(here, weights, 0.0), axis=0, keepdims=True)
        masked = jnp.where(names == block.astype(F32), weights, 0.0)
        out[:, i * rows : (i + 1) * rows] = masked


def terms_kernel(low, tok, z0, z1, z2, z3, mask, mine, other, *refs):
    outs, (work, spread) = refs[:-2], refs[-2:]
    lower = position()[1]
    lanes, rows = mask.shape
    rows = rows // 2
    rank = lanes // (SLICES * low)
    z = 0.0
    for block in (z0, z1, z2, z3):
        z = z + block[...].astype(F32)
    repeat = iota((2 * tok, 2 * rows), 1) // (rows // tok) == iota((2 * tok, 2 * rows), 0)
    z = dot(z.astype(BF16), repeat.astype(BF16), 0, 0)
    work[...] = (z * mask[...]).astype(BF16)
    for r in range(low):
        for j in range(SLICES):
            start = pl.multiple_of((j * low + (lower ^ r)) * rank, rank)
            spread[(r * SLICES + j) * rank : (r * SLICES + j + 1) * rank] = work[
                pl.ds(start, rank)
            ]
    for chunk in range(len(outs) // low):
        block, width = outs[chunk * low].shape
        here = slice(chunk * width, (chunk + 1) * width)
        part = dot(spread[:, :rows], mine[:, here], 1, 0)
        part = (part + dot(spread[:, rows:], other[:, here], 1, 0)).astype(BF16)
        for r in range(low):
            outs[chunk * low + r][...] = part[r * block : (r + 1) * block]


def shards(tokens, expert_ids, route_probs, cotangents, sketch):
    n_expert = lax.axis_size("expert")
    n_dp = lax.axis_size("dp")
    count = n_expert * n_dp
    line = count // SLICES
    low = line // 2
    groups = 2 // n_dp
    tok, width = tokens.shape
    top = expert_ids.shape[1]
    hidden, rank = sketch.shape
    rows = tok * top
    share = width // SLICES
    lanes = count // 2 * rank
    part = hidden // n_dp
    scale = 1.0 / math.sqrt(rows)
    _, lower, place, half = position()
    limit = LIMIT if n_dp == 1 else LARGE
    shape = jax.ShapeDtypeStruct

    def exchange(block, step):
        return lax.ppermute(block, AXES, [(i, i ^ step) for i in range(count)])

    cot = cotangents.reshape(rows, hidden)

    *blocks, pairs = call(
        functools.partial(first_kernel, groups),
        [shape((tok, groups * lanes + share), BF16)] * SLICES + [shape((2 * top, tok), F32)],
        [HBM] * 5,
        [
            pltpu.VMEM((rows, hidden), BF16),
            pltpu.VMEM((rank, hidden), F32),
            pltpu.VMEM((top, tok), jnp.int32),
            pltpu.VMEM((top, tok), F32),
            pltpu.SemaphoreType.DMA((8,)),
            pltpu.SemaphoreType.DMA((SLICES,)),
        ],
        tokens,
        cot,
        sketch.T,
        expert_ids.T,
        route_probs.T,
        limit=LARGE,
    )
    blocks = blocks[:1] + [exchange(blocks[j], j * line) for j in range(1, SLICES)]

    pairs, send = lax.optimization_barrier((pairs, cot))
    pairs = [pairs, exchange(pairs, 1)]
    mine = cot
    if n_dp > 1:
        mine = lax.dynamic_slice_in_dim(cot, half * part, part, axis=1)
        send = lax.dynamic_slice_in_dim(send, (1 - half) * part, part, axis=1)
    other = exchange(send, 1)

    near = [[jnp.concatenate(blocks[i : i + 2], axis=0)] for i in range(0, SLICES, 2)]
    step = 2
    while step < line:
        near = [side + [exchange(b, step) for b in side] for side in near]
        step *= 2
    n = len(near[0])
    skip = lanes if groups == 2 else 0

    far = [exchange(b[:, skip:], 1) for b in near[0]]
    if n_dp == 1:
        work = [
            pltpu.VMEM((4 * n * tok, share), BF16),
            pltpu.VMEM((4 * n * tok, lanes), BF16),
            pltpu.SemaphoreType.DMA((4 * n,)),
        ]
        [columns] = call(
            functools.partial(columns_kernel, n),
            [shape((lanes, share), F32)],
            [HBM] * (2 * n),
            work,
            *near[0],
            *far,
        )
        near[1], columns = lax.optimization_barrier((near[1], columns))
        zs = call(
            functools.partial(z_kernel, n, low),
            [shape((2 * tok, lanes), BF16)] * SLICES + [shape((rank, share), BF16)] * SLICES,
            [VMEM] * 3 + [HBM] * (2 * n),
            work[:2] + [pltpu.VMEM((lanes, share), BF16)] + work[2:],
            columns,
            near[0][0],
            far[0],
            *near[1],
            *[exchange(b[:, skip:], 1) for b in near[1]],
        )
    else:
        far = [far, [exchange(b[:, skip:], 1) for b in near[1]]]
        rows_all = jnp.concatenate(near[0] + far[0] + near[1] + far[1], axis=0)
        columns = dot(rows_all[:, :lanes], rows_all[:, lanes:], 0, 0).astype(BF16)
        zs, own = [], []
        for j in range(SLICES):
            here = slice(j % 2 * tok, (j % 2 + 1) * tok)
            x = jnp.concatenate([near[j // 2][0][here], far[j // 2][0][here]], axis=0)
            start = ((place ^ j) * low + lower) * rank
            own.append(lax.dynamic_slice_in_dim(columns, start, rank, axis=0))
            zs.append(dot(x[:, lanes:], columns, 1, 1).astype(BF16))
        zs = zs + own
    columns = zs[SLICES:]
    zs = list(zs[:1]) + [exchange(zs[j], j * line) for j in range(1, SLICES)]

    [mask] = call(
        functools.partial(mask_kernel, groups),
        [shape((lanes, 2 * rows), F32)],
        [VMEM] * 2,
        [],
        *pairs,
        limit=limit,
    )
    piece = part // CHUNKS
    terms = call(
        functools.partial(terms_kernel, low, tok),
        [shape((SLICES * rank, piece), BF16)] * (low * CHUNKS),
        [VMEM] * (SLICES + 3),
        [pltpu.VMEM((lanes, 2 * rows), BF16)] * 2,
        *zs,
        mask,
        mine,
        other,
        limit=limit,
    )
    columns = list(columns[:1]) + [exchange(columns[j], j * line) for j in range(1, SLICES)]
    kept, gone = [], []
    for i in range(CHUNKS):
        parts = terms[i * low : (i + 1) * low]
        parts = [term.reshape(SLICES, rank, piece) for term in parts]
        step = 2
        while len(parts) > 1:
            got = [exchange(send, step) for send in parts[1::2]]
            if step == 2 and i == 0:
                got[0], *columns = lax.optimization_barrier((got[0], *columns))
                inverse, basis = call(
                    inverse_kernel,
                    [shape((rank, rank), F32), shape((rank, width // n_dp), F32)],
                    [VMEM] * SLICES,
                    [pltpu.VMEM((SLICES, rank, share), BF16)],
                    *columns,
                )
            if step == 2 and i == 1:
                got[0], gone[0], inverse = lax.optimization_barrier((got[0], gone[0], inverse))
            parts = [add(keep, other) for keep, other in zip(parts[::2], got)]
            step *= 2
        own = [lax.dynamic_index_in_dim(parts[0], place ^ j, 0, False) for j in range(SLICES)]
        kept.append(jnp.stack(own[::2]))
        gone.append(exchange(jnp.stack(own[1::2]), line))
    blocks = []
    for keep, other in zip(kept, gone):
        both = add(keep, other)
        blocks += [both[0], exchange(both[1], 2 * line)]
    [coeffs] = call(
        functools.partial(coeffs_kernel, scale),
        [shape((rank, part), F32)],
        [VMEM] * (1 + len(blocks)),
        [],
        inverse,
        *blocks,
    )
    return basis[None], coeffs[None]


def solution(mesh):
    in_specs = (
        P(("group", "expert", "dp"), None),
        P(("group", "expert", "dp"), None),
        P(("group", "expert", "dp"), None),
        P(("group", "expert", "dp"), None, None),
        P(),
    )
    out_specs = (P(("group", "expert"), None, "dp"), P(("group", "expert"), None, "dp"))
    return jax.shard_map(shards, mesh=mesh, in_specs=in_specs, out_specs=out_specs, check_vma=False)
```

```python
import functools
import math

import jax
import jax.numpy as jnp
from jax import lax
from jax.experimental import pallas as pl
from jax.experimental.pallas import tpu as pltpu
from jax.sharding import PartitionSpec as P

AXES = ("expert", "dp")
CHUNKS = 2
SLICES = 4
LIMIT = 12 * 1024 * 1024
LARGE = 56 * 1024 * 1024
VMEM = pl.BlockSpec(memory_space=pltpu.VMEM)
HBM = pl.BlockSpec(memory_space=pltpu.HBM)
BF16 = jnp.bfloat16
F32 = jnp.float32


def dot(left, right, left_dim, right_dim):
    dims = (((left_dim,), (right_dim,)), ((), ()))
    return lax.dot_general(left, right, dims, preferred_element_type=F32)


def add(left, right):
    return (left.astype(F32) + right.astype(F32)).astype(BF16)


def iota(shape, dim):
    return lax.broadcasted_iota(jnp.int32, shape, dim)


def position():
    half = lax.axis_index("dp")
    me = lax.axis_index("expert") * lax.axis_size("dp") + half
    line = lax.axis_size("expert") * lax.axis_size("dp") // SLICES
    return me % 2, me // 2 % (line // 2), me // line, half


def call(body, shapes, spaces, scratch, *args, limit=LIMIT):
    return pl.pallas_call(
        body,
        out_shape=shapes,
        in_specs=spaces,
        out_specs=[VMEM] * len(shapes),
        scratch_shapes=scratch,
        compiler_params=pltpu.CompilerParams(vmem_limit_bytes=limit),
        cost_estimate=pl.CostEstimate(flops=1, bytes_accessed=1, transcendentals=0),
    )(*args)


def pieces(value, count):
    terms = []
    for _ in range(count):
        terms.append(value.astype(BF16))
        value = value - terms[-1].astype(F32)
    return terms


def pair_columns(ids, probs):
    top, tok = ids.shape
    rows = tok * top
    pick = (iota((rows, tok), 0) // top == iota((rows, tok), 1)).astype(BF16)
    here = iota((rows, top), 0) % top == iota((rows, top), 1)
    names = dot(pick, ids.astype(BF16), 1, 1)
    weights, rest = jnp.zeros((rows, top), F32), probs
    for _ in range(3):
        piece = rest.astype(BF16)
        weights = weights + dot(pick, piece, 1, 1)
        rest = rest - piece.astype(F32)
    names = jnp.sum(jnp.where(here, names, 0.0), axis=1, keepdims=True)
    weights = jnp.sum(jnp.where(here, weights, 0.0), axis=1, keepdims=True)
    return names, weights


def load(pairs, sems):
    copies = [pltpu.make_async_copy(src, dst, sems.at[i]) for i, (src, dst) in enumerate(pairs)]
    for copy in copies:
        copy.start()
    return copies


def first_kernel(groups, cot_at, sketch_at, ids_at, probs_at, *refs):
    out, pairs, (cot, sketch, ids, probs, sems) = refs[0], refs[1], refs[2:]
    core = position()[0]
    rows, hidden = cot.shape
    tok = pairs.shape[1]
    top = rows // tok
    rank = sketch.shape[0]
    lanes = out.shape[1] // groups
    parts = 5
    piece = hidden // parts
    sources = [(ids_at, ids), (probs_at, probs), (sketch_at, sketch)]
    for i in range(parts):
        cut = pl.ds(i * piece, piece)
        sources.append((cot_at.at[:, cut], cot.at[:, cut]))
    copies = load(sources, sems)
    copies[0].wait()
    copies[1].wait()
    pairs[:top] = ids[...].astype(F32)
    pairs[top:] = probs[...]
    names, weights = pair_columns(pairs[:top], pairs[top:])
    copies[2].wait()
    both = jnp.concatenate(pieces(sketch[...], 2), axis=0)
    pair = 0.0
    for i in range(parts):
        copies[3 + i].wait()
        here = slice(i * piece, (i + 1) * piece)
        pair = pair + dot(cot[:, here], both[:, here], 1, 1)
    pair = (pair[:, :rank] + pair[:, rank:]) * weights
    lane = iota((rank, lanes), 1)
    tiled = dot(pair.astype(BF16), (iota((rank, lanes), 0) == lane % rank).astype(BF16), 1, 0)
    block = iota((1, lanes), 1) // rank * groups
    pick = (iota((rows, tok), 0) // top == iota((rows, tok), 1)).astype(BF16)
    for i in range(groups):
        name = block + (core ^ i) if groups == 2 else block
        y = jnp.where(names == name.astype(F32), tiled, 0.0).astype(BF16)
        out[:, i * lanes : (i + 1) * lanes] = dot(pick, y, 0, 0).astype(BF16)


def product(refs, x, y, sems):
    lanes = y.shape[1]
    sources = []
    for i in range(4):
        rows = x.shape[0] // 4
        sources.append((refs[i], x.at[pl.ds(i * rows, rows)]))
    for i in range(2):
        rows = y.shape[0] // 2
        sources.append((refs[4 + i].at[:, pl.ds(0, lanes)], y.at[pl.ds(i * rows, rows)]))
    for copy in load(sources, sems):
        copy.wait()
    return dot(y[...], x[...], 0, 0)


def columns_kernel(*refs):
    refs[6][...] = product(refs[:6], *refs[7:])


def z_kernel(low, *refs):
    part, own, outs, columns = refs[0], refs[1:5], refs[11:-4], refs[-4]
    _, lower, place, _ = position()
    total = (part[...] + product(refs[5:11], *refs[-3:])).astype(BF16)
    columns[...] = total
    rank = columns.shape[0] // (SLICES * low)
    rows = own[0].shape[0]
    tok = rows // 2
    z = dot(jnp.concatenate([x[...] for x in own], axis=0), total, 1, 1).astype(BF16)
    for j in range(SLICES):
        for core in range(2):
            start = 2 * core * rows + j * tok
            outs[j][core * tok : (core + 1) * tok] = z[start : start + tok]
        expert = (place ^ j) * low + lower
        outs[SLICES + j][...] = columns[pl.ds(pl.multiple_of(expert * rank, rank), rank)]


def inverse_kernel(c0, c1, c2, c3, inverse, basis, columns):
    _, _, place, half = position()
    rank = inverse.shape[0]
    _, _, share = columns.shape
    gram = 0.0
    for j, block in enumerate((c0, c1, c2, c3)):
        columns[place ^ j] = block[...]
        gram = gram + dot(block[...], block[...], 1, 1)
    row = iota((rank, 128), 0)
    lane = iota((rank, 128), 1)
    eye = (row + rank == lane).astype(F32)
    work = jnp.concatenate([gram, jnp.zeros((rank, 128 - rank), F32)], axis=1) + eye
    for first in range(0, rank, 4):
        heads = [work[first + i : first + i + 1] for i in range(4)]
        sides = [
            jnp.broadcast_to(work[:, first + i : first + i + 1], (rank, 128)) for i in range(4)
        ]
        taken = 0.0
        for i in range(4):
            pivot = first + i
            factor = sides[i] / sides[i][pivot : pivot + 1]
            factor = jnp.where(row > pivot, factor, 0.0)
            taken = taken + factor * heads[i]
            for k in range(i + 1, 4):
                sides[k] = sides[k] - factor * sides[k][pivot : pivot + 1]
                heads[k] = heads[k] - factor[first + k : first + k + 1] * heads[i]
        work = work - taken
    diagonal = jnp.sum(jnp.where(row == lane, work, 0.0), axis=1, keepdims=True)
    result = work[:, rank : 2 * rank] * lax.rsqrt(diagonal)
    inverse[...] = result
    scaled = result * math.sqrt(SLICES * share)
    scaled = jnp.concatenate(pieces(scaled, 3), axis=0)
    count = basis.shape[1] // share
    for i in range(count):
        out = dot(scaled, columns[half * count + i], 1, 0)
        out = out[:rank] + out[rank : 2 * rank] + out[2 * rank :]
        basis[:, i * share : (i + 1) * share] = out


def coeffs_kernel(scale, inverse, *refs):
    blocks, out = refs[:-1], refs[-1]
    rank, size = blocks[0].shape
    left = jnp.concatenate(pieces(inverse[...] * scale, 3), axis=0)
    left = jnp.concatenate([left] * 2, axis=1)
    for i in range(len(blocks) // 2):
        right = jnp.concatenate([b[...] for b in blocks[2 * i : 2 * i + 2]], axis=0)
        part = dot(left, right, 1, 0)
        out[:, i * size : (i + 1) * size] = part[:rank] + part[rank : 2 * rank] + part[2 * rank :]


def mask_kernel(groups, own, pair, out):
    core = position()[0]
    lanes, rows = out.shape
    rows = rows // 2
    top, tok = own.shape[0] // 2, own.shape[1]
    rank = lanes // (lax.axis_size("expert") // groups)
    pick = (iota((tok, rows), 1) // top == iota((tok, rows), 0)).astype(BF16)
    here = iota((top, rows), 1) % top == iota((top, rows), 0)
    block = iota((lanes, 1), 0) // rank * groups + (core if groups == 2 else 0)
    for i, pairs in enumerate((own, pair)):
        names = dot(pairs[:top].astype(BF16), pick, 1, 0)
        weights = sum(dot(piece, pick, 1, 0) for piece in pieces(pairs[top:], 3))
        names = jnp.sum(jnp.where(here, names, 0.0), axis=0, keepdims=True)
        weights = jnp.sum(jnp.where(here, weights, 0.0), axis=0, keepdims=True)
        masked = jnp.where(names == block.astype(F32), weights, 0.0)
        out[:, i * rows : (i + 1) * rows] = masked


def terms_kernel(low, tok, z0, z1, z2, z3, mask, mine, other, *refs):
    outs, (work, spread) = refs[:-2], refs[-2:]
    lower = position()[1]
    lanes, rows = mask.shape
    rows = rows // 2
    rank = lanes // (SLICES * low)
    z = 0.0
    for block in (z0, z1, z2, z3):
        z = z + block[...].astype(F32)
    repeat = iota((2 * tok, 2 * rows), 1) // (rows // tok) == iota((2 * tok, 2 * rows), 0)
    z = dot(z.astype(BF16), repeat.astype(BF16), 0, 0)
    work[...] = (z * mask[...]).astype(BF16)
    for r in range(low):
        for j in range(SLICES):
            start = pl.multiple_of((j * low + (lower ^ r)) * rank, rank)
            spread[(r * SLICES + j) * rank : (r * SLICES + j + 1) * rank] = work[
                pl.ds(start, rank)
            ]
    for chunk in range(len(outs) // low):
        block, width = outs[chunk * low].shape
        here = slice(chunk * width, (chunk + 1) * width)
        part = dot(spread[:, :rows], mine[:, here], 1, 0)
        part = (part + dot(spread[:, rows:], other[:, here], 1, 0)).astype(BF16)
        for r in range(low):
            outs[chunk * low + r][...] = part[r * block : (r + 1) * block]


def shards(tokens, expert_ids, route_probs, cotangents, sketch):
    n_expert = lax.axis_size("expert")
    n_dp = lax.axis_size("dp")
    count = n_expert * n_dp
    line = count // SLICES
    low = line // 2
    groups = 2 // n_dp
    tok, width = tokens.shape
    top = expert_ids.shape[1]
    hidden, rank = sketch.shape
    rows = tok * top
    share = width // SLICES
    lanes = count // 2 * rank
    part = hidden // n_dp
    scale = 1.0 / math.sqrt(rows)
    _, lower, place, half = position()
    limit = LIMIT if n_dp == 1 else LARGE
    shape = jax.ShapeDtypeStruct

    def exchange(block, step):
        return lax.ppermute(block, AXES, [(i, i ^ step) for i in range(count)])

    cot = cotangents.reshape(rows, hidden)

    cuts = [
        lax.dynamic_slice_in_dim(tokens, (place ^ j) * share, share, axis=1) for j in range(SLICES)
    ]
    cuts = cuts[:1] + [exchange(cuts[j], j * line) for j in range(1, SLICES)]

    y, pairs = call(
        functools.partial(first_kernel, groups),
        [shape((tok, groups * lanes), BF16), shape((2 * top, tok), F32)],
        [HBM] * 4,
        [
            pltpu.VMEM((rows, hidden), BF16),
            pltpu.VMEM((rank, hidden), F32),
            pltpu.VMEM((top, tok), jnp.int32),
            pltpu.VMEM((top, tok), F32),
            pltpu.SemaphoreType.DMA((8,)),
        ],
        cot,
        sketch.T,
        expert_ids.T,
        route_probs.T,
        limit=LARGE,
    )

    pairs, send = lax.optimization_barrier((pairs, cot))
    pairs = [pairs, exchange(pairs, 1)]
    mine = cot
    if n_dp > 1:
        mine = lax.dynamic_slice_in_dim(cot, half * part, part, axis=1)
        send = lax.dynamic_slice_in_dim(send, (1 - half) * part, part, axis=1)
    other = exchange(send, 1)

    y, cuts[2], cuts[3] = lax.optimization_barrier((y, cuts[2], cuts[3]))
    ys = [jnp.concatenate([y] + [exchange(y, j * line) for j in range(1, SLICES)], axis=0)]
    xs = [[jnp.concatenate(cuts[:2], axis=0)], [jnp.concatenate(cuts[2:], axis=0)]]
    step = 2
    while step < line:
        xs = [side + [exchange(b, step) for b in side] for side in xs]
        ys = ys + [exchange(b, step) for b in ys]
        step *= 2
    skip = lanes if groups == 2 else 0
    lines = [
        (*near, *[exchange(b, 1) for b in near], y, exchange(y[:, skip:], 1))
        for *near, y in zip(*xs, ys)
    ]

    if n_dp == 1:
        work = [
            pltpu.VMEM((2 * SLICES * tok, share), BF16),
            pltpu.VMEM((2 * SLICES * tok, lanes), BF16),
            pltpu.SemaphoreType.DMA((6,)),
        ]
        [columns] = call(
            columns_kernel, [shape((lanes, share), F32)], [HBM] * 6, work, *lines[0]
        )
        zs = call(
            functools.partial(z_kernel, low),
            [shape((2 * tok, lanes), BF16)] * SLICES + [shape((rank, share), BF16)] * SLICES,
            [VMEM] * 5 + [HBM] * 6,
            [pltpu.VMEM((lanes, share), BF16)] + work,
            columns,
            *lines[0][:4],
            *lines[1],
        )
    else:
        left = jnp.concatenate([y for *_, a, b in lines for y in (a, b)], axis=0)
        right = jnp.concatenate([x for row in lines for x in row[:4]], axis=0)
        columns = dot(left, right, 0, 0).astype(BF16)
        zs, own = [], []
        for j in range(SLICES):
            here = slice(j % 2 * tok, (j % 2 + 1) * tok)
            x = jnp.concatenate([lines[0][j // 2][here], lines[0][2 + j // 2][here]], axis=0)
            start = ((place ^ j) * low + lower) * rank
            own.append(lax.dynamic_slice_in_dim(columns, start, rank, axis=0))
            zs.append(dot(x, columns, 1, 1).astype(BF16))
        zs = zs + own
    columns = zs[SLICES:]
    zs = list(zs[:1]) + [exchange(zs[j], j * line) for j in range(1, SLICES)]

    [mask] = call(
        functools.partial(mask_kernel, groups),
        [shape((lanes, 2 * rows), F32)],
        [VMEM] * 2,
        [],
        *pairs,
        limit=limit,
    )
    piece = part // CHUNKS
    terms = call(
        functools.partial(terms_kernel, low, tok),
        [shape((SLICES * rank, piece), BF16)] * (low * CHUNKS),
        [VMEM] * (SLICES + 3),
        [pltpu.VMEM((lanes, 2 * rows), BF16)] * 2,
        *zs,
        mask,
        mine,
        other,
        limit=limit,
    )
    columns = list(columns[:1]) + [exchange(columns[j], j * line) for j in range(1, SLICES)]
    kept, gone = [], []
    for i in range(CHUNKS):
        parts = terms[i * low : (i + 1) * low]
        parts = [term.reshape(SLICES, rank, piece) for term in parts]
        step = 2
        while len(parts) > 1:
            got = [exchange(send, step) for send in parts[1::2]]
            if step == 2 and i == 0:
                got[0], *columns = lax.optimization_barrier((got[0], *columns))
                inverse, basis = call(
                    inverse_kernel,
                    [shape((rank, rank), F32), shape((rank, width // n_dp), F32)],
                    [VMEM] * SLICES,
                    [pltpu.VMEM((SLICES, rank, share), BF16)],
                    *columns,
                )
            if step == 2 and i == 1:
                got[0], gone[0], inverse = lax.optimization_barrier((got[0], gone[0], inverse))
            parts = [add(keep, other) for keep, other in zip(parts[::2], got)]
            step *= 2
        own = [lax.dynamic_index_in_dim(parts[0], place ^ j, 0, False) for j in range(SLICES)]
        kept.append(jnp.stack(own[::2]))
        gone.append(exchange(jnp.stack(own[1::2]), line))
    blocks = []
    for keep, other in zip(kept, gone):
        both = add(keep, other)
        blocks += [both[0], exchange(both[1], 2 * line)]
    [coeffs] = call(
        functools.partial(coeffs_kernel, scale),
        [shape((rank, part), F32)],
        [VMEM] * (1 + len(blocks)),
        [],
        inverse,
        *blocks,
    )
    return basis[None], coeffs[None]


def solution(mesh):
    in_specs = (
        P(("group", "expert", "dp"), None),
        P(("group", "expert", "dp"), None),
        P(("group", "expert", "dp"), None),
        P(("group", "expert", "dp"), None, None),
        P(),
    )
    out_specs = (P(("group", "expert"), None, "dp"), P(("group", "expert"), None, "dp"))
    return jax.shard_map(shards, mesh=mesh, in_specs=in_specs, out_specs=out_specs, check_vma=False)
```

```python
import functools
import math

import jax
import jax.numpy as jnp
from jax import lax
from jax.experimental import pallas as pl
from jax.experimental.pallas import tpu as pltpu
from jax.sharding import PartitionSpec as P

AXES = ("expert", "dp")
CHUNKS = 2
SLICES = 4
LIMIT = 12 * 1024 * 1024
LARGE = 56 * 1024 * 1024
VMEM = pl.BlockSpec(memory_space=pltpu.VMEM)
HBM = pl.BlockSpec(memory_space=pltpu.HBM)
BF16 = jnp.bfloat16
F32 = jnp.float32


def dot(left, right, left_dim, right_dim):
    dims = (((left_dim,), (right_dim,)), ((), ()))
    return lax.dot_general(left, right, dims, preferred_element_type=F32)


def add(left, right):
    return (left.astype(F32) + right.astype(F32)).astype(BF16)


def iota(shape, dim):
    return lax.broadcasted_iota(jnp.int32, shape, dim)


def position():
    half = lax.axis_index("dp")
    me = lax.axis_index("expert") * lax.axis_size("dp") + half
    line = lax.axis_size("expert") * lax.axis_size("dp") // SLICES
    return me % 2, me // 2 % (line // 2), me // line, half


def call(body, shapes, spaces, scratch, *args, limit=LIMIT):
    return pl.pallas_call(
        body,
        out_shape=shapes,
        in_specs=spaces,
        out_specs=[VMEM] * len(shapes),
        scratch_shapes=scratch,
        compiler_params=pltpu.CompilerParams(vmem_limit_bytes=limit),
        cost_estimate=pl.CostEstimate(flops=1, bytes_accessed=1, transcendentals=0),
    )(*args)


def pieces(value, count):
    terms = []
    for _ in range(count):
        terms.append(value.astype(BF16))
        value = value - terms[-1].astype(F32)
    return terms


def pair_columns(ids, probs):
    top, tok = ids.shape
    rows = tok * top
    pick = (iota((rows, tok), 0) // top == iota((rows, tok), 1)).astype(BF16)
    here = iota((rows, top), 0) % top == iota((rows, top), 1)
    names = dot(pick, ids.astype(BF16), 1, 1)
    weights, rest = jnp.zeros((rows, top), F32), probs
    for _ in range(3):
        piece = rest.astype(BF16)
        weights = weights + dot(pick, piece, 1, 1)
        rest = rest - piece.astype(F32)
    names = jnp.sum(jnp.where(here, names, 0.0), axis=1, keepdims=True)
    weights = jnp.sum(jnp.where(here, weights, 0.0), axis=1, keepdims=True)
    return names, weights


def load(pairs, sems):
    copies = [pltpu.make_async_copy(src, dst, sems.at[i]) for i, (src, dst) in enumerate(pairs)]
    for copy in copies:
        copy.start()
    return copies


def first_kernel(groups, tokens, cot_at, sketch_at, ids_at, probs_at, *refs):
    outs, pairs, (cot, sketch, ids, probs, sems, x_sems) = refs[:SLICES], refs[SLICES], refs[5:]
    core, _, place, _ = position()
    rows = cot.shape[0]
    tok = pairs.shape[1]
    top = rows // tok
    rank = sketch.shape[0]
    share = tokens.shape[1] // SLICES
    lanes = (outs[0].shape[1] - share) // groups
    parts = 4
    piece = rows // parts
    sources = [(ids_at, ids), (probs_at, probs), (sketch_at, sketch)]
    for i in range(parts):
        cut = pl.ds(i * piece, piece)
        sources.append((cot_at.at[cut], cot.at[cut]))
    copies = load(sources, sems)
    sources = []
    for j, out in enumerate(outs):
        cut = pl.ds(pl.multiple_of((place ^ j) * share, share), share)
        sources.append((tokens.at[:, cut], out.at[:, pl.ds(lanes, share)]))
    x_copies = load(sources, x_sems)
    copies[0].wait()
    copies[1].wait()
    pairs[:top] = ids[...].astype(F32)
    pairs[top:] = probs[...]
    names, weights = pair_columns(pairs[:top], pairs[top:])
    copies[2].wait()
    both = jnp.concatenate(pieces(sketch[...], 2), axis=0)
    pair = []
    for i in range(0, parts, 2):
        copies[3 + i].wait()
        copies[4 + i].wait()
        pair.append(dot(cot[i * piece : (i + 2) * piece], both, 1, 1))
    pair = jnp.concatenate(pair, axis=0)
    pair = (pair[:, :rank] + pair[:, rank:]) * weights
    lane = iota((rank, lanes), 1)
    tiled = dot(pair.astype(BF16), (iota((rank, lanes), 0) == lane % rank).astype(BF16), 1, 0)
    block = iota((1, lanes), 1) // rank * groups
    pick = (iota((rows, tok), 0) // top == iota((rows, tok), 1)).astype(BF16)
    for i in range(groups):
        name = block + (core ^ i) if groups == 2 else block
        y = jnp.where(names == name.astype(F32), tiled, 0.0).astype(BF16)
        y = dot(pick, y, 0, 0).astype(BF16)
        for out in outs:
            out[:, i * (lanes + share) : i * (lanes + share) + lanes] = y
    for copy in x_copies:
        copy.wait()


def gather(near, far, x, y, sems):
    share, lanes = x.shape[1], y.shape[1]
    rows = near[0].shape[0]
    sources = []
    for i, (a, b) in enumerate(zip(near, far)):
        cut = pl.ds(2 * i * rows, rows)
        sources.append((a.at[:, pl.ds(0, lanes)], y.at[cut]))
        sources.append((a.at[:, pl.ds(lanes, share)], x.at[cut]))
        cut = pl.ds((2 * i + 1) * rows, rows)
        sources.append((b.at[:, pl.ds(0, share)], x.at[cut]))
        sources.append((b.at[:, pl.ds(share, lanes)], y.at[cut]))
    for copy in load(sources, sems):
        copy.wait()


def columns_kernel(n, *refs):
    out, x, y, sems = refs[2 * n :]
    gather(refs[:n], refs[n : 2 * n], x, y, sems)
    out[...] = dot(y[...], x[...], 0, 0)


def z_kernel(n, low, part, near_a, near_b, far_a, far_b, *refs):
    outs, (x, y, columns, sems) = refs[2 * n : -4], refs[-4:]
    _, lower, place, _ = position()
    gather(refs[:n], refs[n : 2 * n], x, y, sems)
    rank = columns.shape[0] // (SLICES * low)
    share = x.shape[1]
    lanes = y.shape[1]
    rows = near_a.shape[0]
    tok = rows // 2
    total = (part[...] + dot(y[...], x[...], 0, 0)).astype(BF16)
    columns[...] = total
    own = [near_a[:, lanes : lanes + share], near_b[:, lanes : lanes + share]]
    own = jnp.concatenate(own + [far_a[:, :share], far_b[:, :share]], axis=0)
    z = dot(own, total, 1, 1).astype(BF16)
    for j in range(SLICES):
        for core in range(2):
            start = 2 * core * rows + j * tok
            outs[j][core * tok : (core + 1) * tok] = z[start : start + tok]
        expert = (place ^ j) * low + lower
        outs[SLICES + j][...] = columns[pl.ds(pl.multiple_of(expert * rank, rank), rank)]


def inverse_kernel(c0, c1, c2, c3, inverse, basis, columns):
    _, _, place, half = position()
    rank = inverse.shape[0]
    _, _, share = columns.shape
    gram = 0.0
    for j, block in enumerate((c0, c1, c2, c3)):
        columns[place ^ j] = block[...]
        gram = gram + dot(block[...], block[...], 1, 1)
    row = iota((rank, 128), 0)
    lane = iota((rank, 128), 1)
    eye = (row + rank == lane).astype(F32)
    work = jnp.concatenate([gram, jnp.zeros((rank, 128 - rank), F32)], axis=1) + eye
    for first in range(0, rank, 4):
        heads = [work[first + i : first + i + 1] for i in range(4)]
        sides = [
            jnp.broadcast_to(work[:, first + i : first + i + 1], (rank, 128)) for i in range(4)
        ]
        taken = 0.0
        for i in range(4):
            pivot = first + i
            factor = sides[i] / sides[i][pivot : pivot + 1]
            factor = jnp.where(row > pivot, factor, 0.0)
            taken = taken + factor * heads[i]
            for k in range(i + 1, 4):
                sides[k] = sides[k] - factor * sides[k][pivot : pivot + 1]
                heads[k] = heads[k] - factor[first + k : first + k + 1] * heads[i]
        work = work - taken
    diagonal = jnp.sum(jnp.where(row == lane, work, 0.0), axis=1, keepdims=True)
    result = work[:, rank : 2 * rank] * lax.rsqrt(diagonal)
    inverse[...] = result
    scaled = result * math.sqrt(SLICES * share)
    scaled = jnp.concatenate(pieces(scaled, 3), axis=0)
    count = basis.shape[1] // share
    for i in range(count):
        out = dot(scaled, columns[half * count + i], 1, 0)
        out = out[:rank] + out[rank : 2 * rank] + out[2 * rank :]
        basis[:, i * share : (i + 1) * share] = out


def coeffs_kernel(scale, inverse, *refs):
    blocks, out = refs[:-1], refs[-1]
    rank, size = blocks[0].shape
    left = jnp.concatenate(pieces(inverse[...] * scale, 3), axis=0)
    left = jnp.concatenate([left] * 2, axis=1)
    for i in range(len(blocks) // 2):
        right = jnp.concatenate([b[...] for b in blocks[2 * i : 2 * i + 2]], axis=0)
        part = dot(left, right, 1, 0)
        out[:, i * size : (i + 1) * size] = part[:rank] + part[rank : 2 * rank] + part[2 * rank :]


def mask_kernel(groups, own, pair, out):
    core = position()[0]
    lanes, rows = out.shape
    rows = rows // 2
    top, tok = own.shape[0] // 2, own.shape[1]
    rank = lanes // (lax.axis_size("expert") // groups)
    pick = (iota((tok, rows), 1) // top == iota((tok, rows), 0)).astype(BF16)
    here = iota((top, rows), 1) % top == iota((top, rows), 0)
    block = iota((lanes, 1), 0) // rank * groups + (core if groups == 2 else 0)
    for i, pairs in enumerate((own, pair)):
        names = dot(pairs[:top].astype(BF16), pick, 1, 0)
        weights = sum(dot(piece, pick, 1, 0) for piece in pieces(pairs[top:], 3))
        names = jnp.sum(jnp.where(here, names, 0.0), axis=0, keepdims=True)
        weights = jnp.sum(jnp.where(here, weights, 0.0), axis=0, keepdims=True)
        masked = jnp.where(names == block.astype(F32), weights, 0.0)
        out[:, i * rows : (i + 1) * rows] = masked


def terms_kernel(low, tok, z0, z1, z2, z3, mask, mine, other, *refs):
    outs, (work, spread) = refs[:-2], refs[-2:]
    lower = position()[1]
    lanes, rows = mask.shape
    rows = rows // 2
    rank = lanes // (SLICES * low)
    z = 0.0
    for block in (z0, z1, z2, z3):
        z = z + block[...].astype(F32)
    repeat = iota((2 * tok, 2 * rows), 1) // (rows // tok) == iota((2 * tok, 2 * rows), 0)
    z = dot(z.astype(BF16), repeat.astype(BF16), 0, 0)
    work[...] = (z * mask[...]).astype(BF16)
    for r in range(low):
        for j in range(SLICES):
            start = pl.multiple_of((j * low + (lower ^ r)) * rank, rank)
            spread[(r * SLICES + j) * rank : (r * SLICES + j + 1) * rank] = work[
                pl.ds(start, rank)
            ]
    for chunk in range(len(outs) // low):
        block, width = outs[chunk * low].shape
        here = slice(chunk * width, (chunk + 1) * width)
        part = dot(spread[:, :rows], mine[:, here], 1, 0)
        part = (part + dot(spread[:, rows:], other[:, here], 1, 0)).astype(BF16)
        for r in range(low):
            outs[chunk * low + r][...] = part[r * block : (r + 1) * block]


def shards(tokens, expert_ids, route_probs, cotangents, sketch):
    n_expert = lax.axis_size("expert")
    n_dp = lax.axis_size("dp")
    count = n_expert * n_dp
    line = count // SLICES
    low = line // 2
    groups = 2 // n_dp
    tok, width = tokens.shape
    top = expert_ids.shape[1]
    hidden, rank = sketch.shape
    rows = tok * top
    share = width // SLICES
    lanes = count // 2 * rank
    part = hidden // n_dp
    scale = 1.0 / math.sqrt(rows)
    _, lower, place, half = position()
    limit = LIMIT if n_dp == 1 else LARGE
    shape = jax.ShapeDtypeStruct

    def exchange(block, step):
        return lax.ppermute(block, AXES, [(i, i ^ step) for i in range(count)])

    cot = cotangents.reshape(rows, hidden)

    *blocks, pairs = call(
        functools.partial(first_kernel, groups),
        [shape((tok, groups * lanes + share), BF16)] * SLICES + [shape((2 * top, tok), F32)],
        [HBM] * 5,
        [
            pltpu.VMEM((rows, hidden), BF16),
            pltpu.VMEM((rank, hidden), F32),
            pltpu.VMEM((top, tok), jnp.int32),
            pltpu.VMEM((top, tok), F32),
            pltpu.SemaphoreType.DMA((8,)),
            pltpu.SemaphoreType.DMA((SLICES,)),
        ],
        tokens,
        cot,
        sketch.T,
        expert_ids.T,
        route_probs.T,
        limit=LARGE,
    )
    blocks = blocks[:1] + [exchange(blocks[j], j * line) for j in range(1, SLICES)]

    pairs, send = lax.optimization_barrier((pairs, cot))
    pairs = [pairs, exchange(pairs, 1)]
    mine = cot
    if n_dp > 1:
        mine = lax.dynamic_slice_in_dim(cot, half * part, part, axis=1)
        send = lax.dynamic_slice_in_dim(send, (1 - half) * part, part, axis=1)
    other = exchange(send, 1)

    near = [[jnp.concatenate(blocks[i : i + 2], axis=0)] for i in range(0, SLICES, 2)]
    step = 2
    while step < line:
        near = [side + [exchange(b, step) for b in side] for side in near]
        step *= 2
    skip = lanes if groups == 2 else 0

    first = [near[0][0], near[1][0]]
    late = near[0][1:] + near[1][1:]
    far = [exchange(b[:, skip:], 1) for b in first]
    if n_dp == 1:
        [columns] = call(
            functools.partial(columns_kernel, 2),
            [shape((lanes, share), F32)],
            [HBM] * 4,
            [
                pltpu.VMEM((8 * tok, share), BF16),
                pltpu.VMEM((8 * tok, lanes), BF16),
                pltpu.SemaphoreType.DMA((8,)),
            ],
            *first,
            *far,
        )
        late[-1], columns = lax.optimization_barrier((late[-1], columns))
        count_late = len(late)
        zs = call(
            functools.partial(z_kernel, count_late, low),
            [shape((2 * tok, lanes), BF16)] * SLICES + [shape((rank, share), BF16)] * SLICES,
            [VMEM] * 5 + [HBM] * (2 * count_late),
            [
                pltpu.VMEM((4 * count_late * tok, share), BF16),
                pltpu.VMEM((4 * count_late * tok, lanes), BF16),
                pltpu.VMEM((lanes, share), BF16),
                pltpu.SemaphoreType.DMA((4 * count_late,)),
            ],
            columns,
            *first,
            *far,
            *late,
            *[exchange(b[:, skip:], 1) for b in late],
        )
    else:
        far += [exchange(b[:, skip:], 1) for b in late]
        rows_all = jnp.concatenate(first + late + far, axis=0)
        columns = dot(rows_all[:, :lanes], rows_all[:, lanes:], 0, 0).astype(BF16)
        zs, own = [], []
        for j in range(SLICES):
            here = slice(j % 2 * tok, (j % 2 + 1) * tok)
            x = jnp.concatenate([first[j // 2][here], far[j // 2][here]], axis=0)
            start = ((place ^ j) * low + lower) * rank
            own.append(lax.dynamic_slice_in_dim(columns, start, rank, axis=0))
            zs.append(dot(x[:, lanes:], columns, 1, 1).astype(BF16))
        zs = zs + own
    columns = zs[SLICES:]
    zs = list(zs[:1]) + [exchange(zs[j], j * line) for j in range(1, SLICES)]

    [mask] = call(
        functools.partial(mask_kernel, groups),
        [shape((lanes, 2 * rows), F32)],
        [VMEM] * 2,
        [],
        *pairs,
        limit=limit,
    )
    piece = part // CHUNKS
    terms = call(
        functools.partial(terms_kernel, low, tok),
        [shape((SLICES * rank, piece), BF16)] * (low * CHUNKS),
        [VMEM] * (SLICES + 3),
        [pltpu.VMEM((lanes, 2 * rows), BF16)] * 2,
        *zs,
        mask,
        mine,
        other,
        limit=limit,
    )
    columns = list(columns[:1]) + [exchange(columns[j], j * line) for j in range(1, SLICES)]
    kept, gone = [], []
    for i in range(CHUNKS):
        parts = terms[i * low : (i + 1) * low]
        parts = [term.reshape(SLICES, rank, piece) for term in parts]
        step = 2
        while len(parts) > 1:
            got = [exchange(send, step) for send in parts[1::2]]
            if step == 2 and i == 0:
                got[0], *columns = lax.optimization_barrier((got[0], *columns))
                inverse, basis = call(
                    inverse_kernel,
                    [shape((rank, rank), F32), shape((rank, width // n_dp), F32)],
                    [VMEM] * SLICES,
                    [pltpu.VMEM((SLICES, rank, share), BF16)],
                    *columns,
                )
            if step == 2 and i == 1:
                got[0], gone[0], inverse = lax.optimization_barrier((got[0], gone[0], inverse))
            parts = [add(keep, other) for keep, other in zip(parts[::2], got)]
            step *= 2
        own = [lax.dynamic_index_in_dim(parts[0], place ^ j, 0, False) for j in range(SLICES)]
        kept.append(jnp.stack(own[::2]))
        gone.append(exchange(jnp.stack(own[1::2]), line))
    blocks = []
    for keep, other in zip(kept, gone):
        both = add(keep, other)
        blocks += [both[0], exchange(both[1], 2 * line)]
    [coeffs] = call(
        functools.partial(coeffs_kernel, scale),
        [shape((rank, part), F32)],
        [VMEM] * (1 + len(blocks)),
        [],
        inverse,
        *blocks,
    )
    return basis[None], coeffs[None]


def solution(mesh):
    in_specs = (
        P(("group", "expert", "dp"), None),
        P(("group", "expert", "dp"), None),
        P(("group", "expert", "dp"), None),
        P(("group", "expert", "dp"), None, None),
        P(),
    )
    out_specs = (P(("group", "expert"), None, "dp"), P(("group", "expert"), None, "dp"))
    return jax.shard_map(shards, mesh=mesh, in_specs=in_specs, out_specs=out_specs, check_vma=False)
```
